128 devices in a mesh: gx: 8 (over z, x_hi), gy: 8 (over y, x_lo), sa: 2 (over core).
Axes of the slice: x: 4 (x_hi: 2, x_lo: 2; x = x_hi * 2 + x_lo), y: 4, z: 4, core: 2. Of those that a mesh axis runs over, the one named last changes fastest.
Arguments:
- mass_concentration: float32 [8, 2048, 2048], P('sa', 'gx', 'gy'), may hold values from 0.5 to 2
- thermal_reading: float32 [8, 2048, 2048], P('sa', 'gx', 'gy'), may hold values from 0.5 to 4
- eastward_transport_ratio: float32 [8, 2048, 2048], P('sa', 'gx', 'gy'), may hold values from 0.1 to 0.9
- northward_transport_ratio: float32 [8, 2048, 2048], P('sa', 'gx', 'gy'), may hold values from 0.1 to 0.9
- partition_processor: int32 [8, 8], P('gx'), may hold values from 0 to 1, as said below
Outputs:
- advected: float32 [2, 8, 2048, 2048], P(None, 'sa', 'gx', 'gy')
- gradients: float32 [96, 2, 3, 8, 32, 2048], P(('gx', 'sa'), None, None, None, None, 'gy')
- wedge: float32 [96, 8, 32, 2048], P(('gx', 'sa'), None, None, 'gy')
The draws below stay inside these ranges and needn't reach their ends.
Inputs may be any that keep to these rules, and one draw needn't show every extreme that they name: `partition_processor`: in every row of 8 entries at most 6 are 0 and at most 6 are 1.
All inputs are finite; a program needn't handle non-finite values.
Results may differ from the reference program's by a relative error of at most 0.0003.
Values sent between devices are 32-bit elements; how exact they have to be, the bound alone decides.
No kernel may reach another device: no remote copies, remote signals or barrier semaphores. Data moves between devices by JAX's collectives and lax.ppermute only.
A program may use at most 128 MiB of HBM per device.

```python
import math
import jax
import jax.numpy as jnp

CX = 256
SHEET_LEVELS = 8
NP = 8
CAP = 6
PIECE_X_WIDTH = 32
ZONES_ACROSS_LON = 2048
ZONES_ACROSS_LAT = 2048
N_GX = 8


def draw_partition_processor(key, part):
    key = jax.random.fold_in(key, 7)
    count_key, perm_key = jax.random.split(key)
    ones = jax.random.randint(count_key, (N_GX,), NP - CAP, CAP + 1)
    ones = ones.at[0].set(CAP).at[1].set(NP - CAP)
    keys = jax.random.split(perm_key, N_GX)
    perms = jax.vmap(lambda kk: jax.random.permutation(kk, NP))(keys)
    return (perms < ones[:, None]).astype(jnp.int32)


def level_of(own_key, extent, shards, least, largest):
    loudness, own = 1.0, jax.random.fold_in(own_key, 6)
    for position, blocks in shards:
        heights = jnp.exp(jax.random.uniform(jax.random.fold_in(own, position), (blocks,), jnp.float32, least / len(shards), largest / len(shards)))
        loudness = loudness * jnp.repeat(heights, extent[position] // blocks).reshape([-1 if axis == position else 1 for axis in range(len(extent))])
    return loudness


def setup_inputs(seed: int = 0) -> dict:
    seeds = jax.random.split(jax.random.key(seed), 6)
    mass_concentration = jnp.clip(0.5 + 1.5 * jax.random.uniform(seeds[0], (SHEET_LEVELS, ZONES_ACROSS_LON, ZONES_ACROSS_LAT), jnp.float32) ** level_of(seeds[0], (SHEET_LEVELS, ZONES_ACROSS_LON, ZONES_ACROSS_LAT), ((0, 2), (1, 8), (2, 8)), -0.2, 0.2), 0.5, 2.0)
    thermal_reading = jnp.clip(jnp.exp(math.log(4.0) - 2.0794415 * jax.random.uniform(seeds[1], (SHEET_LEVELS, ZONES_ACROSS_LON, ZONES_ACROSS_LAT), jnp.float32) ** level_of(seeds[1], (SHEET_LEVELS, ZONES_ACROSS_LON, ZONES_ACROSS_LAT), ((0, 2), (1, 8), (2, 8)), -0.2, 0.2)), 0.5, 4.0)
    eastward_transport_ratio = jnp.clip(0.1 + 0.79999997 * jax.random.uniform(seeds[2], (SHEET_LEVELS, ZONES_ACROSS_LON, ZONES_ACROSS_LAT), jnp.float32) ** level_of(seeds[2], (SHEET_LEVELS, ZONES_ACROSS_LON, ZONES_ACROSS_LAT), ((0, 2), (1, 8), (2, 8)), -0.2, 0.2), 0.1, 0.9)
    northward_transport_ratio = jnp.clip(0.1 + 0.79999997 * jax.random.uniform(seeds[3], (SHEET_LEVELS, ZONES_ACROSS_LON, ZONES_ACROSS_LAT), jnp.float32) ** level_of(seeds[3], (SHEET_LEVELS, ZONES_ACROSS_LON, ZONES_ACROSS_LAT), ((0, 2), (1, 8), (2, 8)), -0.2, 0.2), 0.1, 0.9)
    partition_processor = draw_partition_processor(jax.random.fold_in(seeds[5], 71), 0)
    return {"mass_concentration": mass_concentration, "thermal_reading": thermal_reading, "eastward_transport_ratio": eastward_transport_ratio, "northward_transport_ratio": northward_transport_ratio, "partition_processor": partition_processor}


def face_flux(qm2, qm1, q0, q1, q2, crs):
    a_right = 7.0 / 12.0 * (q0 + q1) - 1.0 / 12.0 * (qm1 + q2)
    a_left = 7.0 / 12.0 * (qm1 + q0) - 1.0 / 12.0 * (qm2 + q1)
    delta = a_right - a_left
    curve = 6.0 * (q0 - 0.5 * (a_left + a_right))
    return crs * (a_right - 0.5 * crs * (delta - (1.0 - crs * (2.0 / 3.0)) * curve))


def sweep(field, crs, sweep_direction):
    flux = face_flux(jnp.roll(field, 2, sweep_direction), jnp.roll(field, 1, sweep_direction), field,
                     jnp.roll(field, -1, sweep_direction), jnp.roll(field, -2, sweep_direction), crs)
    return field - (flux - jnp.roll(flux, 1, sweep_direction))


def derivative(left_two, left_one, right_one, right_two):
    return (8.0 * (right_one - left_one) - (right_two - left_two)) / 12.0


def place_slots(own, cap):
    npieces = own.shape[0]
    dest = jnp.arange(2, dtype=jnp.int32)[:, None]
    hit = (own[None, :] == dest).astype(jnp.int32)
    rank = jnp.cumsum(hit, axis=1) - 1
    slot = jnp.arange(cap, dtype=jnp.int32)[None, :, None]
    match = hit[:, None, :] * (rank[:, None, :] == slot).astype(jnp.int32)
    index = jnp.sum(match * jnp.arange(npieces, dtype=jnp.int32)[None, None, :], axis=-1)
    valid = jnp.sum(match, axis=-1)
    return index.astype(jnp.int32), valid.astype(jnp.int32)


def roll_deriv(field, sweep_direction):
    return derivative(jnp.roll(field, 2, sweep_direction), jnp.roll(field, 1, sweep_direction),
                      jnp.roll(field, -1, sweep_direction), jnp.roll(field, -2, sweep_direction))


def reference(mass_concentration, thermal_reading, eastward_transport_ratio, northward_transport_ratio, partition_processor):
    physical_quantities = jnp.stack([mass_concentration, thermal_reading])
    xswept = sweep(physical_quantities, eastward_transport_ratio[None], 2)
    advected = sweep(xswept, northward_transport_ratio[None], 3)
    gradient_arrays = jnp.stack([roll_deriv(advected, 2), roll_deriv(advected, 3), roll_deriv(advected, 1)], axis=1)
    rx, ry, rz = gradient_arrays[0, 0], gradient_arrays[0, 1], gradient_arrays[0, 2]
    tx, ty, tz = gradient_arrays[1, 0], gradient_arrays[1, 1], gradient_arrays[1, 2]
    first = ry * tz - rz * ty
    second = rz * tx - rx * tz
    third = rx * ty - ry * tx
    wedge_everything = first * first + second * second + third * third
    index, valid = jax.vmap(lambda row: place_slots(row, CAP))(partition_processor)
    starts = jnp.arange(N_GX, dtype=jnp.int32)[:, None, None] * CX + index * PIECE_X_WIDTH
    grid_cell_values = (starts[..., None] + jnp.arange(PIECE_X_WIDTH, dtype=jnp.int32)).reshape(-1)
    selection_mask = valid.reshape(-1).astype(gradient_arrays.dtype)
    slot_count = selection_mask.shape[0]
    chosen_cells = jnp.take(gradient_arrays, grid_cell_values, axis=3).reshape(2, 3, SHEET_LEVELS, slot_count, PIECE_X_WIDTH, gradient_arrays.shape[-1])
    chosen_cells = chosen_cells * selection_mask[None, None, None, :, None, None]
    gradients = jnp.transpose(chosen_cells, (3, 0, 1, 2, 4, 5))
    wedge_chosen = jnp.take(wedge_everything, grid_cell_values, axis=1).reshape(SHEET_LEVELS, slot_count, PIECE_X_WIDTH, gradient_arrays.shape[-1])
    wedge_chosen = wedge_chosen * selection_mask[None, :, None, None]
    wedge = jnp.transpose(wedge_chosen, (1, 0, 2, 3))
    return advected, gradients, wedge
```

```python
import jax
import jax.numpy as jnp
from jax import lax
from jax.experimental import pallas as pl
from jax.experimental.pallas import tpu as pltpu
from jax.sharding import PartitionSpec as P

CAP = 6
NP = 8
RIM = 8
LANES = 128
F32 = jnp.float32
VMEM_LIMIT = 48 * 1024 * 1024


def ring(count, step):
    return [(i, (i + step) % count) for i in range(count)]


def coefficients(c):
    d = 1.0 - c
    m = c * d
    k_right = m * d
    k_left = m * c
    return k_right, k_left, c - k_right + k_left


def face_value(qm1, q0, q1, q2):
    return (7.0 / 12.0) * (q0 + q1) - (1.0 / 12.0) * (qm1 + q2)


def sweep_rows(load_q, load_c, store, a_scr, f_scr, base, count, chunk):
    done = 0
    while done < count:
        n = min(chunk, count - done)
        r = base + done
        k_right, k_left, k_mid = coefficients(load_c(r, n))
        for f in range(2):
            q0 = load_q(f, r, n)
            a = face_value(load_q(f, r - 1, n), q0, load_q(f, r + 1, n), load_q(f, r + 2, n))
            a_scr[f, pl.ds(8 + done, n), :] = a
            flux = k_right * a - k_left * a_scr[f, pl.ds(7 + done, n), :] + k_mid * q0
            f_scr[f, pl.ds(8 + done, n), :] = flux
            store(f, r, n, q0 - (flux - f_scr[f, pl.ds(7 + done, n), :]))
        done += n


def strip_of(x, shift, strip, lane8, old):
    return jnp.where(lane8 == strip, pltpu.roll(x, shift, 1), old)


def lane_iota(rows):
    return lax.broadcasted_iota(jnp.int32, (rows, LANES), 1)


def edge_rows_kernel(d0, t0, x0, y0, d1, t1, x1, y1, lo, hi):
    for f, (a, b) in enumerate(((d0, d1), (t0, t1), (x0, x1), (y0, y1))):
        for h in range(2):
            lo[f, :, h] = a[:, :, h * LANES : (h + 1) * LANES]
            hi[f, :, h] = b[:, :, h * LANES : (h + 1) * LANES]


def edge_rows(fields):
    planes, rows, cols = fields[0].shape
    last = rows // 8 - 1
    low = pl.BlockSpec((planes, 8, cols), lambda i: (0, 0, 0))
    high = pl.BlockSpec((planes, 8, cols), lambda i: (0, last, 0))
    shape = jax.ShapeDtypeStruct((4, planes, 2, 8, LANES), F32)
    whole = pl.BlockSpec(shape.shape, lambda i: (0,) * 5)
    return pl.pallas_call(
        edge_rows_kernel,
        grid=(1,),
        in_specs=[low] * 4 + [high] * 4,
        out_specs=(whole, whole),
        out_shape=(shape, shape),
        name="edge_rows",
    )(*fields, *fields)


def x_inner_kernel(d, t, cx, cy, xs, pack_l, pack_r, a_scr, f_scr):
    p, h = pl.program_id(0), pl.program_id(1)
    q = (d, t)
    rows = d.shape[1]

    def store(f, r, n, value):
        xs[0, f, 0, pl.ds(RIM + r, n), :] = value

    sweep_rows(
        lambda f, r, n: q[f][0, pl.ds(r, n), :],
        lambda r, n: cx[0, pl.ds(r, n), :],
        store,
        a_scr,
        f_scr,
        6,
        rows - 8,
        32,
    )

    def pack(ref, offset):
        for r in range(RIM, RIM + rows, 32):
            lane8 = lane_iota(32) // 8
            old = ref[pl.ds(r, 32), :]
            for f in range(3):
                strip = f * 4 + p
                x = cy[0, pl.ds(r - RIM, 32), :] if f == 2 else xs[0, f, 0, pl.ds(r, 32), :]
                old = strip_of(x, strip * 8 + offset, strip, lane8, old)
            ref[pl.ds(r, 32), :] = old

    @pl.when(h == 0)
    def _():
        pack(pack_l, 0)

    @pl.when(h == 1)
    def _():
        pack(pack_r, 8)


def x_inner(d, t, cx, cy):
    planes, rows, cols = d.shape
    ext = rows + 2 * RIM
    block = pl.BlockSpec((1, rows, LANES), lambda p, h: (p, 0, h))
    packed = pl.BlockSpec((ext, LANES), lambda p, h: (0, 0))
    return pl.pallas_call(
        x_inner_kernel,
        grid=(planes, 2),
        in_specs=[block] * 4,
        out_specs=(
            pl.BlockSpec((1, 2, 1, ext, LANES), lambda p, h: (p, 0, h, 0, 0)),
            packed,
            packed,
        ),
        out_shape=(
            jax.ShapeDtypeStruct((planes, 2, 2, ext, LANES), F32),
            jax.ShapeDtypeStruct((ext, LANES), F32),
            jax.ShapeDtypeStruct((ext, LANES), F32),
        ),
        scratch_shapes=[pltpu.VMEM((2, ext, LANES), F32)] * 2,
        compiler_params=pltpu.CompilerParams(vmem_limit_bytes=VMEM_LIMIT),
        cost_estimate=pl.CostEstimate(flops=40_000_000, bytes_accessed=8_000_000, transcendentals=0),
        name="x_inner",
    )(d, t, cx, cy)


def x_edge_kernel(
    d, t, cx, left, right, xs_in, pl_in, pr_in, xs, pack_l, pack_r, win, a_scr, f_scr, out
):
    side = pl.program_id(0)
    planes = d.shape[0]

    def run(base, lead, top, rim, rim_at):
        for p in range(planes):
            for h in range(2):
                for f, ref in enumerate((d, t, cx)):
                    win[f, lead : lead + 16, :] = ref[p, :, h * LANES : (h + 1) * LANES]
                    win[f, rim_at : rim_at + 8, :] = rim[f, p, h]

                def store(f, r, n, value):
                    out[f, pl.ds(r, n), :] = value

                sweep_rows(
                    lambda f, r, n: win[f, pl.ds(r, n), :],
                    lambda r, n: win[2, pl.ds(r, n), :],
                    store,
                    a_scr,
                    f_scr,
                    base,
                    16,
                    16,
                )
                for f in range(2):
                    xs[p, f, h] = out[f, top : top + 16, :]
        lane8 = lane_iota(16) // 8
        for h, (src, dst) in enumerate(((pl_in, pack_l), (pr_in, pack_r))):
            old = src[...]
            for p in range(planes):
                for f in range(2):
                    strip = f * 4 + p
                    old = strip_of(xs[p, f, h], (strip * 8 + 8 * h) % LANES, strip, lane8, old)
            dst[...] = old
            at = 0 if rim_at == 0 else 8
            old = old[at : at + 8, :]
            for p in range(planes):
                strip = 8 + p
                old = strip_of(rim[3, p, h], (strip * 8 + 8 * h) % LANES, strip, lane8[:8], old)
            dst[at : at + 8, :] = old

    @pl.when(side == 0)
    def _():
        run(4, 8, 0, left, 0)

    @pl.when(side == 1)
    def _():
        run(6, 0, 8, right, 16)


def x_edge(d, t, cx, left, right, xs, pack_l, pack_r):
    planes, rows, cols = d.shape
    last = rows // 16 - 1
    own = pl.BlockSpec((planes, 16, cols), lambda s: (0, s * last, 0))
    rim = pl.BlockSpec(left.shape, lambda s: (0,) * 5)
    packed = pl.BlockSpec((16, LANES), lambda s: (s * (last + 1), 0))
    return pl.pallas_call(
        x_edge_kernel,
        grid=(2,),
        in_specs=[own] * 3 + [rim] * 2 + [pl.BlockSpec(memory_space=pl.ANY), packed, packed],
        out_specs=(
            pl.BlockSpec((planes, 2, 2, 16, LANES), lambda s: (0, 0, 0, s * (last + 1), 0)),
            packed,
            packed,
        ),
        out_shape=tuple(jax.ShapeDtypeStruct(x.shape, F32) for x in (xs, pack_l, pack_r)),
        input_output_aliases={5: 0, 6: 1, 7: 2},
        scratch_shapes=[
            pltpu.VMEM((3, 32, LANES), F32),
            pltpu.VMEM((2, 32, LANES), F32),
            pltpu.VMEM((2, 32, LANES), F32),
            pltpu.VMEM((2, 32, LANES), F32),
        ],
        compiler_params=pltpu.CompilerParams(vmem_limit_bytes=VMEM_LIMIT),
        name="x_edge",
    )(d, t, cx, left, right, xs, pack_l, pack_r)


def wrapped(left, right, lane, step):
    if step > 0:
        new_l = pltpu.roll(jnp.where(lane < step, right, left), LANES - step, 1)
        new_r = pltpu.roll(jnp.where(lane < step, left, right), LANES - step, 1)
    else:
        new_l = pltpu.roll(jnp.where(lane >= LANES + step, right, left), -step, 1)
        new_r = pltpu.roll(jnp.where(lane >= LANES + step, left, right), -step, 1)
    return new_l, new_r


def y_inner_kernel(xs, cy, left, right, out, c_scr):
    rows = cy.shape[1]
    ext = xs.shape[3]
    for h in range(2):
        c_scr[h, 0:RIM, :] = left[0, 0, h]
        c_scr[h, RIM : RIM + rows, :] = cy[0, :, h * LANES : (h + 1) * LANES]
        c_scr[h, RIM + rows : ext, :] = right[0, 0, h]
    n = 16
    lane = lane_iota(n)

    def body(i, _):
        at = pl.ds(pl.multiple_of(i * n, n), n)
        ks = [coefficients(c_scr[h, at, :]) for h in range(2)]
        for f in range(2):
            q = [xs[0, f, h, at, :] for h in range(2)]
            qm1 = wrapped(*q, lane, -1)
            q1 = wrapped(*q, lane, 1)
            q2 = wrapped(*q, lane, 2)
            a = [face_value(qm1[h], q[h], q1[h], q2[h]) for h in range(2)]
            al = wrapped(*a, lane, -1)
            flux = [ks[h][0] * a[h] - ks[h][1] * al[h] + ks[h][2] * q[h] for h in range(2)]
            before = wrapped(*flux, lane, -1)
            for h in range(2):
                out[0, f, h, at, :] = q[h] - (flux[h] - before[h])
        return 0

    lax.fori_loop(0, ext // n, body, 0, unroll=False)


def y_inner(xs, cy, left, right):
    planes, rows, cols = cy.shape
    ext = rows + 2 * RIM
    block = pl.BlockSpec((1, 2, 2, ext, LANES), lambda p: (p, 0, 0, 0, 0))
    rim = pl.BlockSpec((1, 1, 2, 8, LANES), lambda p: (3, p, 0, 0, 0))
    return pl.pallas_call(
        y_inner_kernel,
        grid=(planes,),
        in_specs=[block, pl.BlockSpec((1, rows, cols), lambda p: (p, 0, 0)), rim, rim],
        out_specs=block,
        out_shape=jax.ShapeDtypeStruct(xs.shape, F32),
        scratch_shapes=[pltpu.VMEM((2, ext, LANES), F32)],
        compiler_params=pltpu.CompilerParams(vmem_limit_bytes=VMEM_LIMIT),
        cost_estimate=pl.CostEstimate(flops=40_000_000, bytes_accessed=8_000_000, transcendentals=0),
        name="y_inner",
    )(xs, cy, left, right)


def strip_sweep(a_part, b_part, lane):
    in8 = lane % 8

    def after(x, step):
        xa, xb = x
        return (
            jnp.where(in8 >= 8 - step, pltpu.roll(xb, 8 - step, 1), pltpu.roll(xa, LANES - step, 1)),
            pltpu.roll(xb, LANES - step, 1),
        )

    def before(x):
        xa, xb = x
        return (
            pltpu.roll(xa, 1, 1),
            jnp.where(in8 < 1, pltpu.roll(xa, LANES - 7, 1), pltpu.roll(xb, 1, 1)),
        )

    def courant(x):
        return jnp.where(lane < 32, pltpu.roll(x, 64, 1), pltpu.roll(x, 96, 1))

    q = (a_part, b_part)
    qm1, q1, q2 = before(q), after(q, 1), after(q, 2)
    a = tuple(face_value(qm1[i], q[i], q1[i], q2[i]) for i in range(2))
    al = before(a)
    flux = []
    for i in range(2):
        k = coefficients(courant(q[i]))
        flux.append(k[0] * a[i] - k[1] * al[i] + k[2] * q[i])
    back = before(tuple(flux))
    return tuple(q[i] - (flux[i] - back[i]) for i in range(2))


def y_edge_kernel(s_in, own_l, own_r, from_l, from_r, s, adv, rims, fix):
    p = pl.program_id(0)
    rows = adv.shape[2]
    ext = s.shape[3]
    n = 16
    lane = lane_iota(n)

    @pl.when(p == 0)
    def _():
        def body(i, _):
            at = pl.ds(pl.multiple_of(i * n, n), n)
            la, lb = strip_sweep(from_l[at, :], own_l[at, :], lane)
            ra, rb = strip_sweep(own_r[at, :], from_r[at, :], lane)
            fix[at, :] = jnp.where(lane % 8 < 4, lb, pltpu.roll(ra, LANES - 8, 1))
            rims[at, :] = jnp.where(lane % 8 < 4, rb, pltpu.roll(la, LANES - 8, 1))
            return 0

        lax.fori_loop(0, ext // n, body, 0, unroll=False)

    for f in range(2):
        shift = LANES - (f * 4 + p) * 8
        for r in range(0, ext, n):
            edge = pltpu.roll(fix[r : r + n, :], shift, 1)
            new_l = jnp.where(lane < 3, edge, s_in[0, f, 0, r : r + n, :])
            new_r = jnp.where(lane >= LANES - 2, edge, s_in[0, f, 1, r : r + n, :])
            s[0, f, 0, r : r + n, :] = new_l
            s[0, f, 1, r : r + n, :] = new_r
        for h in range(2):
            adv[f, 0, :, h * LANES : (h + 1) * LANES] = s[0, f, h, RIM : RIM + rows, :]


def y_edge(swept, own_l, own_r, from_l, from_r):
    planes, _, _, ext, _ = swept.shape
    rows = ext - 2 * RIM
    block = pl.BlockSpec((1, 2, 2, ext, LANES), lambda p: (p, 0, 0, 0, 0))
    packed = pl.BlockSpec((ext, LANES), lambda p: (0, 0))
    return pl.pallas_call(
        y_edge_kernel,
        grid=(planes,),
        in_specs=[block] + [packed] * 4,
        out_specs=(
            block,
            pl.BlockSpec((2, 1, rows, 2 * LANES), lambda p: (0, p, 0, 0)),
            packed,
        ),
        out_shape=(
            jax.ShapeDtypeStruct(swept.shape, F32),
            jax.ShapeDtypeStruct((2, planes, rows, 2 * LANES), F32),
            jax.ShapeDtypeStruct((ext, LANES), F32),
        ),
        scratch_shapes=[pltpu.VMEM((ext, LANES), F32)],
        compiler_params=pltpu.CompilerParams(vmem_limit_bytes=VMEM_LIMIT),
        name="y_edge",
    )(swept, own_l, own_r, from_l, from_r)


def slope(w1, w2):
    return (2.0 / 3.0) * w1 - (1.0 / 12.0) * w2


def gradient_kernel(owner, core, own, other, own_rim, other_rim, grad, wedge):
    slot = pl.program_id(0)
    s = core[0]
    rank = jnp.int32(0)
    piece = jnp.int32(0)
    for j in range(NP):
        mine = owner[0, j] == s
        piece = jnp.where(jnp.logical_and(mine, rank == slot), j, piece)
        rank = rank + mine.astype(jnp.int32)
    used = slot < rank
    width = grad.shape[4]

    @pl.when(jnp.logical_not(used))
    def _():
        grad[...] = jnp.zeros_like(grad)
        wedge[...] = jnp.zeros_like(wedge)

    @pl.when(used)
    def _():
        n = 8
        lane = lane_iota(n)
        first = pl.multiple_of(RIM + piece * width, 8)

        def body(i, _):
            r = pl.multiple_of(first + i * n, n)
            to = pl.ds(pl.multiple_of(i * n, n), n)

            def plane(z, f, h, row):
                ref = own if z < 4 else other
                return ref[z % 4, f, h, pl.ds(row, n), :]

            q = [
                [[plane(z, f, h, r) for h in range(2)] for f in range(2)] for z in range(8)
            ]
            for z in range(8):
                zo = lax.rem(z + 4 * s, 8)
                rim_ref = own_rim if z < 4 else other_rim
                rim = rim_ref[pl.ds(r, n), :]
                g = []
                for f in range(2):
                    lo, hi = q[z][f]
                    edge = pltpu.roll(rim, (LANES - (f * 4 + z % 4) * 8) % LANES, 1)
                    up = [
                        (jnp.where(lane < k, hi, lo), jnp.where(lane < k, edge, hi)) for k in (1, 2)
                    ]
                    down = [
                        (
                            jnp.where(lane >= LANES - k, edge, lo),
                            jnp.where(lane >= LANES - k, lo, hi),
                        )
                        for k in (1, 2)
                    ]
                    for h in range(2):
                        gx = slope(
                            plane(z, f, h, r + 1) - plane(z, f, h, r - 1),
                            plane(z, f, h, r + 2) - plane(z, f, h, r - 2),
                        )
                        gy = slope(
                            pltpu.roll(up[0][h], LANES - 1, 1) - pltpu.roll(down[0][h], 1, 1),
                            pltpu.roll(up[1][h], LANES - 2, 1) - pltpu.roll(down[1][h], 2, 1),
                        )
                        gz = slope(
                            q[(z + 1) % 8][f][h] - q[(z + 7) % 8][f][h],
                            q[(z + 2) % 8][f][h] - q[(z + 6) % 8][f][h],
                        )
                        g.append((gx, gy, gz))
                        cols = slice(h * LANES, (h + 1) * LANES)
                        for k in range(3):
                            grad[0, f, k, zo, to, cols] = g[-1][k]
                for h in range(2):
                    rx, ry, rz = g[h]
                    tx, ty, tz = g[2 + h]
                    a = ry * tz - rz * ty
                    b = rz * tx - rx * tz
                    c = rx * ty - ry * tx
                    wedge[0, zo, to, h * LANES : (h + 1) * LANES] = a * a + b * b + c * c
            return 0

        lax.fori_loop(0, width // n, body, 0, unroll=False)


def gradients_of(owner, core, own, other, own_rim, other_rim):
    planes, _, _, ext, _ = own.shape
    rows = ext - 2 * RIM
    width = rows // NP
    cols = 2 * LANES
    whole = pl.BlockSpec(own.shape, lambda k, o, c: (0,) * 5)
    rim = pl.BlockSpec(own_rim.shape, lambda k, o, c: (0, 0))
    return pl.pallas_call(
        gradient_kernel,
        grid_spec=pltpu.PrefetchScalarGridSpec(
            num_scalar_prefetch=2,
            grid=(CAP,),
            in_specs=[whole, whole, rim, rim],
            out_specs=(
                pl.BlockSpec((1, 2, 3, 8, width, cols), lambda k, o, c: (k, 0, 0, 0, 0, 0)),
                pl.BlockSpec((1, 8, width, cols), lambda k, o, c: (k, 0, 0, 0)),
            ),
        ),
        out_shape=(
            jax.ShapeDtypeStruct((CAP, 2, 3, 8, width, cols), F32),
            jax.ShapeDtypeStruct((CAP, 8, width, cols), F32),
        ),
        compiler_params=pltpu.CompilerParams(vmem_limit_bytes=VMEM_LIMIT),
        name="gradient",
    )(owner, core, own, other, own_rim, other_rim)


def per_device(density, heat, cx, cy, owner):
    nx, ny = lax.axis_size("gx"), lax.axis_size("gy")
    lo, hi = edge_rows((density, heat, cx, cy))
    left = lax.ppermute(hi, "gx", ring(nx, 1))
    right = lax.ppermute(lo, "gx", ring(nx, -1))
    xs, own_l, own_r = x_inner(density, heat, cx, cy)
    xs, own_l, own_r = x_edge(density, heat, cx, left, right, xs, own_l, own_r)
    from_l = lax.ppermute(own_r, "gy", ring(ny, 1))
    from_r = lax.ppermute(own_l, "gy", ring(ny, -1))
    swept = y_inner(xs, cy, left, right)
    swept, advected, rims = y_edge(swept, own_l, own_r, from_l, from_r)
    other = lax.ppermute(swept, "sa", ring(2, 1))
    other_rims = lax.ppermute(rims, "sa", ring(2, 1))
    core = lax.axis_index("sa").astype(jnp.int32).reshape(1)
    gradients, wedge = gradients_of(owner, core, swept, other, rims, other_rims)
    return advected, gradients, wedge


def solution(mesh):
    block = P("sa", "gx", "gy")
    return jax.shard_map(
        per_device,
        mesh=mesh,
        in_specs=(block, block, block, block, P("gx", None)),
        out_specs=(
            P(None, "sa", "gx", "gy"),
            P(("gx", "sa"), None, None, None, None, "gy"),
            P(("gx", "sa"), None, None, "gy"),
        ),
        check_vma=False,
    )
```

```python
import jax
import jax.numpy as jnp
from jax import lax
from jax.experimental import pallas as pl
from jax.experimental.pallas import tpu as pltpu
from jax.sharding import PartitionSpec as P

CAP = 6
NP = 8
RIM = 8
LANES = 128
F32 = jnp.float32
MIB = 1024 * 1024


def ring(count, step):
    return [(i, (i + step) % count) for i in range(count)]


def coefficients(c):
    d = 1.0 - c
    m = c * d
    k_right = m * d
    k_left = m * c
    return k_right, k_left, c - k_right + k_left


def face_value(qm1, q0, q1, q2):
    return (7.0 / 12.0) * (q0 + q1) - (1.0 / 12.0) * (qm1 + q2)


def sweep_rows(load_q, load_c, store, a_scr, f_scr, base, count, chunk, fields=2):
    done = 0
    while done < count:
        n = min(chunk, count - done)
        r = base + done
        k_right, k_left, k_mid = coefficients(load_c(r, n))
        for f in range(fields):
            q0 = load_q(f, r, n)
            a = face_value(load_q(f, r - 1, n), q0, load_q(f, r + 1, n), load_q(f, r + 2, n))
            a_scr[f, pl.ds(8 + done, n), :] = a
            flux = k_right * a - k_left * a_scr[f, pl.ds(7 + done, n), :] + k_mid * q0
            f_scr[f, pl.ds(8 + done, n), :] = flux
            store(f, r, n, q0 - (flux - f_scr[f, pl.ds(7 + done, n), :]))
        done += n


def lane_iota(rows):
    return lax.broadcasted_iota(jnp.int32, (rows, LANES), 1)


def half(h, start=0):
    return slice(start + h * LANES, start + (h + 1) * LANES)


def call(
    kernel, out_shape, operands, name, spaces=None, scratch=(), aliases=None, cost=None, mib=20
):
    vmem = pl.BlockSpec(memory_space=pltpu.VMEM)
    return pl.pallas_call(
        kernel,
        in_specs=[pl.BlockSpec(memory_space=x) for x in spaces] if spaces else [vmem] * len(operands),
        out_specs=jax.tree.map(lambda _: vmem, out_shape),
        out_shape=out_shape,
        scratch_shapes=list(scratch),
        input_output_aliases=aliases or {},
        compiler_params=pltpu.CompilerParams(vmem_limit_bytes=mib * MIB),
        cost_estimate=cost,
        name=name,
    )(*operands)


def out(*shape):
    return jax.ShapeDtypeStruct(shape, F32)


SWEEP_COST = pl.CostEstimate(flops=20_000_000, bytes_accessed=6_000_000, transcendentals=0)


def edge_rows_kernel(d, t, cx, cy, lo, hi, sems):
    rows = d.shape[1]
    copies = []
    for f, ref in enumerate((d, t, cx, cy)):
        copies.append(pltpu.make_async_copy(ref.at[:, 0:RIM, :], lo.at[f], sems.at[f]))
        copies.append(
            pltpu.make_async_copy(ref.at[:, rows - RIM : rows, :], hi.at[f], sems.at[4 + f])
        )
    for c in copies:
        c.start()
    for c in copies:
        c.wait()


def edge_rows(fields):
    planes, _, cols = fields[0].shape
    shape = out(4, planes, RIM, cols)
    return call(
        edge_rows_kernel,
        (shape, shape),
        fields,
        "edge_rows",
        spaces=[pl.ANY] * 4,
        scratch=[pltpu.SemaphoreType.DMA((8,))],
        mib=60,
    )


def x_inner_kernel(d, t, cx, cy, xs, cy_t, win, a_scr, f_scr):
    planes, rows, _ = d.shape

    def body(p, _):
        for h in range(2):
            for f, ref in enumerate((d, t, cx)):
                win[f, 0:rows, :] = ref[p, :, half(h)]

            def store(f, r, n, value):
                xs[p, f, h, pl.ds(RIM + r, n), :] = value

            sweep_rows(
                lambda f, r, n: win[f, pl.ds(r, n), :],
                lambda r, n: win[2, pl.ds(r, n), :],
                store,
                a_scr,
                f_scr,
                6,
                rows - 8,
                32,
            )
            for x in range(2):
                cy_t[p, x, half(h, RIM), :] = cy[p, half(x), half(h)].T
        return 0

    lax.fori_loop(0, planes, body, 0, unroll=False)


def x_inner(d, t, cx, cy):
    planes, rows, cols = d.shape
    ext = rows + 2 * RIM
    return call(
        x_inner_kernel,
        (out(planes, 2, 2, ext, LANES), out(planes, 2, ext, LANES)),
        (d, t, cx, cy),
        "x_inner",
        scratch=[pltpu.VMEM((3, ext, LANES), F32)] + [pltpu.VMEM((2, ext, LANES), F32)] * 2,
        cost=SWEEP_COST,
    )


def edge_sweep(own, rim, high, win, a_scr, f_scr, res):
    lead, rim_at = (0, 16) if high else (8, 0)
    for f in range(3):
        win[f, lead : lead + 16, :] = own(f)
        win[f, rim_at : rim_at + 8, :] = rim(f)

    def store(f, r, n, value):
        res[f, pl.ds(r, n), :] = value

    sweep_rows(
        lambda f, r, n: win[f, pl.ds(r, n), :],
        lambda r, n: win[2, pl.ds(r, n), :],
        store,
        a_scr,
        f_scr,
        6 if high else 4,
        16,
        16,
    )


EDGE_SCRATCH = [
    pltpu.VMEM((3, 32, LANES), F32),
    pltpu.VMEM((2, 32, LANES), F32),
    pltpu.VMEM((2, 32, LANES), F32),
    pltpu.VMEM((2, 32, LANES), F32),
]


def x_edge_kernel(
    d, t, cx, left, right, xs_in, cy_t, xs, x_t, h_t, to_l, to_r, rim_rows, win, a_scr, f_scr, res
):
    planes, rows, _ = d.shape
    ext = rows + 2 * RIM

    for p in range(planes):
        for h in range(2):
            for high in range(2):
                rim = right if high else left
                at = slice(rows - 16, rows) if high else slice(0, 16)
                edge_sweep(
                    lambda f: (d, t, cx)[f][p, at, half(h)],
                    lambda f: rim[f, p, :, half(h)],
                    high,
                    win,
                    a_scr,
                    f_scr,
                    res,
                )
                for f in range(2):
                    k = (f * 4 + p) * 4 + 2 * high
                    if high:
                        xs[p, f, h, rows : rows + RIM, :] = res[f, 8:16, :]
                        rim_rows[h, k : k + 2, :] = res[f, 16:18, :]
                        rim_rows[h, 32 + k : 34 + k, :] = rim[3, p, 0:2, half(h)]
                    else:
                        xs[p, f, h, RIM : 2 * RIM, :] = res[f, 8:16, :]
                        rim_rows[h, k : k + 2, :] = res[f, 6:8, :]
                        rim_rows[h, 32 + k : 34 + k, :] = rim[3, p, 6:8, half(h)]
    for h in range(2):
        h_t[half(h, RIM), :] = rim_rows[h].T
    for p in range(planes):
        for f in range(2):
            for x in range(2):
                for h in range(2):
                    x_t[p, f, x, half(h, RIM), :] = xs[p, f, h, half(x, RIM), :].T
    for buf, at in ((to_l, slice(RIM, 2 * RIM)), (to_r, slice(rows, rows + RIM))):
        for p in range(planes):
            for x in range(2):
                for f in range(2):
                    buf[(p * 2 + f) * 2 + x] = x_t[p, f, x, at, :]
                buf[16 + p * 2 + x] = cy_t[p, x, at, :]
        buf[24] = h_t[at, :]


def x_edge(d, t, cx, left, right, xs, cy_t):
    ext = xs.shape[3]
    return call(
        x_edge_kernel,
        (out(*xs.shape), out(*xs.shape), out(ext, LANES), out(25, RIM, LANES), out(25, RIM, LANES)),
        (d, t, cx, left, right, xs, cy_t),
        "x_edge",
        scratch=[pltpu.VMEM((2, LANES, LANES), F32)] + EDGE_SCRATCH,
        aliases={5: 0},
    )[1:]


def rim_courant(x):
    return pltpu.roll(x, LANES - 32, 1)


def y_inner_kernel(x_t, cy_t, h_t, s_t, sh_t, a_scr, f_scr):
    planes = x_t.shape[0]
    rows = x_t.shape[3] - 2 * RIM

    def run(load_q, load_c, store):
        sweep_rows(load_q, load_c, store, a_scr, f_scr, RIM + 6, rows - 8, 32)

    def body(p, _):
        for x in range(2):

            def store(f, r, n, value):
                s_t[p, f, x, pl.ds(r, n), :] = value

            run(
                lambda f, r, n: x_t[p, f, x, pl.ds(r, n), :],
                lambda r, n: cy_t[p, x, pl.ds(r, n), :],
                store,
            )
        return 0

    lax.fori_loop(0, planes, body, 0, unroll=False)

    def store_rim(f, r, n, value):
        sh_t[pl.ds(r, n), :] = value

    sweep_rows(
        lambda f, r, n: h_t[pl.ds(r, n), :],
        lambda r, n: rim_courant(h_t[pl.ds(r, n), :]),
        store_rim,
        a_scr,
        f_scr,
        RIM + 6,
        rows - 8,
        32,
        fields=1,
    )


def y_inner(x_t, cy_t, h_t):
    ext = x_t.shape[3]
    return call(
        y_inner_kernel,
        (out(*x_t.shape), out(*h_t.shape)),
        (x_t, cy_t, h_t),
        "y_inner",
        scratch=[pltpu.VMEM((2, ext, LANES), F32)] * 2,
        cost=SWEEP_COST,
    )


def y_edge_kernel(
    x_t, cy_t, h_t, from_l, from_r, st_in, sh_in, s_t, sh_t, s, adv, rim_rows, win, a_scr, f_scr, res
):
    planes = x_t.shape[0]
    ext = x_t.shape[3]
    rows = ext - 2 * RIM

    for high in range(2):
        rim = from_r if high else from_l
        at = slice(ext - 24, ext - 8) if high else slice(8, 24)
        to = slice(ext - 16, ext) if high else slice(0, 16)
        got = slice(8, 24) if high else slice(0, 16)
        for p in range(planes):
            for x in range(2):
                edge_sweep(
                    lambda f: cy_t[p, x, at, :] if f == 2 else x_t[p, f, x, at, :],
                    lambda f: rim[16 + p * 2 + x] if f == 2 else rim[(p * 2 + f) * 2 + x],
                    high,
                    win,
                    a_scr,
                    f_scr,
                    res,
                )
                for f in range(2):
                    s_t[p, f, x, to, :] = res[f, got, :]
                    k = (f * 4 + p) * 8
                    if high:
                        rim_rows[x, k : k + 2, :] = res[f, 16:18, :]
                    else:
                        k = (k + LANES - 2) % LANES
                        rim_rows[x, k : k + 2, :] = res[f, 6:8, :]
        edge_sweep(
            lambda f: rim_courant(h_t[at, :]) if f == 2 else h_t[at, :],
            lambda f: rim_courant(rim[24]) if f == 2 else rim[24],
            high,
            win,
            a_scr,
            f_scr,
            res,
        )
        sh_t[to, :] = res[0, got, :]
    for x in range(2):
        s[16, half(x, RIM), :] = rim_rows[x].T
    for h in range(2):
        beyond = sh_t[half(h, RIM), :].T
        for p in range(planes):
            for f in range(2):
                k = (f * 4 + p) * 4
                i = (p * 2 + f) * 2 + h
                s[i, RIM - 2 : RIM, :] = beyond[k : k + 2, :]
                s[i, RIM + rows : RIM + rows + 2, :] = beyond[k + 2 : k + 4, :]
                for x in range(2):
                    block = s_t[p, f, x, half(h, RIM), :].T
                    s[i, half(x, RIM), :] = block
                    adv[f, p, half(x), half(h)] = block


def y_edge(x_t, cy_t, h_t, from_l, from_r, s_t, sh_t):
    planes, _, _, ext, _ = x_t.shape
    rows = ext - 2 * RIM
    res = call(
        y_edge_kernel,
        (
            out(*s_t.shape),
            out(*sh_t.shape),
            out(17, ext, LANES),
            out(2, planes, rows, 2 * LANES),
        ),
        (x_t, cy_t, h_t, from_l, from_r, s_t, sh_t),
        "y_edge",
        scratch=[pltpu.VMEM((2, LANES, LANES), F32)] + EDGE_SCRATCH,
        aliases={5: 0, 6: 1},
    )
    return res[0], res[2], res[3]


def slope(w1, w2):
    return (2.0 / 3.0) * w1 - (1.0 / 12.0) * w2


def rows_slope(ref, r, n):
    return slope(
        ref[pl.ds(r + 1, n), :] - ref[pl.ds(r - 1, n), :],
        ref[pl.ds(r + 2, n), :] - ref[pl.ds(r - 2, n), :],
    )


def own_slopes_kernel(s, s_t, gx, gy):
    planes, _, _, ext, _ = s_t.shape
    rows = ext - 2 * RIM

    def body(p, _):
        for f in range(2):
            for h in range(2):
                ref = s.at[(p * 2 + f) * 2 + h]
                for r in range(0, rows, 64):
                    gx[p, f, h, r : r + 64, :] = rows_slope(ref, RIM + r, 64)
                for x in range(2):
                    ref_t = s_t.at[p, f, x]
                    gy[p, f, h, half(x), :] = rows_slope(ref_t, RIM + h * LANES, LANES).T
        return 0

    lax.fori_loop(0, planes, body, 0, unroll=False)


def own_slopes(s, s_t):
    planes, _, _, ext, _ = s_t.shape
    shape = out(planes, 2, 2, ext - 2 * RIM, LANES)
    return call(own_slopes_kernel, (shape, shape), (s, s_t), "own_slopes", cost=SWEEP_COST)


def gradient_kernel(owner, core, own, other, own_x, own_y, grad, wedge):
    slot = pl.program_id(0)
    s = core[0]
    rank = jnp.int32(0)
    piece = jnp.int32(0)
    for j in range(NP):
        mine = owner[0, j] == s
        piece = jnp.where(jnp.logical_and(mine, rank == slot), j, piece)
        rank = rank + mine.astype(jnp.int32)
    used = slot < rank
    width = grad.shape[4]

    @pl.when(jnp.logical_not(used))
    def _():
        grad[...] = jnp.zeros_like(grad)
        wedge[...] = jnp.zeros_like(wedge)

    @pl.when(used)
    def _():
        n = 8
        lane = lane_iota(n)
        first = pl.multiple_of(piece * width, 8)

        def body(i, _):
            at = pl.multiple_of(first + i * n, n)
            r = pl.multiple_of(RIM + at, n)
            to = pl.ds(pl.multiple_of(i * n, n), n)
            rim = other[16, pl.ds(r, n), :]
            for h in range(2):

                def plane(z, f, row, hh=h):
                    ref = own if z < 4 else other
                    return ref[((z % 4) * 2 + f) * 2 + hh, pl.ds(row, n), :]

                q = [[plane(z, f, r) for f in range(2)] for z in range(8)]
                for z in range(8):
                    zo = lax.rem(z + 4 * s, 8)
                    g = []
                    for f in range(2):
                        if z < 4:
                            x_slope = own_x[z, f, h, pl.ds(at, n), :]
                            y_slope = own_y[z, f, h, pl.ds(at, n), :]
                        else:
                            here = q[z][f]
                            there = plane(z, f, r, 1 - h)
                            beyond = pltpu.roll(rim, (LANES - (f * 4 + z % 4) * 8) % LANES, 1)
                            after = beyond if h else there
                            before = there if h else beyond

                            def step(k):
                                up = pltpu.roll(jnp.where(lane < k, after, here), LANES - k, 1)
                                down = pltpu.roll(
                                    jnp.where(lane >= LANES - k, before, here), k, 1
                                )
                                return up - down

                            x_slope = slope(
                                plane(z, f, r + 1) - plane(z, f, r - 1),
                                plane(z, f, r + 2) - plane(z, f, r - 2),
                            )
                            y_slope = slope(step(1), step(2))
                        z_slope = slope(
                            q[(z + 1) % 8][f] - q[(z + 7) % 8][f],
                            q[(z + 2) % 8][f] - q[(z + 6) % 8][f],
                        )
                        g.append((x_slope, y_slope, z_slope))
                        for k in range(3):
                            grad[0, f, k, zo, to, half(h)] = g[-1][k]
                    rx, ry, rz = g[0]
                    tx, ty, tz = g[1]
                    a = ry * tz - rz * ty
                    b = rz * tx - rx * tz
                    c = rx * ty - ry * tx
                    wedge[0, zo, to, half(h)] = a * a + b * b + c * c
            return 0

        lax.fori_loop(0, width // n, body, 0, unroll=False)


def gradients_of(owner, core, own, other, own_x, own_y):
    rows = own.shape[1] - 2 * RIM
    width = rows // NP
    cols = 2 * LANES
    vmem = pl.BlockSpec(memory_space=pltpu.VMEM)
    return pl.pallas_call(
        gradient_kernel,
        grid_spec=pltpu.PrefetchScalarGridSpec(
            num_scalar_prefetch=2,
            grid=(CAP,),
            in_specs=[vmem] * 4,
            out_specs=(
                pl.BlockSpec((1, 2, 3, 8, width, cols), lambda k, o, c: (k, 0, 0, 0, 0, 0)),
                pl.BlockSpec((1, 8, width, cols), lambda k, o, c: (k, 0, 0, 0)),
            ),
        ),
        out_shape=(
            jax.ShapeDtypeStruct((CAP, 2, 3, 8, width, cols), F32),
            jax.ShapeDtypeStruct((CAP, 8, width, cols), F32),
        ),
        compiler_params=pltpu.CompilerParams(vmem_limit_bytes=20 * MIB),
        name="gradient",
    )(owner, core, own, other, own_x, own_y)


def per_device(density, heat, cx, cy, owner):
    nx, ny = lax.axis_size("gx"), lax.axis_size("gy")
    lo, hi = edge_rows((density, heat, cx, cy))
    left = lax.ppermute(hi, "gx", ring(nx, 1))
    right = lax.ppermute(lo, "gx", ring(nx, -1))
    xs, cy_t = x_inner(density, heat, cx, cy)
    x_t, h_t, to_l, to_r = x_edge(density, heat, cx, left, right, xs, cy_t)
    from_l = lax.ppermute(to_r, "gy", ring(ny, 1))
    from_r = lax.ppermute(to_l, "gy", ring(ny, -1))
    s_t, sh_t = y_inner(x_t, cy_t, h_t)
    s_t, swept, advected = y_edge(x_t, cy_t, h_t, from_l, from_r, s_t, sh_t)
    other = lax.ppermute(swept, "sa", ring(2, 1))
    own_x, own_y = own_slopes(swept, s_t)
    core = lax.axis_index("sa").astype(jnp.int32).reshape(1)
    gradients, wedge = gradients_of(owner, core, swept, other, own_x, own_y)
    return advected, gradients, wedge


def solution(mesh):
    block = P("sa", "gx", "gy")
    return jax.shard_map(
        per_device,
        mesh=mesh,
        in_specs=(block, block, block, block, P("gx", None)),
        out_specs=(
            P(None, "sa", "gx", "gy"),
            P(("gx", "sa"), None, None, None, None, "gy"),
            P(("gx", "sa"), None, None, "gy"),
        ),
        check_vma=False,
    )
```

```python
import jax
import jax.numpy as jnp
from jax import lax
from jax.experimental import pallas as pl
from jax.experimental.pallas import tpu as pltpu
from jax.sharding import PartitionSpec as P

CAP = 6
NP = 8
RIM = 8
LANES = 128
F32 = jnp.float32
MIB = 1024 * 1024


def ring(count, step):
    return [(i, (i + step) % count) for i in range(count)]


def coefficients(c):
    d = 1.0 - c
    m = c * d
    k_right = m * d
    k_left = m * c
    return k_right, k_left, c - k_right + k_left


def face_value(qm1, q0, q1, q2):
    return (7.0 / 12.0) * (q0 + q1) - (1.0 / 12.0) * (qm1 + q2)


def sweep_rows(load_q, load_c, store, a_scr, f_scr, base, count, chunk, fields=2):
    done = 0
    while done < count:
        n = min(chunk, count - done)
        r = base + done
        k_right, k_left, k_mid = coefficients(load_c(r, n))
        for f in range(fields):
            q0 = load_q(f, r, n)
            a = face_value(load_q(f, r - 1, n), q0, load_q(f, r + 1, n), load_q(f, r + 2, n))
            a_scr[f, pl.ds(8 + done, n), :] = a
            flux = k_right * a - k_left * a_scr[f, pl.ds(7 + done, n), :] + k_mid * q0
            f_scr[f, pl.ds(8 + done, n), :] = flux
            store(f, r, n, q0 - (flux - f_scr[f, pl.ds(7 + done, n), :]))
        done += n


def lane_iota(rows):
    return lax.broadcasted_iota(jnp.int32, (rows, LANES), 1)


def half(h, start=0):
    return slice(start + h * LANES, start + (h + 1) * LANES)


def call(
    kernel, out_shape, operands, name, spaces=None, scratch=(), aliases=None, cost=None, mib=20
):
    vmem = pl.BlockSpec(memory_space=pltpu.VMEM)
    return pl.pallas_call(
        kernel,
        in_specs=[pl.BlockSpec(memory_space=x) for x in spaces] if spaces else [vmem] * len(operands),
        out_specs=jax.tree.map(lambda _: vmem, out_shape),
        out_shape=out_shape,
        scratch_shapes=list(scratch),
        input_output_aliases=aliases or {},
        compiler_params=pltpu.CompilerParams(vmem_limit_bytes=mib * MIB),
        cost_estimate=cost,
        name=name,
    )(*operands)


def out(*shape):
    return jax.ShapeDtypeStruct(shape, F32)


SWEEP_COST = pl.CostEstimate(flops=20_000_000, bytes_accessed=6_000_000, transcendentals=0)


LAST = (5, 5, 3, 2)
FIRST = (4, 4, 2, 2)


def padded(rows):
    return -(-rows // 8) * 8


def place(counts, p, f):
    return p * sum(counts) + sum(counts[:f]), counts[f]


def edge_rows_kernel(d, t, cx, cy, lo, hi, first, last, sems):
    planes, rows, _ = d.shape
    copies = []
    for f, ref in enumerate((d, t, cx, cy)):
        copies.append(pltpu.make_async_copy(ref.at[:, 0:RIM, :], first.at[f], sems.at[f]))
        copies.append(
            pltpu.make_async_copy(ref.at[:, rows - RIM : rows, :], last.at[f], sems.at[4 + f])
        )
    for c in copies:
        c.start()
    for c in copies:
        c.wait()
    for p in range(planes):
        for f in range(4):
            at, n = place(FIRST, p, f)
            lo[at : at + n, :] = first[f, p, 0:n, :]
            at, n = place(LAST, p, f)
            hi[at : at + n, :] = last[f, p, RIM - n : RIM, :]


def edge_rows(fields):
    planes, _, cols = fields[0].shape
    tiles = pltpu.VMEM((4, planes, RIM, cols), F32)
    return call(
        edge_rows_kernel,
        (out(padded(planes * sum(FIRST)), cols), out(padded(planes * sum(LAST)), cols)),
        fields,
        "edge_rows",
        spaces=[pl.ANY] * 4,
        scratch=[tiles, tiles, pltpu.SemaphoreType.DMA((8,))],
        mib=56,
    )


def x_inner_kernel(d, t, cx, cy, xs, cy_t, win, a_scr, f_scr):
    planes, rows, _ = d.shape

    def body(p, _):
        for h in range(2):
            for f, ref in enumerate((d, t, cx)):
                win[f, 0:rows, :] = ref[p, :, half(h)]

            def store(f, r, n, value):
                xs[p, f, h, pl.ds(RIM + r, n), :] = value

            sweep_rows(
                lambda f, r, n: win[f, pl.ds(r, n), :],
                lambda r, n: win[2, pl.ds(r, n), :],
                store,
                a_scr,
                f_scr,
                6,
                rows - 8,
                32,
            )
            for x in range(2):
                cy_t[p, x, half(h, RIM), :] = cy[p, half(x), half(h)].T
        return 0

    lax.fori_loop(0, planes, body, 0, unroll=False)


def x_inner(d, t, cx, cy):
    planes, rows, cols = d.shape
    ext = rows + 2 * RIM
    return call(
        x_inner_kernel,
        (out(planes, 2, 2, ext, LANES), out(planes, 2, ext, LANES)),
        (d, t, cx, cy),
        "x_inner",
        scratch=[pltpu.VMEM((3, ext, LANES), F32)] + [pltpu.VMEM((2, ext, LANES), F32)] * 2,
        cost=SWEEP_COST,
    )


def edge_sweep(own, rim, high, win, a_scr, f_scr, res):
    lead, rim_at = (0, 16) if high else (8, 0)
    for f in range(3):
        win[f, lead : lead + 16, :] = own(f)
        beyond = rim(f)
        if beyond is not None:
            n = beyond.shape[0]
            at = rim_at if high else 8 - n
            win[f, at : at + n, :] = beyond

    def store(f, r, n, value):
        res[f, pl.ds(r, n), :] = value

    sweep_rows(
        lambda f, r, n: win[f, pl.ds(r, n), :],
        lambda r, n: win[2, pl.ds(r, n), :],
        store,
        a_scr,
        f_scr,
        6 if high else 4,
        16,
        16,
    )


EDGE_SCRATCH = [
    pltpu.VMEM((3, 32, LANES), F32),
    pltpu.VMEM((2, 32, LANES), F32),
    pltpu.VMEM((2, 32, LANES), F32),
    pltpu.VMEM((2, 32, LANES), F32),
]


def x_edge_kernel(
    d, t, cx, left, right, xs_in, cy_t, xs, x_t, h_t, to_l, to_r, rim_rows, win, a_scr, f_scr, res
):
    planes, rows, _ = d.shape
    ext = rows + 2 * RIM

    for p in range(planes):
        for h in range(2):
            for high in range(2):
                rim, counts = (right, FIRST) if high else (left, LAST)
                at = slice(rows - 16, rows) if high else slice(0, 16)

                def beyond(f):
                    r, n = place(counts, p, f)
                    return rim[r : r + n, half(h)]

                edge_sweep(
                    lambda f: (d, t, cx)[f][p, at, half(h)],
                    beyond,
                    high,
                    win,
                    a_scr,
                    f_scr,
                    res,
                )
                for f in range(2):
                    k = (f * 4 + p) * 4 + 2 * high
                    if high:
                        xs[p, f, h, rows : rows + RIM, :] = res[f, 8:16, :]
                        rim_rows[h, k : k + 2, :] = res[f, 16:18, :]
                        rim_rows[h, 32 + k : 34 + k, :] = beyond(3)
                    else:
                        xs[p, f, h, RIM : 2 * RIM, :] = res[f, 8:16, :]
                        rim_rows[h, k : k + 2, :] = res[f, 6:8, :]
                        rim_rows[h, 32 + k : 34 + k, :] = beyond(3)
    for h in range(2):
        h_t[half(h, RIM), :] = rim_rows[h].T
    for p in range(planes):
        for f in range(2):
            for x in range(2):
                for h in range(2):
                    x_t[p, f, x, half(h, RIM), :] = xs[p, f, h, half(x, RIM), :].T
    for buf, counts in ((to_l, FIRST), (to_r, LAST)):

        def put(i, f, ref):
            at, n = y_place(counts, i, f)
            top = RIM if counts is FIRST else RIM + rows - n
            buf[at : at + n, :] = ref[top : top + n, :]

        for p in range(planes):
            for x in range(2):
                for f in range(2):
                    put((p * 2 + f) * 2 + x, 0, x_t.at[p, f, x])
                put(p * 2 + x, 2, cy_t.at[p, x])
        put(16, 0, h_t)


def y_place(counts, i, f):
    return (17 * counts[0] if f == 2 else 0) + i * counts[f], counts[f]


def y_rim(counts):
    return out(padded(17 * counts[0] + 8 * counts[2]), LANES)


def x_edge(d, t, cx, left, right, xs, cy_t):
    ext = xs.shape[3]
    return call(
        x_edge_kernel,
        (out(*xs.shape), out(*xs.shape), out(ext, LANES), y_rim(FIRST), y_rim(LAST)),
        (d, t, cx, left, right, xs, cy_t),
        "x_edge",
        scratch=[pltpu.VMEM((2, LANES, LANES), F32)] + EDGE_SCRATCH,
        aliases={5: 0},
    )[1:]


def rim_courant(x):
    return pltpu.roll(x, LANES - 32, 1)


def y_inner_kernel(x_t, cy_t, h_t, s_t, sh_t, a_scr, f_scr):
    planes = x_t.shape[0]
    rows = x_t.shape[3] - 2 * RIM

    def run(load_q, load_c, store):
        sweep_rows(load_q, load_c, store, a_scr, f_scr, RIM + 6, rows - 8, 32)

    def body(p, _):
        for x in range(2):

            def store(f, r, n, value):
                s_t[p, f, x, pl.ds(r, n), :] = value

            run(
                lambda f, r, n: x_t[p, f, x, pl.ds(r, n), :],
                lambda r, n: cy_t[p, x, pl.ds(r, n), :],
                store,
            )
        return 0

    lax.fori_loop(0, planes, body, 0, unroll=False)

    def store_rim(f, r, n, value):
        sh_t[pl.ds(r, n), :] = value

    sweep_rows(
        lambda f, r, n: h_t[pl.ds(r, n), :],
        lambda r, n: rim_courant(h_t[pl.ds(r, n), :]),
        store_rim,
        a_scr,
        f_scr,
        RIM + 6,
        rows - 8,
        32,
        fields=1,
    )


def y_inner(x_t, cy_t, h_t):
    ext = x_t.shape[3]
    return call(
        y_inner_kernel,
        (out(*x_t.shape), out(*h_t.shape)),
        (x_t, cy_t, h_t),
        "y_inner",
        scratch=[pltpu.VMEM((2, ext, LANES), F32)] * 2,
        cost=SWEEP_COST,
    )


def y_edge_kernel(
    x_t, cy_t, h_t, from_l, from_r, st_in, sh_in, s_t, sh_t, s, rim_rows, win, a_scr, f_scr, res
):
    planes = x_t.shape[0]
    ext = x_t.shape[3]
    rows = ext - 2 * RIM

    for high in range(2):
        rim, counts = (from_r, FIRST) if high else (from_l, LAST)

        def beyond(i, f):
            r, n = y_place(counts, i, f)
            return rim[r : r + n, :]

        at = slice(ext - 24, ext - 8) if high else slice(8, 24)
        to = slice(ext - 16, ext) if high else slice(0, 16)
        got = slice(8, 24) if high else slice(0, 16)
        for p in range(planes):
            for x in range(2):
                edge_sweep(
                    lambda f: cy_t[p, x, at, :] if f == 2 else x_t[p, f, x, at, :],
                    lambda f: beyond(p * 2 + x if f == 2 else (p * 2 + f) * 2 + x, f),
                    high,
                    win,
                    a_scr,
                    f_scr,
                    res,
                )
                for f in range(2):
                    s_t[p, f, x, to, :] = res[f, got, :]
                    k = (f * 4 + p) * 8
                    if high:
                        k = (k + LANES - 2) % LANES
                        rim_rows[x, k : k + 2, :] = rows_slope(s_t.at[p, f, x], ext - 16, 8)[6:8]
                    else:
                        rim_rows[x, k : k + 2, :] = rows_slope(s_t.at[p, f, x], 8, 8)[0:2]
        edge_sweep(
            lambda f: rim_courant(h_t[at, :]) if f == 2 else h_t[at, :],
            lambda f: rim_courant(beyond(16, 0)) if f == 2 else beyond(16, 0),
            high,
            win,
            a_scr,
            f_scr,
            res,
        )
        sh_t[to, :] = res[0, got, :]
    for x in range(2):
        s[16, half(x, RIM), :] = rim_rows[x].T
    for h in range(2):
        beyond = sh_t[half(h, RIM), :].T
        for p in range(planes):
            for f in range(2):
                k = (f * 4 + p) * 4
                i = (p * 2 + f) * 2 + h
                s[i, RIM - 2 : RIM, :] = beyond[k : k + 2, :]
                s[i, RIM + rows : RIM + rows + 2, :] = beyond[k + 2 : k + 4, :]
                for x in range(2):
                    s[i, half(x, RIM), :] = s_t[p, f, x, half(h, RIM), :].T


def y_edge(x_t, cy_t, h_t, from_l, from_r, s_t, sh_t):
    ext = x_t.shape[3]
    res = call(
        y_edge_kernel,
        (
            out(*s_t.shape),
            out(*sh_t.shape),
            out(17, ext, LANES),
        ),
        (x_t, cy_t, h_t, from_l, from_r, s_t, sh_t),
        "y_edge",
        scratch=[pltpu.VMEM((2, LANES, LANES), F32)] + EDGE_SCRATCH,
        aliases={5: 0, 6: 1},
    )
    return res[2]


def slope(w1, w2):
    return (2.0 / 3.0) * w1 - (1.0 / 12.0) * w2


def rows_slope(ref, r, n):
    return slope(
        ref[pl.ds(r + 1, n), :] - ref[pl.ds(r - 1, n), :],
        ref[pl.ds(r + 2, n), :] - ref[pl.ds(r - 2, n), :],
    )


def columns_slope(pair, turned, store):
    for h in range(2):
        turned[half(h, RIM), :] = pair(h).T
    for h in range(2):
        store(h, rows_slope(turned, RIM + h * LANES, LANES).T)


def edge_columns(strips, k):
    return pltpu.roll(strips, LANES - k * 8, 1)


def with_edge(value, edge, h, lane):
    return jnp.where(lane >= LANES - 2 if h else lane < 2, edge, value)


def piece_of(owner, core, slot):
    rank = jnp.int32(0)
    piece = jnp.int32(0)
    for j in range(NP):
        mine = owner[0, j] == core
        piece = jnp.where(jnp.logical_and(mine, rank == slot), j, piece)
        rank = rank + mine.astype(jnp.int32)
    return piece, slot < rank


def own_slopes_kernel(owner, core, s, adv, grad, own, zeros, turned, adv_sem, sems):
    planes, rows = adv.shape[1:3]
    width = grad.shape[4]
    me = core[0]
    copies = []
    for p in range(planes):
        for f in range(2):
            for h in range(2):
                i = (p * 2 + f) * 2 + h
                copies.append(
                    pltpu.make_async_copy(
                        s.at[i, RIM : RIM + rows, :], adv.at[f, p, :, half(h)], adv_sem.at[i]
                    )
                )
    for c in copies:
        c.start()
    zeros[...] = jnp.zeros_like(zeros)
    mine = pl.ds(pl.multiple_of(planes * me, planes), planes)

    def send(k, f):
        for slot in range(CAP):
            piece, used = piece_of(owner, me, slot)
            to = grad.at[slot, f, k, mine]
            sem = sems.at[slot, f, k]

            @pl.when(used)
            def _():
                at = pl.ds(pl.multiple_of(piece * width, width), width)
                pltpu.make_async_copy(own.at[k, f, :, at, :], to, sem).start()

            @pl.when(jnp.logical_not(used))
            def _():
                pltpu.make_async_copy(zeros, to, sem).start()

    for f in range(2):

        def x_body(p, _):
            for h in range(2):
                ref = s.at[(p * 2 + f) * 2 + h]
                for r in range(0, rows, 64):
                    own[0, f, p, r : r + 64, half(h)] = rows_slope(ref, RIM + r, 64)
            return 0

        lax.fori_loop(0, planes, x_body, 0, unroll=False)
        send(0, f)
    n = 8
    lane = lane_iota(n)
    for f in range(2):

        def y_body(p, _):
            for x in range(2):

                def pair(h):
                    return s[(p * 2 + f) * 2 + h, half(x, RIM), :]

                def store(h, y):
                    own[1, f, p, half(x), half(h)] = y

                columns_slope(pair, turned.at[x], store)
            strip = f * 4 + p
            for r in range(0, rows, n):
                edge = edge_columns(s[16, RIM + r : RIM + r + n, :], strip)
                for h in range(2):
                    at = own.at[1, f, p, r : r + n, half(h)]
                    at[...] = with_edge(at[...], edge, h, lane)
            return 0

        lax.fori_loop(0, planes, y_body, 0, unroll=False)
        send(1, f)
    for c in copies:
        c.wait()
    for slot in range(CAP):
        for f in range(2):
            for k in range(2):
                pltpu.make_async_copy(zeros, grad.at[slot, f, k, mine], sems.at[slot, f, k]).wait()


SMEM = pl.BlockSpec(memory_space=pltpu.SMEM)
VMEM = pl.BlockSpec(memory_space=pltpu.VMEM)
ANY = pl.BlockSpec(memory_space=pl.ANY)


def own_slopes(owner, core, s):
    planes = (s.shape[0] - 1) // 4
    rows = s.shape[1] - 2 * RIM
    cols = 2 * LANES
    width = rows // NP
    return pl.pallas_call(
        own_slopes_kernel,
        in_specs=[SMEM, SMEM, VMEM],
        out_specs=(ANY, ANY, VMEM),
        out_shape=(
            out(2, planes, rows, cols),
            out(CAP, 2, 3, 2 * planes, width, cols),
            out(2, 2, planes, rows, cols),
        ),
        scratch_shapes=[
            pltpu.VMEM((planes, width, cols), F32),
            pltpu.VMEM((2, rows + 2 * RIM, LANES), F32),
            pltpu.SemaphoreType.DMA((16,)),
            pltpu.SemaphoreType.DMA((CAP, 2, 2)),
        ],
        compiler_params=pltpu.CompilerParams(vmem_limit_bytes=20 * MIB),
        cost_estimate=SWEEP_COST,
        name="own_slopes",
    )(owner, core, s)


def gradient_kernel(
    owner, core, own, other, own_xy, grad_in, grad, wedge, part, wpart, turned, zeros, sems, wsems
):
    planes = own_xy.shape[2]
    width = grad.shape[4]
    me = core[0]
    mine = pl.ds(pl.multiple_of(planes * me, planes), planes)
    theirs = pl.ds(pl.multiple_of(planes * (1 - me), planes), planes)
    kinds = ((2, mine), (2, theirs), (0, theirs), (1, theirs))

    def copies(slot, used=True):
        res = []
        for f in range(2):
            for k, (dim, where) in enumerate(kinds):
                src = part.at[slot, f, k] if used else zeros
                res.append(
                    pltpu.make_async_copy(src, grad.at[slot, f, dim, where], sems.at[slot, f, k])
                )
        for k, where in enumerate((mine, theirs)):
            src = wpart.at[slot, k] if used else zeros
            res.append(pltpu.make_async_copy(src, wedge.at[slot, where], wsems.at[slot, k]))
        return res

    def fill(slot, piece):
        n = 8
        lane = lane_iota(n)
        first = pl.multiple_of(piece * width, 8)

        for f in range(2):

            def pair(h):
                at = pl.ds(first + RIM, width)
                return jnp.concatenate(
                    [other[(p * 2 + f) * 2 + h, at, :] for p in range(planes)], axis=0
                )

            def store(h, y):
                for p in range(planes):
                    part[slot, f, 3, p, :, half(h)] = y[p * width : (p + 1) * width, :]

            columns_slope(pair, turned.at[f], store)

        def body(i, _):
            at = pl.multiple_of(first + i * n, n)
            r = pl.multiple_of(RIM + at, n)
            to = pl.ds(pl.multiple_of(i * n, n), n)
            strips = other[16, pl.ds(r, n), :]
            edges = [edge_columns(strips, k) for k in range(2 * planes)]
            for h in range(2):
                cols = half(h)

                def plane(z, f, row):
                    ref = own if z < planes else other
                    return ref[((z % planes) * 2 + f) * 2 + h, pl.ds(row, n), :]

                q = [[plane(z, f, r) for f in range(2)] for z in range(8)]
                for z in range(8):
                    g = []
                    p = z % planes
                    for f in range(2):
                        z_slope = slope(
                            q[(z + 1) % 8][f] - q[(z + 7) % 8][f],
                            q[(z + 2) % 8][f] - q[(z + 6) % 8][f],
                        )
                        part[slot, f, z // planes, p, to, cols] = z_slope
                        if z < planes:
                            x_slope = own_xy[0, f, p, pl.ds(at, n), cols]
                            y_slope = own_xy[1, f, p, pl.ds(at, n), cols]
                        else:
                            x_slope = slope(
                                plane(z, f, r + 1) - plane(z, f, r - 1),
                                plane(z, f, r + 2) - plane(z, f, r - 2),
                            )
                            part[slot, f, 2, p, to, cols] = x_slope
                            y_slope = with_edge(
                                part[slot, f, 3, p, to, cols], edges[f * 4 + p], h, lane
                            )
                            part[slot, f, 3, p, to, cols] = y_slope
                        g.append((x_slope, y_slope, z_slope))
                    rx, ry, rz = g[0]
                    tx, ty, tz = g[1]
                    a = ry * tz - rz * ty
                    b = rz * tx - rx * tz
                    c = rx * ty - ry * tx
                    wpart[slot, z // planes, p, to, cols] = a * a + b * b + c * c
            return 0

        lax.fori_loop(0, width // n, body, 0, unroll=False)

    def slot_body(slot, _):
        piece, used = piece_of(owner, me, slot)

        @pl.when(used)
        def _():
            fill(slot, piece)
            for c in copies(slot):
                c.start()

        @pl.when(jnp.logical_not(used))
        def _():
            for c in copies(slot, False):
                c.start()

        return 0

    zeros[...] = jnp.zeros_like(zeros)
    lax.fori_loop(0, CAP, slot_body, 0, unroll=False)

    def wait_body(slot, _):
        for c in copies(slot):
            c.wait()
        return 0

    lax.fori_loop(0, CAP, wait_body, 0, unroll=False)


def gradients_of(owner, core, own, other, own_xy, grad):
    _, _, planes, rows, cols = own_xy.shape
    width = rows // NP
    return pl.pallas_call(
        gradient_kernel,
        in_specs=[SMEM, SMEM, VMEM, VMEM, VMEM, ANY],
        out_specs=(ANY, ANY),
        out_shape=(out(*grad.shape), out(CAP, 2 * planes, width, cols)),
        scratch_shapes=[
            pltpu.VMEM((CAP, 2, 4, planes, width, cols), F32),
            pltpu.VMEM((CAP, 2, planes, width, cols), F32),
            pltpu.VMEM((2, rows + 2 * RIM, LANES), F32),
            pltpu.VMEM((planes, width, cols), F32),
            pltpu.SemaphoreType.DMA((CAP, 2, 4)),
            pltpu.SemaphoreType.DMA((CAP, 2)),
        ],
        input_output_aliases={5: 0},
        compiler_params=pltpu.CompilerParams(vmem_limit_bytes=24 * MIB),
        name="gradient",
    )(owner, core, own, other, own_xy, grad)


def per_device(density, heat, cx, cy, owner):
    nx, ny = lax.axis_size("gx"), lax.axis_size("gy")
    lo, hi = edge_rows((density, heat, cx, cy))
    left = lax.ppermute(hi, "gx", ring(nx, 1))
    right = lax.ppermute(lo, "gx", ring(nx, -1))
    xs, cy_t = x_inner(density, heat, cx, cy)
    x_t, h_t, to_l, to_r = x_edge(density, heat, cx, left, right, xs, cy_t)
    from_l = lax.ppermute(to_r, "gy", ring(ny, 1))
    from_r = lax.ppermute(to_l, "gy", ring(ny, -1))
    s_t, sh_t = y_inner(x_t, cy_t, h_t)
    swept = y_edge(x_t, cy_t, h_t, from_l, from_r, s_t, sh_t)
    other = lax.ppermute(swept, "sa", ring(2, 1))
    core = lax.axis_index("sa").astype(jnp.int32).reshape(1)
    advected, gradients, own_xy = own_slopes(owner, core, swept)
    gradients, wedge = gradients_of(owner, core, swept, other, own_xy, gradients)
    return advected, gradients, wedge


def solution(mesh):
    block = P("sa", "gx", "gy")
    return jax.shard_map(
        per_device,
        mesh=mesh,
        in_specs=(block, block, block, block, P("gx", None)),
        out_specs=(
            P(None, "sa", "gx", "gy"),
            P(("gx", "sa"), None, None, None, None, "gy"),
            P(("gx", "sa"), None, None, "gy"),
        ),
        check_vma=False,
    )
```

```python
import jax
import jax.numpy as jnp
from jax import lax
from jax.experimental import pallas as pl
from jax.experimental.pallas import tpu as pltpu
from jax.sharding import PartitionSpec as P

CAP = 6
NP = 8
RIM = 8
LANES = 128
F32 = jnp.float32
MIB = 1024 * 1024


def ring(count, step):
    return [(i, (i + step) % count) for i in range(count)]


def coefficients(c):
    d = 1.0 - c
    m = c * d
    k_right = m * d
    k_left = m * c
    return k_right, k_left, c - k_right + k_left


def face_value(qm1, q0, q1, q2):
    return (7.0 / 12.0) * (q0 + q1) - (1.0 / 12.0) * (qm1 + q2)


def sweep_rows(load_q, load_c, store, a_scr, f_scr, base, count, chunk, fields=2):
    done = 0
    while done < count:
        n = min(chunk, count - done)
        r = base + done
        k_right, k_left, k_mid = coefficients(load_c(r, n))
        for f in range(fields):
            q0 = load_q(f, r, n)
            a = face_value(load_q(f, r - 1, n), q0, load_q(f, r + 1, n), load_q(f, r + 2, n))
            a_scr[f, pl.ds(8 + done, n), :] = a
            flux = k_right * a - k_left * a_scr[f, pl.ds(7 + done, n), :] + k_mid * q0
            f_scr[f, pl.ds(8 + done, n), :] = flux
            store(f, r, n, q0 - (flux - f_scr[f, pl.ds(7 + done, n), :]))
        done += n


def lane_iota(rows):
    return lax.broadcasted_iota(jnp.int32, (rows, LANES), 1)


def half(h, start=0):
    return slice(start + h * LANES, start + (h + 1) * LANES)


def call(
    kernel, out_shape, operands, name, spaces=None, scratch=(), aliases=None, cost=None, mib=20,
    out_spaces=None,
):
    vmem = pl.BlockSpec(memory_space=pltpu.VMEM)
    return pl.pallas_call(
        kernel,
        in_specs=[pl.BlockSpec(memory_space=x) for x in spaces] if spaces else [vmem] * len(operands),
        out_specs=tuple(pl.BlockSpec(memory_space=x) for x in out_spaces)
        if out_spaces
        else jax.tree.map(lambda _: vmem, out_shape),
        out_shape=tuple(
            x if space is pl.ANY else pltpu.VMEM(x.shape, F32)
            for x, space in zip(out_shape, out_spaces or [None] * len(out_shape))
        ),
        scratch_shapes=list(scratch),
        input_output_aliases=aliases or {},
        compiler_params=pltpu.CompilerParams(vmem_limit_bytes=mib * MIB),
        cost_estimate=cost,
        name=name,
    )(*operands)


def out(*shape):
    return jax.ShapeDtypeStruct(shape, F32)


SWEEP_COST = pl.CostEstimate(flops=20_000_000, bytes_accessed=6_000_000, transcendentals=0)


LAST = (5, 5, 3, 2)
FIRST = (4, 4, 2, 2)


def padded(rows):
    return -(-rows // 8) * 8


def place(counts, p, f):
    return p * sum(counts) + sum(counts[:f]), counts[f]


def edge_rows_kernel(d, t, cx, cy, lo, hi, first, last, sems):
    planes, rows, _ = d.shape
    copies = []
    for f, ref in enumerate((d, t, cx, cy)):
        copies.append(pltpu.make_async_copy(ref.at[:, 0:RIM, :], first.at[f], sems.at[f]))
        copies.append(
            pltpu.make_async_copy(ref.at[:, rows - RIM : rows, :], last.at[f], sems.at[4 + f])
        )
    for c in copies:
        c.start()
    for c in copies:
        c.wait()
    for p in range(planes):
        for f in range(4):
            at, n = place(FIRST, p, f)
            lo[at : at + n, :] = first[f, p, 0:n, :]
            at, n = place(LAST, p, f)
            hi[at : at + n, :] = last[f, p, RIM - n : RIM, :]


def edge_rows(fields):
    planes, _, cols = fields[0].shape
    tiles = pltpu.VMEM((4, planes, RIM, cols), F32)
    return call(
        edge_rows_kernel,
        (out(padded(planes * sum(FIRST)), cols), out(padded(planes * sum(LAST)), cols)),
        [pltpu.with_memory_space_constraint(x, pltpu.HBM) for x in fields],
        "edge_rows",
        spaces=[pl.ANY] * 4,
        scratch=[tiles, tiles, pltpu.SemaphoreType.DMA((8,))],
        mib=8,
    )


def inner_kernel(d, t, cx, cy, x_e, cy_e, s_t, s, win, xs, x_t, cy_t, a_scr, f_scr):
    planes, rows, _ = d.shape

    def body(p, _):
        for h in range(2):
            for f, ref in enumerate((d, t, cx)):
                win[f, 0:rows, :] = ref[p, :, half(h)]

            def store(f, r, n, value):
                xs[f, h, pl.ds(RIM + r, n), :] = value

            sweep_rows(
                lambda f, r, n: win[f, pl.ds(r, n), :],
                lambda r, n: win[2, pl.ds(r, n), :],
                store,
                a_scr,
                f_scr,
                1,
                rows,
                32,
            )
            for x in range(2):
                cy_t[x, half(h, RIM), :] = cy[p, half(x), half(h)].T
        for x in range(2):
            for f in range(2):
                for h in range(2):
                    x_t[f, x, half(h, RIM), :] = xs[f, h, half(x, RIM), :].T

            def store_t(f, r, n, value):
                s_t[p, f, x, pl.ds(r, n), :] = value

            sweep_rows(
                lambda f, r, n: x_t[f, x, pl.ds(r, n), :],
                lambda r, n: cy_t[x, pl.ds(r, n), :],
                store_t,
                a_scr,
                f_scr,
                RIM + 1,
                rows,
                32,
            )
            for f in range(2):
                for h in range(2):
                    s[(p * 2 + f) * 2 + h, half(x, RIM), :] = s_t[p, f, x, half(h, RIM), :].T
            for high, at in enumerate((slice(RIM, 16 + RIM), slice(rows + RIM - 16, rows + RIM))):
                cy_e[high, p, x] = cy_t[x, at, :]
                for f in range(2):
                    x_e[high, p, f, x] = x_t[f, x, at, :]
        return 0

    lax.fori_loop(0, planes, body, 0, unroll=False)


def inner(d, t, cx, cy):
    planes, rows, cols = d.shape
    ext = rows + 2 * RIM
    return call(
        inner_kernel,
        (
            out(2, planes, 2, 2, 16, LANES),
            out(2, planes, 2, 16, LANES),
            out(planes, 2, 2, ext, LANES),
            out(4 * planes, ext, LANES),
        ),
        (d, t, cx, cy),
        "inner",
        scratch=[pltpu.VMEM((3, ext, LANES), F32)]
        + [pltpu.VMEM((2, 2, ext, LANES), F32)] * 2
        + [pltpu.VMEM((2, ext, LANES), F32)]
        + [pltpu.VMEM((2, ext, LANES), F32)] * 2,
        cost=SWEEP_COST,
        mib=16,
    )


def edge_sweep(own, rim, high, win, a_scr, f_scr, res):
    lead, rim_at = (0, 16) if high else (8, 0)
    for f in range(3):
        win[f, lead : lead + 16, :] = own(f)
        beyond = rim(f)
        if beyond is not None:
            n = beyond.shape[0]
            at = rim_at if high else 8 - n
            win[f, at : at + n, :] = beyond

    def store(f, r, n, value):
        res[f, pl.ds(r, n), :] = value

    sweep_rows(
        lambda f, r, n: win[f, pl.ds(r, n), :],
        lambda r, n: win[2, pl.ds(r, n), :],
        store,
        a_scr,
        f_scr,
        6 if high else 4,
        16,
        16,
    )


EDGE_SCRATCH = [
    pltpu.VMEM((3, 32, LANES), F32),
    pltpu.VMEM((2, 32, LANES), F32),
    pltpu.VMEM((2, 32, LANES), F32),
    pltpu.VMEM((2, 32, LANES), F32),
]


STRIP = 16
EDGE = 5


def x_edge_kernel(
    d,
    t,
    cx,
    cy,
    left,
    right,
    x_e,
    cy_e,
    s_in,
    h_t,
    hc_t,
    to_l,
    to_r,
    s,
    q_rows,
    c_rows,
    win,
    a_scr,
    f_scr,
    res,
):
    del s_in, s
    planes, rows, _ = d.shape

    for p in range(planes):
        for h in range(2):
            for high in range(2):
                rim, counts = (right, FIRST) if high else (left, LAST)
                at = slice(rows - 16, rows) if high else slice(0, 16)

                def beyond(f):
                    r, n = place(counts, p, f)
                    return rim[r : r + n, half(h)]

                edge_sweep(
                    lambda f: (d, t, cx)[f][p, at, half(h)],
                    beyond,
                    high,
                    win,
                    a_scr,
                    f_scr,
                    res,
                )
                for f in range(2):
                    k = (f * 4 + p) * STRIP + EDGE * high
                    if high:
                        q_rows[h, k : k + EDGE, :] = res[f, 13:18, :]
                        c_rows[h, k : k + 3, :] = cy[p, rows - 3 : rows, half(h)]
                        c_rows[h, k + 3 : k + EDGE, :] = beyond(3)
                    else:
                        q_rows[h, k : k + EDGE, :] = res[f, 6:11, :]
                        c_rows[h, k : k + 2, :] = beyond(3)
                        c_rows[h, k + 2 : k + EDGE, :] = cy[p, 0:3, half(h)]
    for h in range(2):
        h_t[half(h, RIM), :] = q_rows[h].T
        hc_t[half(h, RIM), :] = c_rows[h].T
    for buf, counts in ((to_l, FIRST), (to_r, LAST)):

        last = counts is LAST

        def put(i, f, ref, start, stop):
            at, n = y_place(counts, i, f)
            top = stop - n if last else start
            buf[at : at + n, :] = ref[top : top + n, :]

        for p in range(planes):
            for x in range(2):
                for f in range(2):
                    put((p * 2 + f) * 2 + x, 0, x_e.at[int(last), p, f, x], 0, 16)
                put(p * 2 + x, 2, cy_e.at[int(last), p, x], 0, 16)
        put(16, 0, h_t, RIM, RIM + rows)
        put(8, 2, hc_t, RIM, RIM + rows)


def y_place(counts, i, f):
    return (17 * counts[0] if f == 2 else 0) + i * counts[f], counts[f]


def y_rim(counts):
    return out(padded(17 * counts[0] + 9 * counts[2]), LANES)


def x_edge(d, t, cx, cy, left, right, x_e, cy_e, s):
    ext = s.shape[1]
    return call(
        x_edge_kernel,
        (out(ext, LANES), out(ext, LANES), y_rim(FIRST), y_rim(LAST), out(*s.shape)),
        (d, t, cx, cy, left, right, x_e, cy_e, s),
        "x_edge",
        mib=12,
        scratch=[pltpu.VMEM((2, LANES, LANES), F32)] * 2 + EDGE_SCRATCH,
        spaces=[pltpu.VMEM] * 8 + [pl.ANY],
        out_spaces=[pltpu.VMEM] * 4 + [pl.ANY],
        aliases={8: 4},
    )


def slope(w1, w2):
    return (2.0 / 3.0) * w1 - (1.0 / 12.0) * w2


def rows_slope(ref, r, n):
    return slope(
        ref[pl.ds(r + 1, n), :] - ref[pl.ds(r - 1, n), :],
        ref[pl.ds(r + 2, n), :] - ref[pl.ds(r - 2, n), :],
    )


def inner_slopes_kernel(s_t, h_t, hc_t, sh_t, gy_out, gy, a_scr, f_scr, sems):
    planes, _, _, ext, _ = s_t.shape
    rows = ext - 2 * RIM

    def copy(p):
        at = pl.ds(p * 4, 4)
        return pltpu.make_async_copy(gy.at[at], gy_out.at[at], sems.at[p])

    def body(p, _):
        for f in range(2):
            for x in range(2):
                for h in range(2):
                    gy[(p * 2 + f) * 2 + h, half(x), :] = rows_slope(
                        s_t.at[p, f, x], RIM + h * LANES, LANES
                    ).T
        copy(p).start()
        return 0

    lax.fori_loop(0, planes, body, 0, unroll=False)

    def store(f, r, n, value):
        sh_t[pl.ds(r, n), :] = value

    sweep_rows(
        lambda f, r, n: h_t[pl.ds(r, n), :],
        lambda r, n: hc_t[pl.ds(r, n), :],
        store,
        a_scr,
        f_scr,
        RIM + 1,
        rows,
        32,
        fields=1,
    )
    for p in range(planes):
        copy(p).wait()


def inner_slopes(s_t, h_t, hc_t):
    planes, _, _, ext, _ = s_t.shape
    return call(
        inner_slopes_kernel,
        (out(ext, LANES), out(4 * planes, ext - 2 * RIM, LANES)),
        (s_t, h_t, hc_t),
        "inner_slopes",
        mib=8,
        scratch=[pltpu.VMEM((4 * planes, ext - 2 * RIM, LANES), F32)]
        + [pltpu.VMEM((2, ext, LANES), F32)] * 2
        + [pltpu.SemaphoreType.DMA((planes,))],
        out_spaces=[pltpu.VMEM, pl.ANY],
        cost=SWEEP_COST,
    )


VALUES_AT = 2
SLOPES_AT = 9


def y_edge_kernel(
    x_e,
    cy_e,
    h_t,
    hc_t,
    from_l,
    from_r,
    sh_in,
    gy_in,
    sh_t,
    edges,
    gy,
    strips,
    win,
    a_scr,
    f_scr,
    res,
):
    del gy_in, gy
    planes = x_e.shape[1]
    ext = h_t.shape[0]

    for high in range(2):
        rim, counts = (from_r, FIRST) if high else (from_l, LAST)
        at = slice(ext - 24, ext - 8) if high else slice(8, 24)

        def beyond(i, f):
            r, n = y_place(counts, i, f)
            return rim[r : r + n, :]

        for p in range(planes):
            for x in range(2):
                edge_sweep(
                    lambda f: cy_e[high, p, x] if f == 2 else x_e[high, p, f, x],
                    lambda f: beyond(p * 2 + x if f == 2 else (p * 2 + f) * 2 + x, f),
                    high,
                    win,
                    a_scr,
                    f_scr,
                    res,
                )
                for f in range(2):
                    k = (f * 4 + p) * STRIP
                    slopes = rows_slope(res.at[f], 8, 8)
                    if high:
                        strips[x, k : k + 2, :] = res[f, 14:16, :]
                        strips[x, k + 5 : k + 9, :] = slopes[4:8]
                    else:
                        strips[x, k + 2 : k + 5, :] = res[f, 8:11, :]
                        strips[x, k + 9 : k + 14, :] = slopes[0:5]
        edge_sweep(
            lambda f: hc_t[at, :] if f == 2 else h_t[at, :],
            lambda f: beyond(8, 2) if f == 2 else beyond(16, 0),
            high,
            win,
            a_scr,
            f_scr,
            res,
        )
        if high:
            sh_t[ext - 16 : ext, :] = res[0, 8:24, :]
        else:
            sh_t[0:16, :] = res[0, 0:16, :]
    for i in range(2):
        edges[i] = strips[i].T
        edges[2 + i] = sh_t[half(i, RIM), :].T
        edges[4 + i] = rows_slope(sh_t, RIM + i * LANES, LANES).T


def y_edge(x_e, cy_e, h_t, hc_t, from_l, from_r, sh_t, gy):
    return call(
        y_edge_kernel,
        (out(*sh_t.shape), out(6, LANES, LANES), out(*gy.shape)),
        (x_e, cy_e, h_t, hc_t, from_l, from_r, sh_t, gy),
        "y_edge",
        mib=8,
        scratch=[pltpu.VMEM((2, LANES, LANES), F32)] + EDGE_SCRATCH,
        spaces=[pltpu.VMEM] * 7 + [pl.ANY],
        out_spaces=[pltpu.VMEM] * 2 + [pl.ANY],
        aliases={6: 0, 7: 2},
    )[1:]


def finish_field(f, s_in, gy, edges, s, xy, adv=None, ready=None):
    planes, rows = xy.shape[2:4]
    n = 64
    lane = lane_iota(n)

    def body(p, _):
        if ready is not None:
            ready(p, f)
        strip = pl.multiple_of((f * 4 + p) * STRIP, STRIP)
        first = (p * 2 + f) * 2
        for r in range(0, rows, n):
            strips = edges[r // LANES, r % LANES : r % LANES + n, :]
            value = pltpu.roll(strips, LANES - VALUES_AT - strip, 1)
            y_slope = pltpu.roll(strips, LANES - SLOPES_AT - strip, 1)
            to = slice(RIM + r, RIM + r + n)
            for h in range(2):
                q = s_in[first + h, to, :]
                q = jnp.where(lane >= LANES - 2 if h else lane < 3, value, q)
                s[first + h, to, :] = q
                if adv is not None:
                    adv[f, p, r : r + n, half(h)] = q
                xy[1, f, p, r : r + n, half(h)] = jnp.where(
                    lane >= LANES - 4 if h else lane < 5, y_slope, gy[first + h, r : r + n, :]
                )
        for h in range(2):

            def outer(kind, at, count):
                return edges[kind * 2 + h, pl.ds(strip + at, count), :]

            s[first + h, RIM - 2 : RIM + 3, :] = outer(1, 0, EDGE)
            s[first + h, RIM + rows - 3 : RIM + rows + 2, :] = outer(1, EDGE, EDGE)
            for ref, kind in ((xy.at[1, f, p], 2), (None if adv is None else adv.at[f, p], 1)):
                if ref is not None:
                    ref[0:3, half(h)] = outer(kind, 2, 3)
                    ref[rows - 3 : rows, half(h)] = outer(kind, EDGE, 3)
            for r in range(0, rows, n):
                xy[0, f, p, r : r + n, half(h)] = rows_slope(s.at[first + h], RIM + r, n)
        return 0

    lax.fori_loop(0, planes, body, 0, unroll=False)


def piece_of(owner, core, slot):
    rank = jnp.int32(0)
    piece = jnp.int32(0)
    for j in range(NP):
        mine = owner[0, j] == core
        piece = jnp.where(jnp.logical_and(mine, rank == slot), j, piece)
        rank = rank + mine.astype(jnp.int32)
    return piece, slot < rank


def slope_copy(piece, used, src, zeros, to, sem):
    width = zeros.shape[1]

    @pl.when(used)
    def _():
        at = pl.ds(pl.multiple_of(piece * width, width), width)
        pltpu.make_async_copy(src.at[:, at, :], to, sem).start()

    @pl.when(jnp.logical_not(used))
    def _():
        pltpu.make_async_copy(zeros, to, sem).start()


def own_slopes_kernel(
    owner, core, s_in, gy_in, edges, adv, grad, s, xy, gy, buf, zeros, adv_sem, sems, in_sems
):
    planes = xy.shape[2]
    me = core[0]
    mine = pl.ds(pl.multiple_of(planes * me, planes), planes)

    def arrival(p, f):
        at = pl.ds((p * 2 + f) * 2, 2)
        return pltpu.make_async_copy(gy_in.at[at], gy.at[at], in_sems.at[f, p])

    for f in range(2):
        for p in range(planes):
            arrival(p, f).start()
    zeros[...] = jnp.zeros_like(zeros)
    pieces = [piece_of(owner, me, slot) for slot in range(CAP)]

    def adv_copy(f):
        return pltpu.make_async_copy(buf.at[f], adv.at[f], adv_sem.at[f])

    for f in range(2):
        finish_field(f, s_in, gy, edges, s, xy, buf, lambda p, f: arrival(p, f).wait())
        adv_copy(f).start()
        for slot in range(CAP):
            for k in range(2):
                slope_copy(
                    *pieces[slot], xy.at[k, f], zeros, grad.at[slot, f, k, mine], sems.at[slot, f, k]
                )
    for f in range(2):
        adv_copy(f).wait()
        for slot in range(CAP):
            for k in range(2):
                pltpu.make_async_copy(zeros, grad.at[slot, f, k, mine], sems.at[slot, f, k]).wait()


SMEM = pl.BlockSpec(memory_space=pltpu.SMEM)
VMEM = pl.BlockSpec(memory_space=pltpu.VMEM)
ANY = pl.BlockSpec(memory_space=pl.ANY)


def own_slopes(owner, core, s_in, gy, edges):
    planes = s_in.shape[0] // 4
    rows = gy.shape[1]
    cols = 2 * LANES
    width = rows // NP
    return pl.pallas_call(
        own_slopes_kernel,
        in_specs=[SMEM, SMEM, VMEM, ANY, VMEM],
        out_specs=(ANY, ANY, VMEM, VMEM),
        out_shape=(
            out(2, planes, rows, cols),
            out(CAP, 2, 3, 2 * planes, width, cols),
            pltpu.VMEM(s_in.shape, F32),
            pltpu.VMEM((2, 2, planes, rows, cols), F32),
        ),
        scratch_shapes=[
            pltpu.VMEM(gy.shape, F32),
            pltpu.VMEM((2, planes, rows, cols), F32),
            pltpu.VMEM((planes, width, cols), F32),
            pltpu.SemaphoreType.DMA((2,)),
            pltpu.SemaphoreType.DMA((CAP, 2, 2)),
            pltpu.SemaphoreType.DMA((2, planes)),
        ],
        compiler_params=pltpu.CompilerParams(vmem_limit_bytes=14 * MIB),
        cost_estimate=SWEEP_COST,
        name="own_slopes",
    )(owner, core, s_in, gy, edges)


def gradient_kernel(
    owner,
    core,
    own,
    own_xy,
    other_in,
    other_gy,
    other_edges,
    grad_in,
    grad,
    wedge,
    other,
    other_xy,
    other_y,
    part,
    wpart,
    zeros,
    xy_sems,
    sems,
    wsems,
    in_sems,
):
    planes = own_xy.shape[2]
    width = grad.shape[4]
    me = core[0]
    mine = pl.ds(pl.multiple_of(planes * me, planes), planes)
    theirs = pl.ds(pl.multiple_of(planes * (1 - me), planes), planes)

    def arrivals(p, f):
        at = pl.ds((p * 2 + f) * 2, 2)
        return (
            pltpu.make_async_copy(other_in.at[at], other.at[at], in_sems.at[0, f, p]),
            pltpu.make_async_copy(other_gy.at[at], other_y.at[at], in_sems.at[1, f, p]),
        )

    for f in range(2):
        for p in range(planes):
            for c in arrivals(p, f):
                c.start()

    def ready(p, f):
        for c in arrivals(p, f):
            c.wait()

    zeros[...] = jnp.zeros_like(zeros)
    pieces = [piece_of(owner, me, slot) for slot in range(CAP)]
    for f in range(2):
        finish_field(f, other, other_y, other_edges, other, other_xy, ready=ready)
        for slot in range(CAP):
            for k in range(2):
                slope_copy(
                    *pieces[slot],
                    other_xy.at[k, f],
                    zeros,
                    grad.at[slot, f, k, theirs],
                    xy_sems.at[slot, f, k],
                )

    def copies(slot, used=True):
        res = []
        for k, where in enumerate((mine, theirs)):
            for f in range(2):
                src = part.at[slot, f, k] if used else zeros
                res.append(
                    pltpu.make_async_copy(src, grad.at[slot, f, 2, where], sems.at[slot, f, k])
                )
            src = wpart.at[slot, k] if used else zeros
            res.append(pltpu.make_async_copy(src, wedge.at[slot, where], wsems.at[slot, k]))
        return res

    def fill(slot, piece):
        n = 8
        first = pl.multiple_of(piece * width, 8)

        def body(i, _):
            at = pl.multiple_of(first + i * n, n)
            r = pl.multiple_of(RIM + at, n)
            to = pl.ds(pl.multiple_of(i * n, n), n)
            for h in range(2):
                cols = half(h)

                def plane(z, f):
                    ref = own if z < planes else other
                    return ref[((z % planes) * 2 + f) * 2 + h, pl.ds(r, n), :]

                q = [[plane(z, f) for f in range(2)] for z in range(8)]
                for z in range(8):
                    g = []
                    p = z % planes
                    xy = own_xy if z < planes else other_xy
                    for f in range(2):
                        z_slope = slope(
                            q[(z + 1) % 8][f] - q[(z + 7) % 8][f],
                            q[(z + 2) % 8][f] - q[(z + 6) % 8][f],
                        )
                        part[slot, f, z // planes, p, to, cols] = z_slope
                        x_slope = xy[0, f, p, pl.ds(at, n), cols]
                        y_slope = xy[1, f, p, pl.ds(at, n), cols]
                        g.append((x_slope, y_slope, z_slope))
                    rx, ry, rz = g[0]
                    tx, ty, tz = g[1]
                    a = ry * tz - rz * ty
                    b = rz * tx - rx * tz
                    c = rx * ty - ry * tx
                    wpart[slot, z // planes, p, to, cols] = a * a + b * b + c * c
            return 0

        lax.fori_loop(0, width // n, body, 0, unroll=False)

    def slot_body(slot, _):
        piece, used = piece_of(owner, me, slot)

        @pl.when(used)
        def _():
            fill(slot, piece)
            for c in copies(slot):
                c.start()

        @pl.when(jnp.logical_not(used))
        def _():
            for c in copies(slot, False):
                c.start()

        return 0

    lax.fori_loop(0, CAP, slot_body, 0, unroll=False)

    def wait_body(slot, _):
        for f in range(2):
            for k in range(2):
                pltpu.make_async_copy(
                    zeros, grad.at[slot, f, k, theirs], xy_sems.at[slot, f, k]
                ).wait()
        for c in copies(slot):
            c.wait()
        return 0

    lax.fori_loop(0, CAP, wait_body, 0, unroll=False)


def gradients_of(owner, core, own, own_xy, other, other_gy, other_edges, grad):
    _, _, planes, rows, cols = own_xy.shape
    width = rows // NP
    return pl.pallas_call(
        gradient_kernel,
        in_specs=[SMEM, SMEM, VMEM, VMEM, ANY, ANY, VMEM, ANY],
        out_specs=(ANY, ANY),
        out_shape=(out(*grad.shape), out(CAP, 2 * planes, width, cols)),
        scratch_shapes=[
            pltpu.VMEM(own.shape, F32),
            pltpu.VMEM(own_xy.shape, F32),
            pltpu.VMEM(other_gy.shape, F32),
            pltpu.VMEM((CAP, 2, 2, planes, width, cols), F32),
            pltpu.VMEM((CAP, 2, planes, width, cols), F32),
            pltpu.VMEM((planes, width, cols), F32),
            pltpu.SemaphoreType.DMA((CAP, 2, 2)),
            pltpu.SemaphoreType.DMA((CAP, 2, 2)),
            pltpu.SemaphoreType.DMA((CAP, 2)),
            pltpu.SemaphoreType.DMA((2, 2, planes)),
        ],
        input_output_aliases={7: 0},
        compiler_params=pltpu.CompilerParams(vmem_limit_bytes=24 * MIB),
        name="gradient",
    )(owner, core, own, own_xy, other, other_gy, other_edges, grad)


def per_device(density, heat, cx, cy, owner):
    nx, ny = lax.axis_size("gx"), lax.axis_size("gy")
    lo, hi = edge_rows((density, heat, cx, cy))
    left = lax.ppermute(hi, "gx", ring(nx, 1))
    right = lax.ppermute(lo, "gx", ring(nx, -1))
    x_e, cy_e, s_t, swept = inner(density, heat, cx, cy)
    h_t, hc_t, to_l, to_r, swept = x_edge(density, heat, cx, cy, left, right, x_e, cy_e, swept)
    other = lax.ppermute(swept, "sa", ring(2, 1))
    from_l = lax.ppermute(to_r, "gy", ring(ny, 1))
    from_r = lax.ppermute(to_l, "gy", ring(ny, -1))
    sh_t, gy = inner_slopes(s_t, h_t, hc_t)
    edges, gy = y_edge(x_e, cy_e, h_t, hc_t, from_l, from_r, sh_t, gy)
    other_edges = lax.ppermute(edges, "sa", ring(2, 1))
    other_gy = lax.ppermute(gy, "sa", ring(2, 1))
    core = lax.axis_index("sa").astype(jnp.int32).reshape(1)
    advected, gradients, own, own_xy = own_slopes(owner, core, swept, gy, edges)
    gradients, wedge = gradients_of(
        owner, core, own, own_xy, other, other_gy, other_edges, gradients
    )
    return advected, gradients, wedge


def solution(mesh):
    block = P("sa", "gx", "gy")
    return jax.shard_map(
        per_device,
        mesh=mesh,
        in_specs=(block, block, block, block, P("gx", None)),
        out_specs=(
            P(None, "sa", "gx", "gy"),
            P(("gx", "sa"), None, None, None, None, "gy"),
            P(("gx", "sa"), None, None, "gy"),
        ),
        check_vma=False,
    )
```

```python
import jax
import jax.numpy as jnp
from jax import lax
from jax.experimental import pallas as pl
from jax.experimental.pallas import tpu as pltpu
from jax.sharding import PartitionSpec as P

CAP = 6
NP = 8
RIM = 8
LANES = 128
F32 = jnp.float32
MIB = 1024 * 1024


def ring(count, step):
    return [(i, (i + step) % count) for i in range(count)]


def coefficients(c):
    d = 1.0 - c
    m = c * d
    k_right = m * d
    k_left = m * c
    return k_right, k_left, c - k_right + k_left


def face_value(qm1, q0, q1, q2):
    return (7.0 / 12.0) * (q0 + q1) - (1.0 / 12.0) * (qm1 + q2)


def sweep_rows(load_q, load_c, store, a_scr, f_scr, base, count, chunk, fields=2):
    done = 0
    while done < count:
        n = min(chunk, count - done)
        r = base + done
        k_right, k_left, k_mid = coefficients(load_c(r, n))
        for f in range(fields):
            q0 = load_q(f, r, n)
            a = face_value(load_q(f, r - 1, n), q0, load_q(f, r + 1, n), load_q(f, r + 2, n))
            a_scr[f, pl.ds(8 + done, n), :] = a
            flux = k_right * a - k_left * a_scr[f, pl.ds(7 + done, n), :] + k_mid * q0
            f_scr[f, pl.ds(8 + done, n), :] = flux
            store(f, r, n, q0 - (flux - f_scr[f, pl.ds(7 + done, n), :]))
        done += n


def lane_iota(rows):
    return lax.broadcasted_iota(jnp.int32, (rows, LANES), 1)


def half(h, start=0):
    return slice(start + h * LANES, start + (h + 1) * LANES)


def call(
    kernel, out_shape, operands, name, spaces=None, scratch=(), aliases=None, cost=None, mib=20,
    out_spaces=None,
):
    vmem = pl.BlockSpec(memory_space=pltpu.VMEM)
    return pl.pallas_call(
        kernel,
        in_specs=[pl.BlockSpec(memory_space=x) for x in spaces] if spaces else [vmem] * len(operands),
        out_specs=tuple(pl.BlockSpec(memory_space=x) for x in out_spaces)
        if out_spaces
        else jax.tree.map(lambda _: vmem, out_shape),
        out_shape=tuple(
            x if space is pl.ANY else pltpu.VMEM(x.shape, F32)
            for x, space in zip(out_shape, out_spaces or [None] * len(out_shape))
        ),
        scratch_shapes=list(scratch),
        input_output_aliases=aliases or {},
        compiler_params=pltpu.CompilerParams(vmem_limit_bytes=mib * MIB),
        cost_estimate=cost,
        name=name,
    )(*operands)


def out(*shape):
    return jax.ShapeDtypeStruct(shape, F32)


SWEEP_COST = pl.CostEstimate(flops=20_000_000, bytes_accessed=6_000_000, transcendentals=0)


LAST = (5, 5, 3, 2)
FIRST = (4, 4, 2, 2)


def padded(rows):
    return -(-rows // 8) * 8


def place(counts, p, f):
    return p * sum(counts) + sum(counts[:f]), counts[f]


def edge_rows_kernel(d, t, cx, cy, lo, hi, first, last, sems):
    planes, rows, _ = d.shape
    copies = []
    for f, ref in enumerate((d, t, cx, cy)):
        copies.append(pltpu.make_async_copy(ref.at[:, 0:RIM, :], first.at[f], sems.at[f]))
        copies.append(
            pltpu.make_async_copy(ref.at[:, rows - RIM : rows, :], last.at[f], sems.at[4 + f])
        )
    for c in copies:
        c.start()
    for c in copies:
        c.wait()
    for p in range(planes):
        for f in range(4):
            at, n = place(FIRST, p, f)
            lo[at : at + n, :] = first[f, p, 0:n, :]
            at, n = place(LAST, p, f)
            hi[at : at + n, :] = last[f, p, RIM - n : RIM, :]


def edge_rows(fields):
    planes, _, cols = fields[0].shape
    tiles = pltpu.VMEM((4, planes, RIM, cols), F32)
    return call(
        edge_rows_kernel,
        (out(padded(planes * sum(FIRST)), cols), out(padded(planes * sum(LAST)), cols)),
        [pltpu.with_memory_space_constraint(x, pltpu.HBM) for x in fields],
        "edge_rows",
        spaces=[pl.ANY] * 4,
        scratch=[tiles, tiles, pltpu.SemaphoreType.DMA((8,))],
        mib=8,
    )


def inner_kernel(d, t, cx, cy, x_e, cy_e, s_t, s, win, xs, x_t, cy_t, a_scr, f_scr):
    planes, rows, _ = d.shape

    def body(p, _):
        for h in range(2):
            for f, ref in enumerate((d, t, cx)):
                win[f, 0:rows, :] = ref[p, :, half(h)]

            def store(f, r, n, value):
                xs[f, h, pl.ds(RIM + r, n), :] = value

            sweep_rows(
                lambda f, r, n: win[f, pl.ds(r, n), :],
                lambda r, n: win[2, pl.ds(r, n), :],
                store,
                a_scr,
                f_scr,
                1,
                rows,
                32,
            )
            for x in range(2):
                cy_t[x, half(h, RIM), :] = cy[p, half(x), half(h)].T
        for x in range(2):
            for f in range(2):
                for h in range(2):
                    x_t[f, x, half(h, RIM), :] = xs[f, h, half(x, RIM), :].T

            def store_t(f, r, n, value):
                s_t[p, f, x, pl.ds(r, n), :] = value

            sweep_rows(
                lambda f, r, n: x_t[f, x, pl.ds(r, n), :],
                lambda r, n: cy_t[x, pl.ds(r, n), :],
                store_t,
                a_scr,
                f_scr,
                RIM + 1,
                rows,
                32,
            )
            for f in range(2):
                for h in range(2):
                    s[(p * 2 + f) * 2 + h, half(x, RIM), :] = s_t[p, f, x, half(h, RIM), :].T
            for high, at in enumerate((slice(RIM, 16 + RIM), slice(rows + RIM - 16, rows + RIM))):
                cy_e[high, p, x] = cy_t[x, at, :]
                for f in range(2):
                    x_e[high, p, f, x] = x_t[f, x, at, :]
        return 0

    lax.fori_loop(0, planes, body, 0, unroll=False)


def inner(d, t, cx, cy):
    planes, rows, cols = d.shape
    ext = rows + 2 * RIM
    return call(
        inner_kernel,
        (
            out(2, planes, 2, 2, 16, LANES),
            out(2, planes, 2, 16, LANES),
            out(planes, 2, 2, ext, LANES),
            out(4 * planes, ext, LANES),
        ),
        (d, t, cx, cy),
        "inner",
        scratch=[pltpu.VMEM((3, ext, LANES), F32)]
        + [pltpu.VMEM((2, 2, ext, LANES), F32)] * 2
        + [pltpu.VMEM((2, ext, LANES), F32)]
        + [pltpu.VMEM((2, ext, LANES), F32)] * 2,
        cost=SWEEP_COST,
        mib=16,
    )


def edge_sweep(own, rim, high, win, a_scr, f_scr, res):
    lead, rim_at = (0, 16) if high else (8, 0)
    for f in range(3):
        win[f, lead : lead + 16, :] = own(f)
        beyond = rim(f)
        if beyond is not None:
            n = beyond.shape[0]
            at = rim_at if high else 8 - n
            win[f, at : at + n, :] = beyond

    def store(f, r, n, value):
        res[f, pl.ds(r, n), :] = value

    sweep_rows(
        lambda f, r, n: win[f, pl.ds(r, n), :],
        lambda r, n: win[2, pl.ds(r, n), :],
        store,
        a_scr,
        f_scr,
        6 if high else 4,
        16,
        16,
    )


EDGE_SCRATCH = [
    pltpu.VMEM((3, 32, LANES), F32),
    pltpu.VMEM((2, 32, LANES), F32),
    pltpu.VMEM((2, 32, LANES), F32),
    pltpu.VMEM((2, 32, LANES), F32),
]


STRIP = 16
EDGE = 5


def x_edge_kernel(
    d,
    t,
    cx,
    cy,
    left,
    right,
    x_e,
    cy_e,
    s_in,
    h_t,
    hc_t,
    to_l,
    to_r,
    s,
    q_rows,
    c_rows,
    win,
    a_scr,
    f_scr,
    res,
):
    del s_in, s
    planes, rows, _ = d.shape

    for p in range(planes):
        for h in range(2):
            for high in range(2):
                rim, counts = (right, FIRST) if high else (left, LAST)
                at = slice(rows - 16, rows) if high else slice(0, 16)

                def beyond(f):
                    r, n = place(counts, p, f)
                    return rim[r : r + n, half(h)]

                edge_sweep(
                    lambda f: (d, t, cx)[f][p, at, half(h)],
                    beyond,
                    high,
                    win,
                    a_scr,
                    f_scr,
                    res,
                )
                for f in range(2):
                    k = (f * 4 + p) * STRIP + EDGE * high
                    if high:
                        q_rows[h, k : k + EDGE, :] = res[f, 13:18, :]
                        c_rows[h, k : k + 3, :] = cy[p, rows - 3 : rows, half(h)]
                        c_rows[h, k + 3 : k + EDGE, :] = beyond(3)
                    else:
                        q_rows[h, k : k + EDGE, :] = res[f, 6:11, :]
                        c_rows[h, k : k + 2, :] = beyond(3)
                        c_rows[h, k + 2 : k + EDGE, :] = cy[p, 0:3, half(h)]
    for h in range(2):
        h_t[half(h, RIM), :] = q_rows[h].T
        hc_t[half(h, RIM), :] = c_rows[h].T
    for buf, counts in ((to_l, FIRST), (to_r, LAST)):

        last = counts is LAST

        def put(i, f, ref, start, stop):
            at, n = y_place(counts, i, f)
            top = stop - n if last else start
            buf[at : at + n, :] = ref[top : top + n, :]

        for p in range(planes):
            for x in range(2):
                for f in range(2):
                    put((p * 2 + f) * 2 + x, 0, x_e.at[int(last), p, f, x], 0, 16)
                put(p * 2 + x, 2, cy_e.at[int(last), p, x], 0, 16)
        put(16, 0, h_t, RIM, RIM + rows)
        put(8, 2, hc_t, RIM, RIM + rows)


def y_place(counts, i, f):
    return (17 * counts[0] if f == 2 else 0) + i * counts[f], counts[f]


def y_rim(counts):
    return out(padded(17 * counts[0] + 9 * counts[2]), LANES)


def x_edge(d, t, cx, cy, left, right, x_e, cy_e, s):
    ext = s.shape[1]
    return call(
        x_edge_kernel,
        (out(ext, LANES), out(ext, LANES), y_rim(FIRST), y_rim(LAST), out(*s.shape)),
        (d, t, cx, cy, left, right, x_e, cy_e, s),
        "x_edge",
        mib=12,
        scratch=[pltpu.VMEM((2, LANES, LANES), F32)] * 2 + EDGE_SCRATCH,
        spaces=[pltpu.VMEM] * 8 + [pl.ANY],
        out_spaces=[pltpu.VMEM] * 4 + [pl.ANY],
        aliases={8: 4},
    )


def slope(w1, w2):
    return (2.0 / 3.0) * w1 - (1.0 / 12.0) * w2


def rows_slope(ref, r, n):
    return slope(
        ref[pl.ds(r + 1, n), :] - ref[pl.ds(r - 1, n), :],
        ref[pl.ds(r + 2, n), :] - ref[pl.ds(r - 2, n), :],
    )


def inner_slopes_kernel(s_t, h_t, hc_t, sh_t, gy_out, gy, a_scr, f_scr, sems):
    planes, _, _, ext, _ = s_t.shape
    rows = ext - 2 * RIM

    def copy(p):
        at = pl.ds(p * 4, 4)
        return pltpu.make_async_copy(gy.at[at], gy_out.at[at], sems.at[p])

    def body(p, _):
        for f in range(2):
            for x in range(2):
                for h in range(2):
                    gy[(p * 2 + f) * 2 + h, half(x), :] = rows_slope(
                        s_t.at[p, f, x], RIM + h * LANES, LANES
                    ).T
        copy(p).start()
        return 0

    lax.fori_loop(0, planes, body, 0, unroll=False)

    def store(f, r, n, value):
        sh_t[pl.ds(r, n), :] = value

    sweep_rows(
        lambda f, r, n: h_t[pl.ds(r, n), :],
        lambda r, n: hc_t[pl.ds(r, n), :],
        store,
        a_scr,
        f_scr,
        RIM + 1,
        rows,
        32,
        fields=1,
    )
    for p in range(planes):
        copy(p).wait()


def inner_slopes(s_t, h_t, hc_t):
    planes, _, _, ext, _ = s_t.shape
    return call(
        inner_slopes_kernel,
        (out(ext, LANES), out(4 * planes, ext - 2 * RIM, LANES)),
        (s_t, h_t, hc_t),
        "inner_slopes",
        mib=8,
        scratch=[pltpu.VMEM((4 * planes, ext - 2 * RIM, LANES), F32)]
        + [pltpu.VMEM((2, ext, LANES), F32)] * 2
        + [pltpu.SemaphoreType.DMA((planes,))],
        out_spaces=[pltpu.VMEM, pl.ANY],
        cost=SWEEP_COST,
    )


VALUES_AT = 2
SLOPES_AT = 9


def y_edge_kernel(
    x_e,
    cy_e,
    h_t,
    hc_t,
    from_l,
    from_r,
    sh_in,
    sh_t,
    edges,
    strips,
    win,
    a_scr,
    f_scr,
    res,
):
    planes = x_e.shape[1]
    ext = h_t.shape[0]

    for high in range(2):
        rim, counts = (from_r, FIRST) if high else (from_l, LAST)
        at = slice(ext - 24, ext - 8) if high else slice(8, 24)

        def beyond(i, f):
            r, n = y_place(counts, i, f)
            return rim[r : r + n, :]

        for p in range(planes):
            for x in range(2):
                edge_sweep(
                    lambda f: cy_e[high, p, x] if f == 2 else x_e[high, p, f, x],
                    lambda f: beyond(p * 2 + x if f == 2 else (p * 2 + f) * 2 + x, f),
                    high,
                    win,
                    a_scr,
                    f_scr,
                    res,
                )
                for f in range(2):
                    k = (f * 4 + p) * STRIP
                    slopes = rows_slope(res.at[f], 8, 8)
                    if high:
                        strips[x, k : k + 2, :] = res[f, 14:16, :]
                        strips[x, k + 5 : k + 9, :] = slopes[4:8]
                    else:
                        strips[x, k + 2 : k + 5, :] = res[f, 8:11, :]
                        strips[x, k + 9 : k + 14, :] = slopes[0:5]
        edge_sweep(
            lambda f: hc_t[at, :] if f == 2 else h_t[at, :],
            lambda f: beyond(8, 2) if f == 2 else beyond(16, 0),
            high,
            win,
            a_scr,
            f_scr,
            res,
        )
        if high:
            sh_t[ext - 16 : ext, :] = res[0, 8:24, :]
        else:
            sh_t[0:16, :] = res[0, 0:16, :]
    for i in range(2):
        edges[i] = strips[i].T
        edges[2 + i] = sh_t[half(i, RIM), :].T
        edges[4 + i] = rows_slope(sh_t, RIM + i * LANES, LANES).T


def y_edge(x_e, cy_e, h_t, hc_t, from_l, from_r, sh_t):
    return call(
        y_edge_kernel,
        (out(*sh_t.shape), out(6, LANES, LANES)),
        (x_e, cy_e, h_t, hc_t, from_l, from_r, sh_t),
        "y_edge",
        mib=8,
        scratch=[pltpu.VMEM((2, LANES, LANES), F32)] + EDGE_SCRATCH,
        aliases={6: 0},
    )[1]


def finish_field(f, s_in, gy, edges, s, xy, adv=None, ready=None):
    planes, width = xy.shape[3:5]
    rows = NP * width
    n = 2 * width
    lane = lane_iota(n)

    def put(dim, p, r, h, value):
        for i in range(n // width):
            xy[f, r // width + i, dim, p, :, half(h)] = value[i * width : (i + 1) * width]

    def body(p, _):
        if ready is not None:
            ready(p, f)
        strip = pl.multiple_of((f * 4 + p) * STRIP, STRIP)
        first = (p * 2 + f) * 2
        for r in range(0, rows, n):
            strips = edges[r // LANES, r % LANES : r % LANES + n, :]
            value = pltpu.roll(strips, LANES - VALUES_AT - strip, 1)
            y_slope = pltpu.roll(strips, LANES - SLOPES_AT - strip, 1)
            to = slice(RIM + r, RIM + r + n)
            for h in range(2):
                q = s_in[first + h, to, :]
                q = jnp.where(lane >= LANES - 2 if h else lane < 3, value, q)
                s[first + h, to, :] = q
                if adv is not None:
                    adv[f, p, r : r + n, half(h)] = q
                y = gy[first + h, r : r + n, :]
                put(1, p, r, h, jnp.where(lane >= LANES - 4 if h else lane < 5, y_slope, y))
        for h in range(2):

            def outer(kind, at, count):
                return edges[kind * 2 + h, pl.ds(strip + at, count), :]

            s[first + h, RIM - 2 : RIM + 3, :] = outer(1, 0, EDGE)
            s[first + h, RIM + rows - 3 : RIM + rows + 2, :] = outer(1, EDGE, EDGE)
            if adv is not None:
                adv[f, p, 0:3, half(h)] = outer(1, 2, 3)
                adv[f, p, rows - 3 : rows, half(h)] = outer(1, EDGE, 3)
            xy[f, 0, 1, p, 0:3, half(h)] = outer(2, 2, 3)
            xy[f, NP - 1, 1, p, width - 3 : width, half(h)] = outer(2, EDGE, 3)
            for r in range(0, rows, n):
                put(0, p, r, h, rows_slope(s.at[first + h], RIM + r, n))
        return 0

    lax.fori_loop(0, planes, body, 0, unroll=False)


def piece_of(owner, core, slot):
    rank = jnp.int32(0)
    piece = jnp.int32(0)
    for j in range(NP):
        mine = owner[0, j] == core
        piece = jnp.where(jnp.logical_and(mine, rank == slot), j, piece)
        rank = rank + mine.astype(jnp.int32)
    return piece, slot < rank


def clear(used, *refs):
    @pl.when(jnp.logical_not(used))
    def _():
        for ref in refs:
            ref[...] = jnp.zeros_like(ref)


def start_copy(used, src, zeros, to, sem):
    @pl.when(used)
    def _():
        pltpu.make_async_copy(src, to, sem).start()

    @pl.when(jnp.logical_not(used))
    def _():
        pltpu.make_async_copy(zeros, to, sem).start()


def own_slopes_kernel(
    owner, core, s_in, gy_in, edges, adv, grad, s, xy, gy, buf, zeros, adv_sem, sems, in_sems
):
    planes = xy.shape[3]
    me = core[0]
    mine = pl.ds(pl.multiple_of(planes * me, planes), planes)

    def arrival(p, f):
        at = pl.ds((p * 2 + f) * 2, 2)
        return pltpu.make_async_copy(gy_in.at[at], gy.at[at], in_sems.at[f, p])

    for f in range(2):
        for p in range(planes):
            arrival(p, f).start()
    pieces = [piece_of(owner, me, slot) for slot in range(CAP)]
    clear(pieces[-1][1], zeros)

    def adv_copy(f):
        return pltpu.make_async_copy(buf.at[f], adv.at[f], adv_sem.at[f])

    for f in range(2):
        finish_field(f, s_in, gy, edges, s, xy, buf, lambda p, f: arrival(p, f).wait())
        adv_copy(f).start()
        if f == 0:
            for slot, (piece, used) in enumerate(pieces):
                start_copy(used, xy.at[0, piece], zeros, grad.at[slot, 0, 0:2, mine], sems.at[slot])
    for f in range(2):
        adv_copy(f).wait()
    for slot in range(CAP):
        pltpu.make_async_copy(zeros, grad.at[slot, 0, 0:2, mine], sems.at[slot]).wait()


SMEM = pl.BlockSpec(memory_space=pltpu.SMEM)
VMEM = pl.BlockSpec(memory_space=pltpu.VMEM)
ANY = pl.BlockSpec(memory_space=pl.ANY)


def own_slopes(owner, core, s_in, gy, edges):
    planes = s_in.shape[0] // 4
    rows = gy.shape[1]
    cols = 2 * LANES
    width = rows // NP
    return pl.pallas_call(
        own_slopes_kernel,
        in_specs=[SMEM, SMEM, VMEM, ANY, VMEM],
        out_specs=(ANY, ANY, VMEM, VMEM),
        out_shape=(
            out(2, planes, rows, cols),
            out(CAP, 2, 3, 2 * planes, width, cols),
            pltpu.VMEM(s_in.shape, F32),
            pltpu.VMEM((2, NP, 2, planes, width, cols), F32),
        ),
        scratch_shapes=[
            pltpu.VMEM(gy.shape, F32),
            pltpu.VMEM((2, planes, rows, cols), F32),
            pltpu.VMEM((2, planes, width, cols), F32),
            pltpu.SemaphoreType.DMA((2,)),
            pltpu.SemaphoreType.DMA((CAP,)),
            pltpu.SemaphoreType.DMA((2, planes)),
        ],
        compiler_params=pltpu.CompilerParams(vmem_limit_bytes=14 * MIB),
        cost_estimate=SWEEP_COST,
        name="own_slopes",
    )(owner, core, s_in, gy, edges)


def gradient_kernel(
    owner,
    core,
    own,
    own_xy,
    other_in,
    other_gy,
    other_edges,
    grad_in,
    grad,
    wedge,
    other,
    other_xy,
    other_y,
    part,
    wpart,
    zeros,
    xy_zeros,
    in_sems,
    own_sems,
    xy_sems,
    sems,
):
    planes, width = own_xy.shape[3:5]
    me = core[0]
    mine = pl.ds(pl.multiple_of(planes * me, planes), planes)
    theirs = pl.ds(pl.multiple_of(planes * (1 - me), planes), planes)

    def arrivals(p, f):
        at = pl.ds((p * 2 + f) * 2, 2)
        return (
            pltpu.make_async_copy(other_in.at[at], other.at[at], in_sems.at[0, f, p]),
            pltpu.make_async_copy(other_gy.at[at], other_y.at[at], in_sems.at[1, f, p]),
        )

    def ready(p, f):
        for c in arrivals(p, f):
            c.wait()

    for f in range(2):
        for p in range(planes):
            for c in arrivals(p, f):
                c.start()
    pieces = [piece_of(owner, me, slot) for slot in range(CAP)]
    clear(pieces[-1][1], zeros, xy_zeros)
    for slot, (piece, used) in enumerate(pieces):
        start_copy(
            used, own_xy.at[1, piece], xy_zeros, grad.at[slot, 1, 0:2, mine], own_sems.at[slot]
        )
    for f in range(2):
        finish_field(f, other, other_y, other_edges, other, other_xy, ready=ready)
        for slot, (piece, used) in enumerate(pieces):
            start_copy(
                used,
                other_xy.at[f, piece],
                xy_zeros,
                grad.at[slot, f, 0:2, theirs],
                xy_sems.at[slot, f],
            )

    def targets(slot):
        return grad.at[slot, 0, 2], grad.at[slot, 1, 2], wedge.at[slot]

    def fill(slot, piece):
        n = 8
        first = pl.multiple_of(piece * width, 8)

        def body(i, _):
            r = pl.ds(pl.multiple_of(RIM + first + i * n, n), n)
            to = pl.ds(pl.multiple_of(i * n, n), n)
            for h in range(2):
                cols = half(h)

                def plane(z, f):
                    ref = own if z < planes else other
                    return ref[((z % planes) * 2 + f) * 2 + h, r, :]

                q = [[plane(z, f) for f in range(2)] for z in range(8)]
                for z in range(8):
                    g = []
                    p = z % planes
                    zo = lax.rem(z + planes * me, 2 * planes)
                    xy = own_xy if z < planes else other_xy
                    for f in range(2):
                        z_slope = slope(
                            q[(z + 1) % 8][f] - q[(z + 7) % 8][f],
                            q[(z + 2) % 8][f] - q[(z + 6) % 8][f],
                        )
                        part[slot, f, zo, to, cols] = z_slope
                        g.append((xy[f, piece, 0, p, to, cols], xy[f, piece, 1, p, to, cols], z_slope))
                    rx, ry, rz = g[0]
                    tx, ty, tz = g[1]
                    a = ry * tz - rz * ty
                    b = rz * tx - rx * tz
                    c = rx * ty - ry * tx
                    wpart[slot, zo, to, cols] = a * a + b * b + c * c
            return 0

        lax.fori_loop(0, width // n, body, 0, unroll=False)

    def slot_body(slot, _):
        piece, used = piece_of(owner, me, slot)

        @pl.when(used)
        def _():
            fill(slot, piece)

        sources = part.at[slot, 0], part.at[slot, 1], wpart.at[slot]
        for k, (src, to) in enumerate(zip(sources, targets(slot))):
            start_copy(used, src, zeros, to, sems.at[slot, k])
        return 0

    lax.fori_loop(0, CAP, slot_body, 0, unroll=False)

    def wait_body(slot, _):
        pltpu.make_async_copy(xy_zeros, grad.at[slot, 1, 0:2, mine], own_sems.at[slot]).wait()
        for f in range(2):
            pltpu.make_async_copy(
                xy_zeros, grad.at[slot, f, 0:2, theirs], xy_sems.at[slot, f]
            ).wait()
        for k, to in enumerate(targets(slot)):
            pltpu.make_async_copy(zeros, to, sems.at[slot, k]).wait()
        return 0

    lax.fori_loop(0, CAP, wait_body, 0, unroll=False)


def gradients_of(owner, core, own, own_xy, other, other_gy, other_edges, grad):
    planes, width, cols = own_xy.shape[3:]
    return pl.pallas_call(
        gradient_kernel,
        in_specs=[SMEM, SMEM, VMEM, VMEM, ANY, ANY, VMEM, ANY],
        out_specs=(ANY, ANY),
        out_shape=(out(*grad.shape), out(CAP, 2 * planes, width, cols)),
        scratch_shapes=[
            pltpu.VMEM(own.shape, F32),
            pltpu.VMEM(own_xy.shape, F32),
            pltpu.VMEM(other_gy.shape, F32),
            pltpu.VMEM((CAP, 2, 2 * planes, width, cols), F32),
            pltpu.VMEM((CAP, 2 * planes, width, cols), F32),
            pltpu.VMEM((2 * planes, width, cols), F32),
            pltpu.VMEM((2, planes, width, cols), F32),
            pltpu.SemaphoreType.DMA((2, 2, planes)),
            pltpu.SemaphoreType.DMA((CAP,)),
            pltpu.SemaphoreType.DMA((CAP, 2)),
            pltpu.SemaphoreType.DMA((CAP, 3)),
        ],
        input_output_aliases={7: 0},
        compiler_params=pltpu.CompilerParams(vmem_limit_bytes=24 * MIB),
        name="gradient",
    )(owner, core, own, own_xy, other, other_gy, other_edges, grad)


def per_device(density, heat, cx, cy, owner):
    nx, ny = lax.axis_size("gx"), lax.axis_size("gy")
    lo, hi = edge_rows((density, heat, cx, cy))
    left = lax.ppermute(hi, "gx", ring(nx, 1))
    right = lax.ppermute(lo, "gx", ring(nx, -1))
    x_e, cy_e, s_t, swept = inner(density, heat, cx, cy)
    h_t, hc_t, to_l, to_r, swept = x_edge(density, heat, cx, cy, left, right, x_e, cy_e, swept)
    other = lax.ppermute(swept, "sa", ring(2, 1))
    from_l = lax.ppermute(to_r, "gy", ring(ny, 1))
    from_r = lax.ppermute(to_l, "gy", ring(ny, -1))
    sh_t, gy = inner_slopes(s_t, h_t, hc_t)
    gy, from_l, from_r = lax.optimization_barrier((gy, from_l, from_r))
    other_gy = lax.ppermute(gy, "sa", ring(2, 1))
    edges = y_edge(x_e, cy_e, h_t, hc_t, from_l, from_r, sh_t)
    other_edges = lax.ppermute(edges, "sa", ring(2, 1))
    core = lax.axis_index("sa").astype(jnp.int32).reshape(1)
    advected, gradients, own, own_xy = own_slopes(owner, core, swept, gy, edges)
    gradients, wedge = gradients_of(
        owner, core, own, own_xy, other, other_gy, other_edges, gradients
    )
    return advected, gradients, wedge


def solution(mesh):
    block = P("sa", "gx", "gy")
    return jax.shard_map(
        per_device,
        mesh=mesh,
        in_specs=(block, block, block, block, P("gx", None)),
        out_specs=(
            P(None, "sa", "gx", "gy"),
            P(("gx", "sa"), None, None, None, None, "gy"),
            P(("gx", "sa"), None, None, "gy"),
        ),
        check_vma=False,
    )
```

```python
import jax
import jax.numpy as jnp
from jax import lax
from jax.experimental import pallas as pl
from jax.experimental.pallas import tpu as pltpu
from jax.sharding import PartitionSpec as P

CAP = 6
NP = 8
RIM = 8
LANES = 128
F32 = jnp.float32
MIB = 1024 * 1024


def ring(count, step):
    return [(i, (i + step) % count) for i in range(count)]


def coefficients(c):
    d = 1.0 - c
    m = c * d
    k_right = m * d
    k_left = m * c
    return k_right, k_left, c - k_right + k_left


def face_value(qm1, q0, q1, q2):
    return (7.0 / 12.0) * (q0 + q1) - (1.0 / 12.0) * (qm1 + q2)


def sweep_rows(load_q, load_c, store, a_scr, f_scr, base, count, chunk, fields=2):
    done = 0
    while done < count:
        n = min(chunk, count - done)
        r = base + done
        k_right, k_left, k_mid = coefficients(load_c(r, n))
        for f in range(fields):
            q0 = load_q(f, r, n)
            a = face_value(load_q(f, r - 1, n), q0, load_q(f, r + 1, n), load_q(f, r + 2, n))
            a_scr[f, pl.ds(8 + done, n), :] = a
            flux = k_right * a - k_left * a_scr[f, pl.ds(7 + done, n), :] + k_mid * q0
            f_scr[f, pl.ds(8 + done, n), :] = flux
            store(f, r, n, q0 - (flux - f_scr[f, pl.ds(7 + done, n), :]))
        done += n


def lane_iota(rows):
    return lax.broadcasted_iota(jnp.int32, (rows, LANES), 1)


def half(h, start=0):
    return slice(start + h * LANES, start + (h + 1) * LANES)


def call(
    kernel, out_shape, operands, name, spaces=None, scratch=(), aliases=None, cost=None, mib=20,
    out_spaces=None,
):
    vmem = pl.BlockSpec(memory_space=pltpu.VMEM)
    return pl.pallas_call(
        kernel,
        in_specs=[pl.BlockSpec(memory_space=x) for x in spaces] if spaces else [vmem] * len(operands),
        out_specs=tuple(pl.BlockSpec(memory_space=x) for x in out_spaces)
        if out_spaces
        else jax.tree.map(lambda _: vmem, out_shape),
        out_shape=tuple(
            x if space is pl.ANY else pltpu.VMEM(x.shape, F32)
            for x, space in zip(out_shape, out_spaces or [None] * len(out_shape))
        ),
        scratch_shapes=list(scratch),
        input_output_aliases=aliases or {},
        compiler_params=pltpu.CompilerParams(vmem_limit_bytes=mib * MIB),
        cost_estimate=cost,
        name=name,
    )(*operands)


def out(*shape):
    return jax.ShapeDtypeStruct(shape, F32)


SWEEP_COST = pl.CostEstimate(flops=20_000_000, bytes_accessed=6_000_000, transcendentals=0)


LAST = (5, 5, 3, 2)
FIRST = (4, 4, 2, 2)


def padded(rows):
    return -(-rows // 8) * 8


def place(counts, p, f):
    return p * sum(counts) + sum(counts[:f]), counts[f]


def edge_rows_kernel(d, t, cx, cy, lo, hi, first, last, sems):
    planes, rows, _ = d.shape
    copies = []
    for f, ref in enumerate((d, t, cx, cy)):
        copies.append(pltpu.make_async_copy(ref.at[:, 0:RIM, :], first.at[f], sems.at[f]))
        copies.append(
            pltpu.make_async_copy(ref.at[:, rows - RIM : rows, :], last.at[f], sems.at[4 + f])
        )
    for c in copies:
        c.start()
    for c in copies:
        c.wait()
    for p in range(planes):
        for f in range(4):
            at, n = place(FIRST, p, f)
            lo[at : at + n, :] = first[f, p, 0:n, :]
            at, n = place(LAST, p, f)
            hi[at : at + n, :] = last[f, p, RIM - n : RIM, :]


def edge_rows(fields):
    planes, _, cols = fields[0].shape
    tiles = pltpu.VMEM((4, planes, RIM, cols), F32)
    return call(
        edge_rows_kernel,
        (out(padded(planes * sum(FIRST)), cols), out(padded(planes * sum(LAST)), cols)),
        [pltpu.with_memory_space_constraint(x, pltpu.HBM) for x in fields],
        "edge_rows",
        spaces=[pl.ANY] * 4,
        scratch=[tiles, tiles, pltpu.SemaphoreType.DMA((8,))],
        mib=8,
    )


def inner_kernel(d, t, cx, cy, x_e, cy_e, s_t, s, win, xs, x_t, cy_t, a_scr, f_scr):
    planes, rows, _ = d.shape

    def body(p, _):
        for h in range(2):
            for f, ref in enumerate((d, t, cx)):
                win[f, 0:rows, :] = ref[p, :, half(h)]

            def store(f, r, n, value):
                xs[f, h, pl.ds(RIM + r, n), :] = value

            sweep_rows(
                lambda f, r, n: win[f, pl.ds(r, n), :],
                lambda r, n: win[2, pl.ds(r, n), :],
                store,
                a_scr,
                f_scr,
                1,
                rows,
                32,
            )
            for x in range(2):
                cy_t[x, half(h, RIM), :] = cy[p, half(x), half(h)].T
        for x in range(2):
            for f in range(2):
                for h in range(2):
                    x_t[f, x, half(h, RIM), :] = xs[f, h, half(x, RIM), :].T

            def store_t(f, r, n, value):
                s_t[p, f, x, pl.ds(r, n), :] = value

            sweep_rows(
                lambda f, r, n: x_t[f, x, pl.ds(r, n), :],
                lambda r, n: cy_t[x, pl.ds(r, n), :],
                store_t,
                a_scr,
                f_scr,
                RIM + 1,
                rows,
                32,
            )
            for f in range(2):
                for h in range(2):
                    s[(p * 2 + f) * 2 + h, half(x, RIM), :] = s_t[p, f, x, half(h, RIM), :].T
            for high, at in enumerate((slice(RIM, 16 + RIM), slice(rows + RIM - 16, rows + RIM))):
                cy_e[high, p, x] = cy_t[x, at, :]
                for f in range(2):
                    x_e[high, p, f, x] = x_t[f, x, at, :]
        return 0

    lax.fori_loop(0, planes, body, 0, unroll=False)


def inner(d, t, cx, cy):
    planes, rows, cols = d.shape
    ext = rows + 2 * RIM
    return call(
        inner_kernel,
        (
            out(2, planes, 2, 2, 16, LANES),
            out(2, planes, 2, 16, LANES),
            out(planes, 2, 2, ext, LANES),
            out(4 * planes, ext, LANES),
        ),
        (d, t, cx, cy),
        "inner",
        scratch=[pltpu.VMEM((3, ext, LANES), F32)]
        + [pltpu.VMEM((2, 2, ext, LANES), F32)] * 2
        + [pltpu.VMEM((2, ext, LANES), F32)]
        + [pltpu.VMEM((2, ext, LANES), F32)] * 2,
        cost=SWEEP_COST,
        mib=16,
    )


def edge_sweep(own, rim, high, win, a_scr, f_scr, res):
    lead, rim_at = (0, 16) if high else (8, 0)
    for f in range(3):
        win[f, lead : lead + 16, :] = own(f)
        beyond = rim(f)
        if beyond is not None:
            n = beyond.shape[0]
            at = rim_at if high else 8 - n
            win[f, at : at + n, :] = beyond

    def store(f, r, n, value):
        res[f, pl.ds(r, n), :] = value

    sweep_rows(
        lambda f, r, n: win[f, pl.ds(r, n), :],
        lambda r, n: win[2, pl.ds(r, n), :],
        store,
        a_scr,
        f_scr,
        6 if high else 4,
        16,
        16,
    )


EDGE_SCRATCH = [
    pltpu.VMEM((3, 32, LANES), F32),
    pltpu.VMEM((2, 32, LANES), F32),
    pltpu.VMEM((2, 32, LANES), F32),
    pltpu.VMEM((2, 32, LANES), F32),
]


STRIP = 16
EDGE = 5


def x_edge_kernel(
    d,
    t,
    cx,
    cy,
    left,
    right,
    x_e,
    cy_e,
    s_in,
    h_t,
    hc_t,
    to_l,
    to_r,
    s,
    q_rows,
    c_rows,
    win,
    a_scr,
    f_scr,
    res,
):
    del s_in, s
    planes, rows, _ = d.shape

    for p in range(planes):
        for h in range(2):
            for high in range(2):
                rim, counts = (right, FIRST) if high else (left, LAST)
                at = slice(rows - 16, rows) if high else slice(0, 16)

                def beyond(f):
                    r, n = place(counts, p, f)
                    return rim[r : r + n, half(h)]

                edge_sweep(
                    lambda f: (d, t, cx)[f][p, at, half(h)],
                    beyond,
                    high,
                    win,
                    a_scr,
                    f_scr,
                    res,
                )
                for f in range(2):
                    k = (f * 4 + p) * STRIP + EDGE * high
                    if high:
                        q_rows[h, k : k + EDGE, :] = res[f, 13:18, :]
                        c_rows[h, k : k + 3, :] = cy[p, rows - 3 : rows, half(h)]
                        c_rows[h, k + 3 : k + EDGE, :] = beyond(3)
                    else:
                        q_rows[h, k : k + EDGE, :] = res[f, 6:11, :]
                        c_rows[h, k : k + 2, :] = beyond(3)
                        c_rows[h, k + 2 : k + EDGE, :] = cy[p, 0:3, half(h)]
    for h in range(2):
        h_t[half(h, RIM), :] = q_rows[h].T
        hc_t[half(h, RIM), :] = c_rows[h].T
    for buf, counts in ((to_l, FIRST), (to_r, LAST)):

        last = counts is LAST

        def put(i, f, ref, start, stop):
            at, n = y_place(counts, i, f)
            top = stop - n if last else start
            buf[at : at + n, :] = ref[top : top + n, :]

        for p in range(planes):
            for x in range(2):
                for f in range(2):
                    put((p * 2 + f) * 2 + x, 0, x_e.at[int(last), p, f, x], 0, 16)
                put(p * 2 + x, 2, cy_e.at[int(last), p, x], 0, 16)
        put(16, 0, h_t, RIM, RIM + rows)
        put(8, 2, hc_t, RIM, RIM + rows)


def y_place(counts, i, f):
    return (17 * counts[0] if f == 2 else 0) + i * counts[f], counts[f]


def y_rim(counts):
    return out(padded(17 * counts[0] + 9 * counts[2]), LANES)


def x_edge(d, t, cx, cy, left, right, x_e, cy_e, s):
    ext = s.shape[1]
    return call(
        x_edge_kernel,
        (out(ext, LANES), out(ext, LANES), y_rim(FIRST), y_rim(LAST), out(*s.shape)),
        (d, t, cx, cy, left, right, x_e, cy_e, s),
        "x_edge",
        mib=12,
        scratch=[pltpu.VMEM((2, LANES, LANES), F32)] * 2 + EDGE_SCRATCH,
        spaces=[pltpu.VMEM] * 8 + [pl.ANY],
        out_spaces=[pltpu.VMEM] * 4 + [pl.ANY],
        aliases={8: 4},
    )


def slope(w1, w2):
    return (2.0 / 3.0) * w1 - (1.0 / 12.0) * w2


def rows_slope(ref, r, n):
    return slope(
        ref[pl.ds(r + 1, n), :] - ref[pl.ds(r - 1, n), :],
        ref[pl.ds(r + 2, n), :] - ref[pl.ds(r - 2, n), :],
    )


def inner_slopes_kernel(s_t, h_t, hc_t, sh_t, gy_out, gy, a_scr, f_scr, sems):
    planes, _, _, ext, _ = s_t.shape
    rows = ext - 2 * RIM

    def copy(p):
        at = pl.ds(p * 4, 4)
        return pltpu.make_async_copy(gy.at[at], gy_out.at[at], sems.at[p])

    def body(p, _):
        for f in range(2):
            for x in range(2):
                for h in range(2):
                    gy[(p * 2 + f) * 2 + h, half(x), :] = rows_slope(
                        s_t.at[p, f, x], RIM + h * LANES, LANES
                    ).T
        copy(p).start()
        return 0

    lax.fori_loop(0, planes, body, 0, unroll=False)

    def store(f, r, n, value):
        sh_t[pl.ds(r, n), :] = value

    sweep_rows(
        lambda f, r, n: h_t[pl.ds(r, n), :],
        lambda r, n: hc_t[pl.ds(r, n), :],
        store,
        a_scr,
        f_scr,
        RIM + 1,
        rows,
        32,
        fields=1,
    )
    for p in range(planes):
        copy(p).wait()


def inner_slopes(s_t, h_t, hc_t):
    planes, _, _, ext, _ = s_t.shape
    return call(
        inner_slopes_kernel,
        (out(ext, LANES), out(4 * planes, ext - 2 * RIM, LANES)),
        (s_t, h_t, hc_t),
        "inner_slopes",
        mib=8,
        scratch=[pltpu.VMEM((4 * planes, ext - 2 * RIM, LANES), F32)]
        + [pltpu.VMEM((2, ext, LANES), F32)] * 2
        + [pltpu.SemaphoreType.DMA((planes,))],
        out_spaces=[pltpu.VMEM, pl.ANY],
        cost=SWEEP_COST,
    )


VALUES_AT = 2
SLOPES_AT = 9


def y_edge_kernel(
    x_e,
    cy_e,
    h_t,
    hc_t,
    from_l,
    from_r,
    sh_in,
    sh_t,
    edges,
    strips,
    win,
    a_scr,
    f_scr,
    res,
):
    planes = x_e.shape[1]
    ext = h_t.shape[0]

    for high in range(2):
        rim, counts = (from_r, FIRST) if high else (from_l, LAST)
        at = slice(ext - 24, ext - 8) if high else slice(8, 24)

        def beyond(i, f):
            r, n = y_place(counts, i, f)
            return rim[r : r + n, :]

        for p in range(planes):
            for x in range(2):
                edge_sweep(
                    lambda f: cy_e[high, p, x] if f == 2 else x_e[high, p, f, x],
                    lambda f: beyond(p * 2 + x if f == 2 else (p * 2 + f) * 2 + x, f),
                    high,
                    win,
                    a_scr,
                    f_scr,
                    res,
                )
                for f in range(2):
                    k = (f * 4 + p) * STRIP
                    slopes = rows_slope(res.at[f], 8, 8)
                    if high:
                        strips[x, k : k + 2, :] = res[f, 14:16, :]
                        strips[x, k + 5 : k + 9, :] = slopes[4:8]
                    else:
                        strips[x, k + 2 : k + 5, :] = res[f, 8:11, :]
                        strips[x, k + 9 : k + 14, :] = slopes[0:5]
        edge_sweep(
            lambda f: hc_t[at, :] if f == 2 else h_t[at, :],
            lambda f: beyond(8, 2) if f == 2 else beyond(16, 0),
            high,
            win,
            a_scr,
            f_scr,
            res,
        )
        if high:
            sh_t[ext - 16 : ext, :] = res[0, 8:24, :]
        else:
            sh_t[0:16, :] = res[0, 0:16, :]
    for i in range(2):
        edges[i] = strips[i].T
        edges[2 + i] = sh_t[half(i, RIM), :].T
        edges[4 + i] = rows_slope(sh_t, RIM + i * LANES, LANES).T


def y_edge(x_e, cy_e, h_t, hc_t, from_l, from_r, sh_t):
    return call(
        y_edge_kernel,
        (out(*sh_t.shape), out(6, LANES, LANES)),
        (x_e, cy_e, h_t, hc_t, from_l, from_r, sh_t),
        "y_edge",
        mib=8,
        scratch=[pltpu.VMEM((2, LANES, LANES), F32)] + EDGE_SCRATCH,
        aliases={6: 0},
    )[1]


def finish_field(f, s_in, gy, edges, s, xy, adv=None, ready=None):
    planes, width = xy.shape[3:5]
    rows = NP * width
    n = 2 * width
    lane = lane_iota(n)

    def put(dim, p, r, h, value):
        for i in range(n // width):
            xy[f, r // width + i, dim, p, :, half(h)] = value[i * width : (i + 1) * width]

    def body(p, _):
        if ready is not None:
            ready(p, f)
        strip = pl.multiple_of((f * 4 + p) * STRIP, STRIP)
        first = (p * 2 + f) * 2
        for r in range(0, rows, n):
            strips = edges[r // LANES, r % LANES : r % LANES + n, :]
            value = pltpu.roll(strips, LANES - VALUES_AT - strip, 1)
            y_slope = pltpu.roll(strips, LANES - SLOPES_AT - strip, 1)
            to = slice(RIM + r, RIM + r + n)
            for h in range(2):
                q = s_in[first + h, to, :]
                q = jnp.where(lane >= LANES - 2 if h else lane < 3, value, q)
                s[first + h, to, :] = q
                if adv is not None:
                    adv[f, p, r : r + n, half(h)] = q
                y = gy[first + h, r : r + n, :]
                put(1, p, r, h, jnp.where(lane >= LANES - 4 if h else lane < 5, y_slope, y))
        for h in range(2):

            def outer(kind, at, count):
                return edges[kind * 2 + h, pl.ds(strip + at, count), :]

            s[first + h, RIM - 2 : RIM + 3, :] = outer(1, 0, EDGE)
            s[first + h, RIM + rows - 3 : RIM + rows + 2, :] = outer(1, EDGE, EDGE)
            if adv is not None:
                adv[f, p, 0:3, half(h)] = outer(1, 2, 3)
                adv[f, p, rows - 3 : rows, half(h)] = outer(1, EDGE, 3)
            xy[f, 0, 1, p, 0:3, half(h)] = outer(2, 2, 3)
            xy[f, NP - 1, 1, p, width - 3 : width, half(h)] = outer(2, EDGE, 3)
            for r in range(0, rows, n):
                put(0, p, r, h, rows_slope(s.at[first + h], RIM + r, n))
        return 0

    lax.fori_loop(0, planes, body, 0, unroll=False)


def piece_of(owner, core, slot):
    rank = jnp.int32(0)
    piece = jnp.int32(0)
    for j in range(NP):
        mine = owner[0, j] == core
        piece = jnp.where(jnp.logical_and(mine, rank == slot), j, piece)
        rank = rank + mine.astype(jnp.int32)
    return piece, slot < rank


def clear(used, *refs):
    @pl.when(jnp.logical_not(used))
    def _():
        for ref in refs:
            ref[...] = jnp.zeros_like(ref)


def start_copy(used, src, zeros, to, sem):
    @pl.when(used)
    def _():
        pltpu.make_async_copy(src, to, sem).start()

    @pl.when(jnp.logical_not(used))
    def _():
        pltpu.make_async_copy(zeros, to, sem).start()


def own_slopes_kernel(
    owner,
    core,
    s_in,
    gy_in,
    edges,
    other_in,
    adv,
    grad,
    s,
    xy,
    other,
    gy,
    buf,
    zeros,
    adv_sem,
    sems,
    in_sems,
    other_sem,
):
    planes = xy.shape[3]
    me = core[0]
    mine = pl.ds(pl.multiple_of(planes * me, planes), planes)

    def arrival(p, f):
        at = pl.ds((p * 2 + f) * 2, 2)
        return pltpu.make_async_copy(gy_in.at[at], gy.at[at], in_sems.at[f, p])

    for f in range(2):
        for p in range(planes):
            arrival(p, f).start()
    bring = pltpu.make_async_copy(other_in, other, other_sem)
    bring.start()
    pieces = [piece_of(owner, me, slot) for slot in range(CAP)]
    clear(pieces[-1][1], zeros)

    def adv_copy(f):
        return pltpu.make_async_copy(buf.at[f], adv.at[f], adv_sem.at[f])

    for f in range(2):
        finish_field(f, s_in, gy, edges, s, xy, buf, lambda p, f: arrival(p, f).wait())
        adv_copy(f).start()
        for slot, (piece, used) in enumerate(pieces):
            start_copy(used, xy.at[f, piece], zeros, grad.at[slot, f, 0:2, mine], sems.at[slot, f])
    bring.wait()
    for f in range(2):
        adv_copy(f).wait()
        for slot in range(CAP):
            pltpu.make_async_copy(zeros, grad.at[slot, f, 0:2, mine], sems.at[slot, f]).wait()


SMEM = pl.BlockSpec(memory_space=pltpu.SMEM)
VMEM = pl.BlockSpec(memory_space=pltpu.VMEM)
ANY = pl.BlockSpec(memory_space=pl.ANY)


def own_slopes(owner, core, s_in, gy, edges, other):
    planes = s_in.shape[0] // 4
    rows = gy.shape[1]
    cols = 2 * LANES
    width = rows // NP
    return pl.pallas_call(
        own_slopes_kernel,
        in_specs=[SMEM, SMEM, VMEM, ANY, VMEM, ANY],
        out_specs=(ANY, ANY, VMEM, VMEM, VMEM),
        input_output_aliases={2: 2},
        out_shape=(
            out(2, planes, rows, cols),
            out(CAP, 2, 3, 2 * planes, width, cols),
            pltpu.VMEM(s_in.shape, F32),
            pltpu.VMEM((2, NP, 2, planes, width, cols), F32),
            pltpu.VMEM(other.shape, F32),
        ),
        scratch_shapes=[
            pltpu.VMEM(gy.shape, F32),
            pltpu.VMEM((2, planes, rows, cols), F32),
            pltpu.VMEM((2, planes, width, cols), F32),
            pltpu.SemaphoreType.DMA((2,)),
            pltpu.SemaphoreType.DMA((CAP, 2)),
            pltpu.SemaphoreType.DMA((2, planes)),
            pltpu.SemaphoreType.DMA,
        ],
        compiler_params=pltpu.CompilerParams(vmem_limit_bytes=14 * MIB),
        cost_estimate=SWEEP_COST,
        name="own_slopes",
    )(owner, core, s_in, gy, edges, other)


def gradient_kernel(
    owner,
    core,
    own,
    own_xy,
    other_in,
    other_gy,
    other_edges,
    grad_in,
    grad,
    wedge,
    other,
    other_xy,
    other_y,
    part,
    wpart,
    zeros,
    xy_zeros,
    in_sems,
    xy_sems,
    sems,
):
    planes, width = own_xy.shape[3:5]
    me = core[0]
    mine = pl.ds(pl.multiple_of(planes * me, planes), planes)
    theirs = pl.ds(pl.multiple_of(planes * (1 - me), planes), planes)

    def arrival(p, f):
        at = pl.ds((p * 2 + f) * 2, 2)
        return pltpu.make_async_copy(other_gy.at[at], other_y.at[at], in_sems.at[f, p])

    def ready(p, f):
        arrival(p, f).wait()

    for f in range(2):
        for p in range(planes):
            arrival(p, f).start()
    pieces = [piece_of(owner, me, slot) for slot in range(CAP)]
    clear(pieces[-1][1], zeros, xy_zeros)
    for f in range(2):
        finish_field(f, other_in, other_y, other_edges, other, other_xy, ready=ready)
        for slot, (piece, used) in enumerate(pieces):
            start_copy(
                used,
                other_xy.at[f, piece],
                xy_zeros,
                grad.at[slot, f, 0:2, theirs],
                xy_sems.at[slot, f],
            )

    def targets(slot):
        return grad.at[slot, 0, 2], grad.at[slot, 1, 2], wedge.at[slot]

    def fill(slot, piece):
        n = 8
        first = pl.multiple_of(piece * width, 8)

        def body(i, _):
            r = pl.ds(pl.multiple_of(RIM + first + i * n, n), n)
            to = pl.ds(pl.multiple_of(i * n, n), n)
            for h in range(2):
                cols = half(h)

                def plane(z, f):
                    ref = own if z < planes else other
                    return ref[((z % planes) * 2 + f) * 2 + h, r, :]

                q = [[plane(z, f) for f in range(2)] for z in range(8)]
                for z in range(8):
                    g = []
                    p = z % planes
                    zo = lax.rem(z + planes * me, 2 * planes)
                    xy = own_xy if z < planes else other_xy
                    for f in range(2):
                        z_slope = slope(
                            q[(z + 1) % 8][f] - q[(z + 7) % 8][f],
                            q[(z + 2) % 8][f] - q[(z + 6) % 8][f],
                        )
                        part[slot, f, zo, to, cols] = z_slope
                        g.append((xy[f, piece, 0, p, to, cols], xy[f, piece, 1, p, to, cols], z_slope))
                    rx, ry, rz = g[0]
                    tx, ty, tz = g[1]
                    a = ry * tz - rz * ty
                    b = rz * tx - rx * tz
                    c = rx * ty - ry * tx
                    wpart[slot, zo, to, cols] = a * a + b * b + c * c
            return 0

        lax.fori_loop(0, width // n, body, 0, unroll=False)

    def slot_body(slot, _):
        piece, used = piece_of(owner, me, slot)

        @pl.when(used)
        def _():
            fill(slot, piece)

        sources = part.at[slot, 0], part.at[slot, 1], wpart.at[slot]
        for k, (src, to) in enumerate(zip(sources, targets(slot))):
            start_copy(used, src, zeros, to, sems.at[slot, k])
        return 0

    lax.fori_loop(0, CAP, slot_body, 0, unroll=False)

    def wait_body(slot, _):
        for f in range(2):
            pltpu.make_async_copy(
                xy_zeros, grad.at[slot, f, 0:2, theirs], xy_sems.at[slot, f]
            ).wait()
        for k, to in enumerate(targets(slot)):
            pltpu.make_async_copy(zeros, to, sems.at[slot, k]).wait()
        return 0

    lax.fori_loop(0, CAP, wait_body, 0, unroll=False)


def gradients_of(owner, core, own, own_xy, other, other_gy, other_edges, grad):
    planes, width, cols = own_xy.shape[3:]
    return pl.pallas_call(
        gradient_kernel,
        in_specs=[SMEM, SMEM, VMEM, VMEM, VMEM, ANY, VMEM, ANY],
        out_specs=(ANY, ANY),
        out_shape=(out(*grad.shape), out(CAP, 2 * planes, width, cols)),
        scratch_shapes=[
            pltpu.VMEM(own.shape, F32),
            pltpu.VMEM(own_xy.shape, F32),
            pltpu.VMEM(other_gy.shape, F32),
            pltpu.VMEM((CAP, 2, 2 * planes, width, cols), F32),
            pltpu.VMEM((CAP, 2 * planes, width, cols), F32),
            pltpu.VMEM((2 * planes, width, cols), F32),
            pltpu.VMEM((2, planes, width, cols), F32),
            pltpu.SemaphoreType.DMA((2, planes)),
            pltpu.SemaphoreType.DMA((CAP, 2)),
            pltpu.SemaphoreType.DMA((CAP, 3)),
        ],
        input_output_aliases={7: 0},
        compiler_params=pltpu.CompilerParams(vmem_limit_bytes=24 * MIB),
        name="gradient",
    )(owner, core, own, own_xy, other, other_gy, other_edges, grad)


def per_device(density, heat, cx, cy, owner):
    nx, ny = lax.axis_size("gx"), lax.axis_size("gy")
    lo, hi = edge_rows((density, heat, cx, cy))
    left = lax.ppermute(hi, "gx", ring(nx, 1))
    right = lax.ppermute(lo, "gx", ring(nx, -1))
    x_e, cy_e, s_t, swept = inner(density, heat, cx, cy)
    h_t, hc_t, to_l, to_r, swept = x_edge(density, heat, cx, cy, left, right, x_e, cy_e, swept)
    other = lax.ppermute(swept, "sa", ring(2, 1))
    from_l = lax.ppermute(to_r, "gy", ring(ny, 1))
    from_r = lax.ppermute(to_l, "gy", ring(ny, -1))
    sh_t, gy = inner_slopes(s_t, h_t, hc_t)
    gy, from_l, from_r = lax.optimization_barrier((gy, from_l, from_r))
    other_gy = lax.ppermute(gy, "sa", ring(2, 1))
    edges = y_edge(x_e, cy_e, h_t, hc_t, from_l, from_r, sh_t)
    other_edges = lax.ppermute(edges, "sa", ring(2, 1))
    core = lax.axis_index("sa").astype(jnp.int32).reshape(1)
    advected, gradients, own, own_xy, other = own_slopes(owner, core, swept, gy, edges, other)
    gradients, wedge = gradients_of(
        owner, core, own, own_xy, other, other_gy, other_edges, gradients
    )
    return advected, gradients, wedge


def solution(mesh):
    block = P("sa", "gx", "gy")
    return jax.shard_map(
        per_device,
        mesh=mesh,
        in_specs=(block, block, block, block, P("gx", None)),
        out_specs=(
            P(None, "sa", "gx", "gy"),
            P(("gx", "sa"), None, None, None, None, "gy"),
            P(("gx", "sa"), None, None, "gy"),
        ),
        check_vma=False,
    )
```

```python
import jax
import jax.numpy as jnp
from jax import lax
from jax.experimental import pallas as pl
from jax.experimental.pallas import tpu as pltpu
from jax.sharding import PartitionSpec as P

CAP = 6
NP = 8
RIM = 8
LANES = 128
F32 = jnp.float32
MIB = 1024 * 1024


def ring(count, step):
    return [(i, (i + step) % count) for i in range(count)]


def coefficients(c):
    d = 1.0 - c
    m = c * d
    k_right = m * d
    k_left = m * c
    return k_right, k_left, c - k_right + k_left


def face_value(qm1, q0, q1, q2):
    return (7.0 / 12.0) * (q0 + q1) - (1.0 / 12.0) * (qm1 + q2)


def sweep_rows(load_q, load_c, store, a_scr, f_scr, base, count, chunk, fields=2):
    done = 0
    while done < count:
        n = min(chunk, count - done)
        r = base + done
        k_right, k_left, k_mid = coefficients(load_c(r, n))
        for f in range(fields):
            q0 = load_q(f, r, n)
            a = face_value(load_q(f, r - 1, n), q0, load_q(f, r + 1, n), load_q(f, r + 2, n))
            a_scr[f, pl.ds(8 + done, n), :] = a
            flux = k_right * a - k_left * a_scr[f, pl.ds(7 + done, n), :] + k_mid * q0
            f_scr[f, pl.ds(8 + done, n), :] = flux
            store(f, r, n, q0 - (flux - f_scr[f, pl.ds(7 + done, n), :]))
        done += n


def lane_iota(rows):
    return lax.broadcasted_iota(jnp.int32, (rows, LANES), 1)


def half(h, start=0):
    return slice(start + h * LANES, start + (h + 1) * LANES)


def call(
    kernel, out_shape, operands, name, spaces=None, scratch=(), aliases=None, cost=None, mib=20,
    out_spaces=None,
):
    vmem = pl.BlockSpec(memory_space=pltpu.VMEM)
    return pl.pallas_call(
        kernel,
        in_specs=[pl.BlockSpec(memory_space=x) for x in spaces] if spaces else [vmem] * len(operands),
        out_specs=tuple(pl.BlockSpec(memory_space=x) for x in out_spaces)
        if out_spaces
        else jax.tree.map(lambda _: vmem, out_shape),
        out_shape=tuple(
            x if space is pl.ANY else pltpu.VMEM(x.shape, F32)
            for x, space in zip(out_shape, out_spaces or [None] * len(out_shape))
        ),
        scratch_shapes=list(scratch),
        input_output_aliases=aliases or {},
        compiler_params=pltpu.CompilerParams(vmem_limit_bytes=mib * MIB),
        cost_estimate=cost,
        name=name,
    )(*operands)


def out(*shape):
    return jax.ShapeDtypeStruct(shape, F32)


SWEEP_COST = pl.CostEstimate(flops=20_000_000, bytes_accessed=6_000_000, transcendentals=0)


LAST = (5, 5, 3, 2)
FIRST = (4, 4, 2, 2)


def padded(rows):
    return -(-rows // 8) * 8


def place(counts, p, f):
    return p * sum(counts) + sum(counts[:f]), counts[f]


def edge_rows_kernel(d, t, cx, cy, lo, hi, first, last, sems):
    planes, rows, _ = d.shape
    copies = []
    for f, ref in enumerate((d, t, cx, cy)):
        copies.append(pltpu.make_async_copy(ref.at[:, 0:RIM, :], first.at[f], sems.at[f]))
        copies.append(
            pltpu.make_async_copy(ref.at[:, rows - RIM : rows, :], last.at[f], sems.at[4 + f])
        )
    for c in copies:
        c.start()
    for c in copies:
        c.wait()
    for p in range(planes):
        for f in range(4):
            at, n = place(FIRST, p, f)
            lo[at : at + n, :] = first[f, p, 0:n, :]
            at, n = place(LAST, p, f)
            hi[at : at + n, :] = last[f, p, RIM - n : RIM, :]


def edge_rows(fields):
    planes, _, cols = fields[0].shape
    tiles = pltpu.VMEM((4, planes, RIM, cols), F32)
    return call(
        edge_rows_kernel,
        (out(padded(planes * sum(FIRST)), cols), out(padded(planes * sum(LAST)), cols)),
        [pltpu.with_memory_space_constraint(x, pltpu.HBM) for x in fields],
        "edge_rows",
        spaces=[pl.ANY] * 4,
        scratch=[tiles, tiles, pltpu.SemaphoreType.DMA((8,))],
        mib=8,
    )


def inner_kernel(d, t, cx, cy, x_e, cy_e, s_t, s, win, xs, x_t, cy_t, a_scr, f_scr):
    planes, rows, _ = d.shape

    def body(p, _):
        for h in range(2):
            for f, ref in enumerate((d, t, cx)):
                win[f, 0:rows, :] = ref[p, :, half(h)]

            def store(f, r, n, value):
                xs[f, h, pl.ds(RIM + r, n), :] = value

            sweep_rows(
                lambda f, r, n: win[f, pl.ds(r, n), :],
                lambda r, n: win[2, pl.ds(r, n), :],
                store,
                a_scr,
                f_scr,
                1,
                rows,
                32,
            )
            for x in range(2):
                cy_t[x, half(h, RIM), :] = cy[p, half(x), half(h)].T
        for x in range(2):
            for f in range(2):
                for h in range(2):
                    x_t[f, x, half(h, RIM), :] = xs[f, h, half(x, RIM), :].T

            def store_t(f, r, n, value):
                s_t[p, f, x, pl.ds(r, n), :] = value

            sweep_rows(
                lambda f, r, n: x_t[f, x, pl.ds(r, n), :],
                lambda r, n: cy_t[x, pl.ds(r, n), :],
                store_t,
                a_scr,
                f_scr,
                RIM + 1,
                rows,
                32,
            )
            for f in range(2):
                for h in range(2):
                    s[(p * 2 + f) * 2 + h, half(x, RIM), :] = s_t[p, f, x, half(h, RIM), :].T
            for high, at in enumerate((slice(RIM, 16 + RIM), slice(rows + RIM - 16, rows + RIM))):
                cy_e[high, p, x] = cy_t[x, at, :]
                for f in range(2):
                    x_e[high, p, f, x] = x_t[f, x, at, :]
        return 0

    lax.fori_loop(0, planes, body, 0, unroll=False)


def inner(d, t, cx, cy):
    planes, rows, cols = d.shape
    ext = rows + 2 * RIM
    return call(
        inner_kernel,
        (
            out(2, planes, 2, 2, 16, LANES),
            out(2, planes, 2, 16, LANES),
            out(planes, 2, 2, ext, LANES),
            out(4 * planes, ext, LANES),
        ),
        (d, t, cx, cy),
        "inner",
        scratch=[pltpu.VMEM((3, ext, LANES), F32)]
        + [pltpu.VMEM((2, 2, ext, LANES), F32)] * 2
        + [pltpu.VMEM((2, ext, LANES), F32)]
        + [pltpu.VMEM((2, ext, LANES), F32)] * 2,
        cost=SWEEP_COST,
        mib=16,
    )


def edge_sweep(own, rim, high, win, a_scr, f_scr, res):
    lead, rim_at = (0, 16) if high else (8, 0)
    for f in range(3):
        win[f, lead : lead + 16, :] = own(f)
        beyond = rim(f)
        if beyond is not None:
            n = beyond.shape[0]
            at = rim_at if high else 8 - n
            win[f, at : at + n, :] = beyond

    def store(f, r, n, value):
        res[f, pl.ds(r, n), :] = value

    sweep_rows(
        lambda f, r, n: win[f, pl.ds(r, n), :],
        lambda r, n: win[2, pl.ds(r, n), :],
        store,
        a_scr,
        f_scr,
        6 if high else 4,
        16,
        16,
    )


EDGE_SCRATCH = [
    pltpu.VMEM((3, 32, LANES), F32),
    pltpu.VMEM((2, 32, LANES), F32),
    pltpu.VMEM((2, 32, LANES), F32),
    pltpu.VMEM((2, 32, LANES), F32),
]


STRIP = 16
EDGE = 5


def x_edge_kernel(
    d,
    t,
    cx,
    cy,
    left,
    right,
    x_e,
    cy_e,
    h_t,
    hc_t,
    to_l,
    to_r,
    q_rows,
    c_rows,
    win,
    a_scr,
    f_scr,
    res,
):
    planes, rows, _ = d.shape

    for p in range(planes):
        for h in range(2):
            for high in range(2):
                rim, counts = (right, FIRST) if high else (left, LAST)
                at = slice(rows - 16, rows) if high else slice(0, 16)

                def beyond(f):
                    r, n = place(counts, p, f)
                    return rim[r : r + n, half(h)]

                edge_sweep(
                    lambda f: (d, t, cx)[f][p, at, half(h)],
                    beyond,
                    high,
                    win,
                    a_scr,
                    f_scr,
                    res,
                )
                for f in range(2):
                    k = (f * 4 + p) * STRIP + EDGE * high
                    if high:
                        q_rows[h, k : k + EDGE, :] = res[f, 13:18, :]
                        c_rows[h, k : k + 3, :] = cy[p, rows - 3 : rows, half(h)]
                        c_rows[h, k + 3 : k + EDGE, :] = beyond(3)
                    else:
                        q_rows[h, k : k + EDGE, :] = res[f, 6:11, :]
                        c_rows[h, k : k + 2, :] = beyond(3)
                        c_rows[h, k + 2 : k + EDGE, :] = cy[p, 0:3, half(h)]
    for h in range(2):
        h_t[half(h, RIM), :] = q_rows[h].T
        hc_t[half(h, RIM), :] = c_rows[h].T
    for buf, counts in ((to_l, FIRST), (to_r, LAST)):

        last = counts is LAST

        def put(i, f, ref, start, stop):
            at, n = y_place(counts, i, f)
            top = stop - n if last else start
            buf[at : at + n, :] = ref[top : top + n, :]

        for p in range(planes):
            for x in range(2):
                for f in range(2):
                    put((p * 2 + f) * 2 + x, 0, x_e.at[int(last), p, f, x], 0, 16)
                put(p * 2 + x, 2, cy_e.at[int(last), p, x], 0, 16)
        put(16, 0, h_t, RIM, RIM + rows)
        put(8, 2, hc_t, RIM, RIM + rows)


def y_place(counts, i, f):
    return (17 * counts[0] if f == 2 else 0) + i * counts[f], counts[f]


def y_rim(counts):
    return out(padded(17 * counts[0] + 9 * counts[2]), LANES)


def x_edge(d, t, cx, cy, left, right, x_e, cy_e):
    ext = d.shape[1] + 2 * RIM
    return call(
        x_edge_kernel,
        (out(ext, LANES), out(ext, LANES), y_rim(FIRST), y_rim(LAST)),
        (d, t, cx, cy, left, right, x_e, cy_e),
        "x_edge",
        mib=12,
        scratch=[pltpu.VMEM((2, LANES, LANES), F32)] * 2 + EDGE_SCRATCH,
    )


def slope(w1, w2):
    return (2.0 / 3.0) * w1 - (1.0 / 12.0) * w2


def rows_slope(ref, r, n):
    return slope(
        ref[pl.ds(r + 1, n), :] - ref[pl.ds(r - 1, n), :],
        ref[pl.ds(r + 2, n), :] - ref[pl.ds(r - 2, n), :],
    )


def inner_slopes_kernel(s_t, h_t, hc_t, gy, sh_t, a_scr, f_scr):
    planes, _, _, ext, _ = s_t.shape
    rows = ext - 2 * RIM

    def body(p, _):
        for f in range(2):
            for x in range(2):
                for h in range(2):
                    gy[(p * 2 + f) * 2 + h, half(x), :] = rows_slope(
                        s_t.at[p, f, x], RIM + h * LANES, LANES
                    ).T
        return 0

    lax.fori_loop(0, planes, body, 0, unroll=False)

    def store(f, r, n, value):
        sh_t[pl.ds(r, n), :] = value

    sweep_rows(
        lambda f, r, n: h_t[pl.ds(r, n), :],
        lambda r, n: hc_t[pl.ds(r, n), :],
        store,
        a_scr,
        f_scr,
        RIM + 1,
        rows,
        32,
        fields=1,
    )


def inner_slopes(s_t, h_t, hc_t):
    planes, _, _, ext, _ = s_t.shape
    return call(
        inner_slopes_kernel,
        (out(4 * planes, ext - 2 * RIM, LANES), out(ext, LANES)),
        (s_t, h_t, hc_t),
        "inner_slopes",
        mib=8,
        scratch=[pltpu.VMEM((2, ext, LANES), F32)] * 2,
        cost=SWEEP_COST,
    )


VALUES_AT = 2
SLOPES_AT = 9


def y_edge_kernel(
    x_e,
    cy_e,
    h_t,
    hc_t,
    from_l,
    from_r,
    sh_in,
    sh_t,
    edges,
    strips,
    win,
    a_scr,
    f_scr,
    res,
):
    planes = x_e.shape[1]
    ext = h_t.shape[0]

    for high in range(2):
        rim, counts = (from_r, FIRST) if high else (from_l, LAST)
        at = slice(ext - 24, ext - 8) if high else slice(8, 24)

        def beyond(i, f):
            r, n = y_place(counts, i, f)
            return rim[r : r + n, :]

        for p in range(planes):
            for x in range(2):
                edge_sweep(
                    lambda f: cy_e[high, p, x] if f == 2 else x_e[high, p, f, x],
                    lambda f: beyond(p * 2 + x if f == 2 else (p * 2 + f) * 2 + x, f),
                    high,
                    win,
                    a_scr,
                    f_scr,
                    res,
                )
                for f in range(2):
                    k = (f * 4 + p) * STRIP
                    slopes = rows_slope(res.at[f], 8, 8)
                    if high:
                        strips[x, k : k + 2, :] = res[f, 14:16, :]
                        strips[x, k + 5 : k + 9, :] = slopes[4:8]
                    else:
                        strips[x, k + 2 : k + 5, :] = res[f, 8:11, :]
                        strips[x, k + 9 : k + 14, :] = slopes[0:5]
        edge_sweep(
            lambda f: hc_t[at, :] if f == 2 else h_t[at, :],
            lambda f: beyond(8, 2) if f == 2 else beyond(16, 0),
            high,
            win,
            a_scr,
            f_scr,
            res,
        )
        if high:
            sh_t[ext - 16 : ext, :] = res[0, 8:24, :]
        else:
            sh_t[0:16, :] = res[0, 0:16, :]
    for i in range(2):
        edges[i] = strips[i].T
        edges[2 + i] = sh_t[half(i, RIM), :].T
        edges[4 + i] = rows_slope(sh_t, RIM + i * LANES, LANES).T


def y_edge(x_e, cy_e, h_t, hc_t, from_l, from_r, sh_t):
    return call(
        y_edge_kernel,
        (out(*sh_t.shape), out(6, LANES, LANES)),
        (x_e, cy_e, h_t, hc_t, from_l, from_r, sh_t),
        "y_edge",
        mib=8,
        scratch=[pltpu.VMEM((2, LANES, LANES), F32)] + EDGE_SCRATCH,
        aliases={6: 0},
    )[1]


def finish_field(f, s_in, gy, edges, s, xy, adv=None):
    planes, width = xy.shape[3:5]
    rows = NP * width
    n = 2 * width
    lane = lane_iota(n)

    def put(dim, p, r, h, value):
        for i in range(n // width):
            xy[f, r // width + i, dim, p, :, half(h)] = value[i * width : (i + 1) * width]

    def body(p, _):
        strip = pl.multiple_of((f * 4 + p) * STRIP, STRIP)
        first = (p * 2 + f) * 2
        for r in range(0, rows, n):
            strips = edges[r // LANES, r % LANES : r % LANES + n, :]
            value = pltpu.roll(strips, LANES - VALUES_AT - strip, 1)
            y_slope = pltpu.roll(strips, LANES - SLOPES_AT - strip, 1)
            to = slice(RIM + r, RIM + r + n)
            for h in range(2):
                q = s_in[first + h, to, :]
                q = jnp.where(lane >= LANES - 2 if h else lane < 3, value, q)
                s[first + h, to, :] = q
                if adv is not None:
                    adv[f, p, r : r + n, half(h)] = q
                y = gy[first + h, r : r + n, :]
                put(1, p, r, h, jnp.where(lane >= LANES - 4 if h else lane < 5, y_slope, y))
        for h in range(2):

            def outer(kind, at, count):
                return edges[kind * 2 + h, pl.ds(strip + at, count), :]

            s[first + h, RIM - 2 : RIM + 3, :] = outer(1, 0, EDGE)
            s[first + h, RIM + rows - 3 : RIM + rows + 2, :] = outer(1, EDGE, EDGE)
            if adv is not None:
                adv[f, p, 0:3, half(h)] = outer(1, 2, 3)
                adv[f, p, rows - 3 : rows, half(h)] = outer(1, EDGE, 3)
            xy[f, 0, 1, p, 0:3, half(h)] = outer(2, 2, 3)
            xy[f, NP - 1, 1, p, width - 3 : width, half(h)] = outer(2, EDGE, 3)
            for r in range(0, rows, n):
                put(0, p, r, h, rows_slope(s.at[first + h], RIM + r, n))
        return 0

    lax.fori_loop(0, planes, body, 0, unroll=False)


def piece_of(owner, core, slot):
    rank = jnp.int32(0)
    piece = jnp.int32(0)
    for j in range(NP):
        mine = owner[0, j] == core
        piece = jnp.where(jnp.logical_and(mine, rank == slot), j, piece)
        rank = rank + mine.astype(jnp.int32)
    return piece, slot < rank


def clear(used, *refs):
    @pl.when(jnp.logical_not(used))
    def _():
        for ref in refs:
            ref[...] = jnp.zeros_like(ref)


def start_copy(used, src, zeros, to, sem):
    @pl.when(used)
    def _():
        pltpu.make_async_copy(src, to, sem).start()

    @pl.when(jnp.logical_not(used))
    def _():
        pltpu.make_async_copy(zeros, to, sem).start()


def own_slopes_kernel(owner, s_in, gy, edges, adv, grad, s, xy, buf, zeros, adv_sem, sems):
    planes = xy.shape[3]
    me = lax.axis_index("sa")
    mine = pl.ds(pl.multiple_of(planes * me, planes), planes)
    pieces = [piece_of(owner, me, slot) for slot in range(CAP)]
    clear(pieces[-1][1], zeros)

    def adv_copy(f):
        return pltpu.make_async_copy(buf.at[f], adv.at[f], adv_sem.at[f])

    for f in range(2):
        finish_field(f, s_in, gy, edges, s, xy, buf)
        adv_copy(f).start()
        for slot, (piece, used) in enumerate(pieces):
            start_copy(used, xy.at[f, piece], zeros, grad.at[slot, f, 0:2, mine], sems.at[slot, f])
    for f in range(2):
        adv_copy(f).wait()
        for slot in range(CAP):
            pltpu.make_async_copy(zeros, grad.at[slot, f, 0:2, mine], sems.at[slot, f]).wait()


SMEM = pl.BlockSpec(memory_space=pltpu.SMEM)
VMEM = pl.BlockSpec(memory_space=pltpu.VMEM)
ANY = pl.BlockSpec(memory_space=pl.ANY)


def own_slopes(owner, s_in, gy, edges):
    planes = s_in.shape[0] // 4
    rows = gy.shape[1]
    cols = 2 * LANES
    width = rows // NP
    return pl.pallas_call(
        own_slopes_kernel,
        in_specs=[SMEM, VMEM, VMEM, VMEM],
        out_specs=(ANY, ANY, VMEM, VMEM),
        out_shape=(
            out(2, planes, rows, cols),
            out(CAP, 2, 3, 2 * planes, width, cols),
            pltpu.VMEM(s_in.shape, F32),
            pltpu.VMEM((2, NP, 2, planes, width, cols), F32),
        ),
        scratch_shapes=[
            pltpu.VMEM((2, planes, rows, cols), F32),
            pltpu.VMEM((2, planes, width, cols), F32),
            pltpu.SemaphoreType.DMA((2,)),
            pltpu.SemaphoreType.DMA((CAP, 2)),
        ],
        compiler_params=pltpu.CompilerParams(vmem_limit_bytes=14 * MIB),
        cost_estimate=SWEEP_COST,
        name="own_slopes",
    )(owner, s_in, gy, edges)


def gradient_kernel(
    owner,
    own,
    own_xy,
    other_in,
    other_gy,
    other_edges,
    grad_in,
    grad,
    wedge,
    other,
    other_xy,
    part,
    wpart,
    zeros,
    xy_zeros,
    xy_sems,
    sems,
):
    planes, width = own_xy.shape[3:5]
    me = lax.axis_index("sa")
    mine = pl.ds(pl.multiple_of(planes * me, planes), planes)
    theirs = pl.ds(pl.multiple_of(planes * (1 - me), planes), planes)

    pieces = [piece_of(owner, me, slot) for slot in range(CAP)]
    clear(pieces[-1][1], zeros, xy_zeros)
    for f in range(2):
        finish_field(f, other_in, other_gy, other_edges, other, other_xy)
        for slot, (piece, used) in enumerate(pieces):
            start_copy(
                used,
                other_xy.at[f, piece],
                xy_zeros,
                grad.at[slot, f, 0:2, theirs],
                xy_sems.at[slot, f],
            )

    def targets(slot):
        return grad.at[slot, 0, 2], grad.at[slot, 1, 2], wedge.at[slot]

    def fill(slot, piece):
        n = 8
        first = pl.multiple_of(piece * width, 8)

        def body(i, _):
            r = pl.ds(pl.multiple_of(RIM + first + i * n, n), n)
            to = pl.ds(pl.multiple_of(i * n, n), n)
            for h in range(2):
                cols = half(h)

                def plane(z, f):
                    ref = own if z < planes else other
                    return ref[((z % planes) * 2 + f) * 2 + h, r, :]

                q = [[plane(z, f) for f in range(2)] for z in range(8)]
                for z in range(8):
                    g = []
                    p = z % planes
                    zo = lax.rem(z + planes * me, 2 * planes)
                    xy = own_xy if z < planes else other_xy
                    for f in range(2):
                        z_slope = slope(
                            q[(z + 1) % 8][f] - q[(z + 7) % 8][f],
                            q[(z + 2) % 8][f] - q[(z + 6) % 8][f],
                        )
                        part[slot, f, zo, to, cols] = z_slope
                        g.append((xy[f, piece, 0, p, to, cols], xy[f, piece, 1, p, to, cols], z_slope))
                    rx, ry, rz = g[0]
                    tx, ty, tz = g[1]
                    a = ry * tz - rz * ty
                    b = rz * tx - rx * tz
                    c = rx * ty - ry * tx
                    wpart[slot, zo, to, cols] = a * a + b * b + c * c
            return 0

        lax.fori_loop(0, width // n, body, 0, unroll=False)

    def slot_body(slot, _):
        piece, used = piece_of(owner, me, slot)

        @pl.when(used)
        def _():
            fill(slot, piece)

        sources = part.at[slot, 0], part.at[slot, 1], wpart.at[slot]
        for k, (src, to) in enumerate(zip(sources, targets(slot))):
            start_copy(used, src, zeros, to, sems.at[slot, k])
        return 0

    lax.fori_loop(0, CAP, slot_body, 0, unroll=False)

    def wait_body(slot, _):
        for f in range(2):
            pltpu.make_async_copy(
                xy_zeros, grad.at[slot, f, 0:2, theirs], xy_sems.at[slot, f]
            ).wait()
        for k, to in enumerate(targets(slot)):
            pltpu.make_async_copy(zeros, to, sems.at[slot, k]).wait()
        return 0

    lax.fori_loop(0, CAP, wait_body, 0, unroll=False)


def gradients_of(owner, own, own_xy, other, other_gy, other_edges, grad):
    planes, width, cols = own_xy.shape[3:]
    return pl.pallas_call(
        gradient_kernel,
        in_specs=[SMEM, VMEM, VMEM, VMEM, VMEM, VMEM, ANY],
        out_specs=(ANY, ANY),
        out_shape=(out(*grad.shape), out(CAP, 2 * planes, width, cols)),
        scratch_shapes=[
            pltpu.VMEM(own.shape, F32),
            pltpu.VMEM(own_xy.shape, F32),
            pltpu.VMEM((CAP, 2, 2 * planes, width, cols), F32),
            pltpu.VMEM((CAP, 2 * planes, width, cols), F32),
            pltpu.VMEM((2 * planes, width, cols), F32),
            pltpu.VMEM((2, planes, width, cols), F32),
            pltpu.SemaphoreType.DMA((CAP, 2)),
            pltpu.SemaphoreType.DMA((CAP, 3)),
        ],
        input_output_aliases={6: 0},
        compiler_params=pltpu.CompilerParams(vmem_limit_bytes=24 * MIB),
        name="gradient",
    )(owner, own, own_xy, other, other_gy, other_edges, grad)


def per_device(density, heat, cx, cy, owner):
    nx, ny = lax.axis_size("gx"), lax.axis_size("gy")
    lo, hi = edge_rows((density, heat, cx, cy))
    left = lax.ppermute(hi, "gx", ring(nx, 1))
    right = lax.ppermute(lo, "gx", ring(nx, -1))
    x_e, cy_e, s_t, swept = inner(density, heat, cx, cy)
    h_t, hc_t, to_l, to_r = x_edge(density, heat, cx, cy, left, right, x_e, cy_e)
    sent, to_l, to_r = lax.optimization_barrier((swept, to_l, to_r))
    other = lax.ppermute(sent, "sa", ring(2, 1))
    from_l = lax.ppermute(to_r, "gy", ring(ny, 1))
    from_r = lax.ppermute(to_l, "gy", ring(ny, -1))
    gy, sh_t = inner_slopes(s_t, h_t, hc_t)
    sent, from_l, from_r = lax.optimization_barrier((gy, from_l, from_r))
    other_gy = lax.ppermute(sent, "sa", ring(2, 1))
    edges = y_edge(x_e, cy_e, h_t, hc_t, from_l, from_r, sh_t)
    other_edges = lax.ppermute(edges, "sa", ring(2, 1))
    advected, gradients, own, own_xy = own_slopes(owner, swept, gy, edges)
    gradients, wedge = gradients_of(owner, own, own_xy, other, other_gy, other_edges, gradients)
    return advected, gradients, wedge


def solution(mesh):
    block = P("sa", "gx", "gy")
    return jax.shard_map(
        per_device,
        mesh=mesh,
        in_specs=(block, block, block, block, P("gx", None)),
        out_specs=(
            P(None, "sa", "gx", "gy"),
            P(("gx", "sa"), None, None, None, None, "gy"),
            P(("gx", "sa"), None, None, "gy"),
        ),
        check_vma=False,
    )
```

```python
import jax
import jax.numpy as jnp
from jax import lax
from jax.experimental import pallas as pl
from jax.experimental.pallas import tpu as pltpu
from jax.sharding import PartitionSpec as P

CAP = 6
NP = 8
RIM = 8
LANES = 128
F32 = jnp.float32
MIB = 1024 * 1024


def ring(count, step):
    return [(i, (i + step) % count) for i in range(count)]


def coefficients(c):
    d = 1.0 - c
    m = c * d
    k_right = m * d
    k_left = m * c
    return k_right, k_left, c - k_right + k_left


def face_value(qm1, q0, q1, q2):
    return (7.0 / 12.0) * (q0 + q1) - (1.0 / 12.0) * (qm1 + q2)


def sweep_rows(load_q, load_c, store, a_scr, f_scr, base, count, chunk, fields=2):
    done = 0
    while done < count:
        n = min(chunk, count - done)
        r = base + done
        k_right, k_left, k_mid = coefficients(load_c(r, n))
        for f in range(fields):
            q0 = load_q(f, r, n)
            a = face_value(load_q(f, r - 1, n), q0, load_q(f, r + 1, n), load_q(f, r + 2, n))
            a_scr[f, pl.ds(8 + done, n), :] = a
            flux = k_right * a - k_left * a_scr[f, pl.ds(7 + done, n), :] + k_mid * q0
            f_scr[f, pl.ds(8 + done, n), :] = flux
            store(f, r, n, q0 - (flux - f_scr[f, pl.ds(7 + done, n), :]))
        done += n


def lane_iota(rows):
    return lax.broadcasted_iota(jnp.int32, (rows, LANES), 1)


def half(h, start=0):
    return slice(start + h * LANES, start + (h + 1) * LANES)


def call(
    kernel, out_shape, operands, name, spaces=None, scratch=(), aliases=None, cost=None, mib=20,
    out_spaces=None,
):
    vmem = pl.BlockSpec(memory_space=pltpu.VMEM)
    return pl.pallas_call(
        kernel,
        in_specs=[pl.BlockSpec(memory_space=x) for x in spaces] if spaces else [vmem] * len(operands),
        out_specs=tuple(pl.BlockSpec(memory_space=x) for x in out_spaces)
        if out_spaces
        else jax.tree.map(lambda _: vmem, out_shape),
        out_shape=tuple(
            x if space is pl.ANY else pltpu.VMEM(x.shape, F32)
            for x, space in zip(out_shape, out_spaces or [None] * len(out_shape))
        ),
        scratch_shapes=list(scratch),
        input_output_aliases=aliases or {},
        compiler_params=pltpu.CompilerParams(vmem_limit_bytes=mib * MIB),
        cost_estimate=cost,
        name=name,
    )(*operands)


def out(*shape):
    return jax.ShapeDtypeStruct(shape, F32)


SWEEP_COST = pl.CostEstimate(flops=20_000_000, bytes_accessed=6_000_000, transcendentals=0)


LAST = (5, 5, 3, 2)
FIRST = (4, 4, 2, 2)


def padded(rows):
    return -(-rows // 8) * 8


def place(counts, p, f):
    return p * sum(counts) + sum(counts[:f]), counts[f]


def edge_rows_kernel(d, t, cx, cy, lo, hi, first, last, sems):
    planes, rows, _ = d.shape
    copies = []
    for f, ref in enumerate((d, t, cx, cy)):
        copies.append(pltpu.make_async_copy(ref.at[:, 0:RIM, :], first.at[f], sems.at[f]))
        copies.append(
            pltpu.make_async_copy(ref.at[:, rows - RIM : rows, :], last.at[f], sems.at[4 + f])
        )
    for c in copies:
        c.start()
    for c in copies:
        c.wait()
    for p in range(planes):
        for f in range(4):
            at, n = place(FIRST, p, f)
            lo[at : at + n, :] = first[f, p, 0:n, :]
            at, n = place(LAST, p, f)
            hi[at : at + n, :] = last[f, p, RIM - n : RIM, :]


def edge_rows(fields):
    planes, _, cols = fields[0].shape
    tiles = pltpu.VMEM((4, planes, RIM, cols), F32)
    return call(
        edge_rows_kernel,
        (out(padded(planes * sum(FIRST)), cols), out(padded(planes * sum(LAST)), cols)),
        [pltpu.with_memory_space_constraint(x, pltpu.HBM) for x in fields],
        "edge_rows",
        spaces=[pl.ANY] * 4,
        scratch=[tiles, tiles, pltpu.SemaphoreType.DMA((8,))],
        mib=8,
    )


def inner_kernel(d, t, cx, cy, x_e, cy_e, s_t, s, win, xs, x_t, cy_t, a_scr, f_scr):
    planes, rows, _ = d.shape

    def body(p, _):
        for h in range(2):
            for f, ref in enumerate((d, t, cx)):
                win[f, 0:rows, :] = ref[p, :, half(h)]

            def store(f, r, n, value):
                xs[f, h, pl.ds(RIM + r, n), :] = value

            sweep_rows(
                lambda f, r, n: win[f, pl.ds(r, n), :],
                lambda r, n: win[2, pl.ds(r, n), :],
                store,
                a_scr,
                f_scr,
                1,
                rows,
                32,
            )
            for x in range(2):
                cy_t[x, half(h, RIM), :] = cy[p, half(x), half(h)].T
        for x in range(2):
            for f in range(2):
                for h in range(2):
                    x_t[f, x, half(h, RIM), :] = xs[f, h, half(x, RIM), :].T

            def store_t(f, r, n, value):
                s_t[p, f, x, pl.ds(r, n), :] = value

            sweep_rows(
                lambda f, r, n: x_t[f, x, pl.ds(r, n), :],
                lambda r, n: cy_t[x, pl.ds(r, n), :],
                store_t,
                a_scr,
                f_scr,
                RIM + 1,
                rows,
                32,
            )
            for f in range(2):
                for h in range(2):
                    s[(p * 2 + f) * 2 + h, half(x, RIM), :] = s_t[p, f, x, half(h, RIM), :].T
            for high, at in enumerate((slice(RIM, 16 + RIM), slice(rows + RIM - 16, rows + RIM))):
                cy_e[high, p, x] = cy_t[x, at, :]
                for f in range(2):
                    x_e[high, p, f, x] = x_t[f, x, at, :]
        return 0

    lax.fori_loop(0, planes, body, 0, unroll=False)


def inner(d, t, cx, cy):
    planes, rows, cols = d.shape
    ext = rows + 2 * RIM
    return call(
        inner_kernel,
        (
            out(2, planes, 2, 2, 16, LANES),
            out(2, planes, 2, 16, LANES),
            out(planes, 2, 2, ext, LANES),
            out(4 * planes, ext, LANES),
        ),
        (d, t, cx, cy),
        "inner",
        scratch=[pltpu.VMEM((3, ext, LANES), F32)]
        + [pltpu.VMEM((2, 2, ext, LANES), F32)] * 2
        + [pltpu.VMEM((2, ext, LANES), F32)]
        + [pltpu.VMEM((2, ext, LANES), F32)] * 2,
        cost=SWEEP_COST,
        mib=16,
    )


def edge_sweep(own, rim, high, win, a_scr, f_scr, res):
    lead, rim_at = (0, 16) if high else (8, 0)
    for f in range(3):
        win[f, lead : lead + 16, :] = own(f)
        beyond = rim(f)
        if beyond is not None:
            n = beyond.shape[0]
            at = rim_at if high else 8 - n
            win[f, at : at + n, :] = beyond

    def store(f, r, n, value):
        res[f, pl.ds(r, n), :] = value

    sweep_rows(
        lambda f, r, n: win[f, pl.ds(r, n), :],
        lambda r, n: win[2, pl.ds(r, n), :],
        store,
        a_scr,
        f_scr,
        6 if high else 4,
        16,
        16,
    )


EDGE_SCRATCH = [
    pltpu.VMEM((3, 32, LANES), F32),
    pltpu.VMEM((2, 32, LANES), F32),
    pltpu.VMEM((2, 32, LANES), F32),
    pltpu.VMEM((2, 32, LANES), F32),
]


STRIP = 16
EDGE = 5


def x_edge_kernel(
    d,
    t,
    cx,
    cy,
    left,
    right,
    x_e,
    cy_e,
    h_t,
    hc_t,
    to_l,
    to_r,
    q_rows,
    c_rows,
    win,
    a_scr,
    f_scr,
    res,
):
    planes, rows, _ = d.shape

    for p in range(planes):
        for h in range(2):
            for high in range(2):
                rim, counts = (right, FIRST) if high else (left, LAST)
                at = slice(rows - 16, rows) if high else slice(0, 16)

                def beyond(f):
                    r, n = place(counts, p, f)
                    return rim[r : r + n, half(h)]

                edge_sweep(
                    lambda f: (d, t, cx)[f][p, at, half(h)],
                    beyond,
                    high,
                    win,
                    a_scr,
                    f_scr,
                    res,
                )
                for f in range(2):
                    k = (f * 4 + p) * STRIP + EDGE * high
                    if high:
                        q_rows[h, k : k + EDGE, :] = res[f, 13:18, :]
                        c_rows[h, k : k + 3, :] = cy[p, rows - 3 : rows, half(h)]
                        c_rows[h, k + 3 : k + EDGE, :] = beyond(3)
                    else:
                        q_rows[h, k : k + EDGE, :] = res[f, 6:11, :]
                        c_rows[h, k : k + 2, :] = beyond(3)
                        c_rows[h, k + 2 : k + EDGE, :] = cy[p, 0:3, half(h)]
    for h in range(2):
        h_t[half(h, RIM), :] = q_rows[h].T
        hc_t[half(h, RIM), :] = c_rows[h].T
    for buf, counts in ((to_l, FIRST), (to_r, LAST)):

        last = counts is LAST

        def put(i, f, ref, start, stop):
            at, n = y_place(counts, i, f)
            top = stop - n if last else start
            buf[at : at + n, :] = ref[top : top + n, :]

        for p in range(planes):
            for x in range(2):
                for f in range(2):
                    put((p * 2 + f) * 2 + x, 0, x_e.at[int(last), p, f, x], 0, 16)
                put(p * 2 + x, 2, cy_e.at[int(last), p, x], 0, 16)
        put(16, 0, h_t, RIM, RIM + rows)
        put(8, 2, hc_t, RIM, RIM + rows)


def y_place(counts, i, f):
    return (17 * counts[0] if f == 2 else 0) + i * counts[f], counts[f]


def y_rim(counts):
    return out(padded(17 * counts[0] + 9 * counts[2]), LANES)


def x_edge(d, t, cx, cy, left, right, x_e, cy_e):
    ext = d.shape[1] + 2 * RIM
    return call(
        x_edge_kernel,
        (out(ext, LANES), out(ext, LANES), y_rim(FIRST), y_rim(LAST)),
        (d, t, cx, cy, left, right, x_e, cy_e),
        "x_edge",
        mib=12,
        scratch=[pltpu.VMEM((2, LANES, LANES), F32)] * 2 + EDGE_SCRATCH,
    )


def slope(w1, w2):
    return (2.0 / 3.0) * w1 - (1.0 / 12.0) * w2


def rows_slope(ref, r, n):
    return slope(
        ref[pl.ds(r + 1, n), :] - ref[pl.ds(r - 1, n), :],
        ref[pl.ds(r + 2, n), :] - ref[pl.ds(r - 2, n), :],
    )


def inner_slopes_kernel(s_t, h_t, hc_t, gy, sh_t, a_scr, f_scr):
    planes, _, _, ext, _ = s_t.shape
    rows = ext - 2 * RIM

    def body(p, _):
        for f in range(2):
            for x in range(2):
                for h in range(2):
                    gy[(p * 2 + f) * 2 + h, half(x), :] = rows_slope(
                        s_t.at[p, f, x], RIM + h * LANES, LANES
                    ).T
        return 0

    lax.fori_loop(0, planes, body, 0, unroll=False)

    def store(f, r, n, value):
        sh_t[pl.ds(r, n), :] = value

    sweep_rows(
        lambda f, r, n: h_t[pl.ds(r, n), :],
        lambda r, n: hc_t[pl.ds(r, n), :],
        store,
        a_scr,
        f_scr,
        RIM + 1,
        rows,
        32,
        fields=1,
    )


def inner_slopes(s_t, h_t, hc_t):
    planes, _, _, ext, _ = s_t.shape
    return call(
        inner_slopes_kernel,
        (out(4 * planes, ext - 2 * RIM, LANES), out(ext, LANES)),
        (s_t, h_t, hc_t),
        "inner_slopes",
        mib=8,
        scratch=[pltpu.VMEM((2, ext, LANES), F32)] * 2,
        cost=SWEEP_COST,
    )


VALUES_AT = 2
SLOPES_AT = 9


def y_edge_kernel(
    x_e,
    cy_e,
    h_t,
    hc_t,
    from_l,
    from_r,
    sh_in,
    sh_t,
    edges,
    strips,
    win,
    a_scr,
    f_scr,
    res,
):
    planes = x_e.shape[1]
    ext = h_t.shape[0]

    for high in range(2):
        rim, counts = (from_r, FIRST) if high else (from_l, LAST)
        at = slice(ext - 24, ext - 8) if high else slice(8, 24)

        def beyond(i, f):
            r, n = y_place(counts, i, f)
            return rim[r : r + n, :]

        for p in range(planes):
            for x in range(2):
                edge_sweep(
                    lambda f: cy_e[high, p, x] if f == 2 else x_e[high, p, f, x],
                    lambda f: beyond(p * 2 + x if f == 2 else (p * 2 + f) * 2 + x, f),
                    high,
                    win,
                    a_scr,
                    f_scr,
                    res,
                )
                for f in range(2):
                    k = (f * 4 + p) * STRIP
                    slopes = rows_slope(res.at[f], 8, 8)
                    if high:
                        strips[x, k : k + 2, :] = res[f, 14:16, :]
                        strips[x, k + 5 : k + 9, :] = slopes[4:8]
                    else:
                        strips[x, k + 2 : k + 5, :] = res[f, 8:11, :]
                        strips[x, k + 9 : k + 14, :] = slopes[0:5]
        edge_sweep(
            lambda f: hc_t[at, :] if f == 2 else h_t[at, :],
            lambda f: beyond(8, 2) if f == 2 else beyond(16, 0),
            high,
            win,
            a_scr,
            f_scr,
            res,
        )
        if high:
            sh_t[ext - 16 : ext, :] = res[0, 8:24, :]
        else:
            sh_t[0:16, :] = res[0, 0:16, :]
    for i in range(2):
        edges[i] = strips[i].T
        edges[2 + i] = sh_t[half(i, RIM), :].T
        edges[4 + i] = rows_slope(sh_t, RIM + i * LANES, LANES).T


def y_edge(x_e, cy_e, h_t, hc_t, from_l, from_r, sh_t):
    return call(
        y_edge_kernel,
        (out(*sh_t.shape), out(6, LANES, LANES)),
        (x_e, cy_e, h_t, hc_t, from_l, from_r, sh_t),
        "y_edge",
        mib=8,
        scratch=[pltpu.VMEM((2, LANES, LANES), F32)] + EDGE_SCRATCH,
        aliases={6: 0},
    )[1]


def finish_field(f, s_in, gy, edges, s, xy, adv=None):
    planes, width = xy.shape[3:5]
    rows = NP * width
    n = 2 * width
    lane = lane_iota(n)

    def put(dim, p, r, h, value):
        for i in range(n // width):
            xy[f, r // width + i, dim, p, :, half(h)] = value[i * width : (i + 1) * width]

    def body(p, _):
        strip = pl.multiple_of((f * 4 + p) * STRIP, STRIP)
        first = (p * 2 + f) * 2
        for r in range(0, rows, n):
            strips = edges[r // LANES, r % LANES : r % LANES + n, :]
            value = pltpu.roll(strips, LANES - VALUES_AT - strip, 1)
            y_slope = pltpu.roll(strips, LANES - SLOPES_AT - strip, 1)
            to = slice(RIM + r, RIM + r + n)
            for h in range(2):
                q = s_in[first + h, to, :]
                q = jnp.where(lane >= LANES - 2 if h else lane < 3, value, q)
                s[first + h, to, :] = q
                if adv is not None:
                    adv[f, p, r : r + n, half(h)] = q
                y = gy[first + h, r : r + n, :]
                put(1, p, r, h, jnp.where(lane >= LANES - 4 if h else lane < 5, y_slope, y))
        for h in range(2):

            def outer(kind, at, count):
                return edges[kind * 2 + h, pl.ds(strip + at, count), :]

            s[first + h, RIM - 2 : RIM + 3, :] = outer(1, 0, EDGE)
            s[first + h, RIM + rows - 3 : RIM + rows + 2, :] = outer(1, EDGE, EDGE)
            if adv is not None:
                adv[f, p, 0:3, half(h)] = outer(1, 2, 3)
                adv[f, p, rows - 3 : rows, half(h)] = outer(1, EDGE, 3)
            xy[f, 0, 1, p, 0:3, half(h)] = outer(2, 2, 3)
            xy[f, NP - 1, 1, p, width - 3 : width, half(h)] = outer(2, EDGE, 3)
            for r in range(0, rows, n):
                put(0, p, r, h, rows_slope(s.at[first + h], RIM + r, n))
        return 0

    lax.fori_loop(0, planes, body, 0, unroll=False)


def piece_of(owner, core, slot):
    rank = jnp.int32(0)
    piece = jnp.int32(0)
    for j in range(NP):
        mine = owner[0, j] == core
        piece = jnp.where(jnp.logical_and(mine, rank == slot), j, piece)
        rank = rank + mine.astype(jnp.int32)
    return piece, slot < rank


def clear(used, *refs):
    @pl.when(jnp.logical_not(used))
    def _():
        for ref in refs:
            ref[...] = jnp.zeros_like(ref)


def start_copy(used, src, zeros, to, sem):
    @pl.when(used)
    def _():
        pltpu.make_async_copy(src, to, sem).start()

    @pl.when(jnp.logical_not(used))
    def _():
        pltpu.make_async_copy(zeros, to, sem).start()


def own_slopes_kernel(owner, s_in, gy, edges, adv, grad, s, xy, buf, zeros, adv_sem, sems):
    planes = xy.shape[3]
    me = lax.axis_index("sa")
    mine = pl.ds(pl.multiple_of(planes * me, planes), planes)
    pieces = [piece_of(owner, me, slot) for slot in range(CAP)]
    clear(pieces[-1][1], zeros)

    def adv_copy(f):
        return pltpu.make_async_copy(buf.at[f], adv.at[f], adv_sem.at[f])

    for f in range(2):
        finish_field(f, s_in, gy, edges, s, xy, buf)
        adv_copy(f).start()
        if f == 0:
            for slot, (piece, used) in enumerate(pieces):
                start_copy(used, xy.at[0, piece], zeros, grad.at[slot, 0, 0:2, mine], sems.at[slot])
    for f in range(2):
        adv_copy(f).wait()
    for slot in range(CAP):
        pltpu.make_async_copy(zeros, grad.at[slot, 0, 0:2, mine], sems.at[slot]).wait()


SMEM = pl.BlockSpec(memory_space=pltpu.SMEM)
VMEM = pl.BlockSpec(memory_space=pltpu.VMEM)
ANY = pl.BlockSpec(memory_space=pl.ANY)


def own_slopes(owner, s_in, gy, edges):
    planes = s_in.shape[0] // 4
    rows = gy.shape[1]
    cols = 2 * LANES
    width = rows // NP
    return pl.pallas_call(
        own_slopes_kernel,
        in_specs=[SMEM, VMEM, VMEM, VMEM],
        out_specs=(ANY, ANY, VMEM, VMEM),
        out_shape=(
            out(2, planes, rows, cols),
            out(CAP, 2, 3, 2 * planes, width, cols),
            pltpu.VMEM(s_in.shape, F32),
            pltpu.VMEM((2, NP, 2, planes, width, cols), F32),
        ),
        scratch_shapes=[
            pltpu.VMEM((2, planes, rows, cols), F32),
            pltpu.VMEM((2, planes, width, cols), F32),
            pltpu.SemaphoreType.DMA((2,)),
            pltpu.SemaphoreType.DMA((CAP,)),
        ],
        compiler_params=pltpu.CompilerParams(vmem_limit_bytes=14 * MIB),
        cost_estimate=SWEEP_COST,
        name="own_slopes",
    )(owner, s_in, gy, edges)


def gradient_kernel(
    owner,
    own,
    own_xy,
    other_in,
    other_gy,
    other_edges,
    grad_in,
    grad,
    wedge,
    other,
    other_xy,
    part,
    wpart,
    zeros,
    xy_zeros,
    own_sems,
    xy_sems,
    sems,
):
    planes, width = own_xy.shape[3:5]
    me = lax.axis_index("sa")
    mine = pl.ds(pl.multiple_of(planes * me, planes), planes)
    theirs = pl.ds(pl.multiple_of(planes * (1 - me), planes), planes)

    pieces = [piece_of(owner, me, slot) for slot in range(CAP)]
    clear(pieces[-1][1], zeros, xy_zeros)
    for slot, (piece, used) in enumerate(pieces):
        start_copy(
            used, own_xy.at[1, piece], xy_zeros, grad.at[slot, 1, 0:2, mine], own_sems.at[slot]
        )
    for f in range(2):
        finish_field(f, other_in, other_gy, other_edges, other, other_xy)
        for slot, (piece, used) in enumerate(pieces):
            start_copy(
                used,
                other_xy.at[f, piece],
                xy_zeros,
                grad.at[slot, f, 0:2, theirs],
                xy_sems.at[slot, f],
            )

    def targets(slot):
        return grad.at[slot, 0, 2], grad.at[slot, 1, 2], wedge.at[slot]

    def fill(slot, piece):
        n = 8
        first = pl.multiple_of(piece * width, 8)

        def body(i, _):
            r = pl.ds(pl.multiple_of(RIM + first + i * n, n), n)
            to = pl.ds(pl.multiple_of(i * n, n), n)
            for h in range(2):
                cols = half(h)

                def plane(z, f):
                    ref = own if z < planes else other
                    return ref[((z % planes) * 2 + f) * 2 + h, r, :]

                q = [[plane(z, f) for f in range(2)] for z in range(8)]
                for z in range(8):
                    g = []
                    p = z % planes
                    zo = lax.rem(z + planes * me, 2 * planes)
                    xy = own_xy if z < planes else other_xy
                    for f in range(2):
                        z_slope = slope(
                            q[(z + 1) % 8][f] - q[(z + 7) % 8][f],
                            q[(z + 2) % 8][f] - q[(z + 6) % 8][f],
                        )
                        part[slot, f, zo, to, cols] = z_slope
                        g.append((xy[f, piece, 0, p, to, cols], xy[f, piece, 1, p, to, cols], z_slope))
                    rx, ry, rz = g[0]
                    tx, ty, tz = g[1]
                    a = ry * tz - rz * ty
                    b = rz * tx - rx * tz
                    c = rx * ty - ry * tx
                    wpart[slot, zo, to, cols] = a * a + b * b + c * c
            return 0

        lax.fori_loop(0, width // n, body, 0, unroll=False)

    def slot_body(slot, _):
        piece, used = piece_of(owner, me, slot)

        @pl.when(used)
        def _():
            fill(slot, piece)

        sources = part.at[slot, 0], part.at[slot, 1], wpart.at[slot]
        for k, (src, to) in enumerate(zip(sources, targets(slot))):
            start_copy(used, src, zeros, to, sems.at[slot, k])
        return 0

    lax.fori_loop(0, CAP, slot_body, 0, unroll=False)

    def wait_body(slot, _):
        pltpu.make_async_copy(xy_zeros, grad.at[slot, 1, 0:2, mine], own_sems.at[slot]).wait()
        for f in range(2):
            pltpu.make_async_copy(
                xy_zeros, grad.at[slot, f, 0:2, theirs], xy_sems.at[slot, f]
            ).wait()
        for k, to in enumerate(targets(slot)):
            pltpu.make_async_copy(zeros, to, sems.at[slot, k]).wait()
        return 0

    lax.fori_loop(0, CAP, wait_body, 0, unroll=False)


def gradients_of(owner, own, own_xy, other, other_gy, other_edges, grad):
    planes, width, cols = own_xy.shape[3:]
    return pl.pallas_call(
        gradient_kernel,
        in_specs=[SMEM, VMEM, VMEM, VMEM, VMEM, VMEM, ANY],
        out_specs=(ANY, ANY),
        out_shape=(out(*grad.shape), out(CAP, 2 * planes, width, cols)),
        scratch_shapes=[
            pltpu.VMEM(own.shape, F32),
            pltpu.VMEM(own_xy.shape, F32),
            pltpu.VMEM((CAP, 2, 2 * planes, width, cols), F32),
            pltpu.VMEM((CAP, 2 * planes, width, cols), F32),
            pltpu.VMEM((2 * planes, width, cols), F32),
            pltpu.VMEM((2, planes, width, cols), F32),
            pltpu.SemaphoreType.DMA((CAP,)),
            pltpu.SemaphoreType.DMA((CAP, 2)),
            pltpu.SemaphoreType.DMA((CAP, 3)),
        ],
        input_output_aliases={6: 0},
        compiler_params=pltpu.CompilerParams(vmem_limit_bytes=24 * MIB),
        name="gradient",
    )(owner, own, own_xy, other, other_gy, other_edges, grad)


def per_device(density, heat, cx, cy, owner):
    nx, ny = lax.axis_size("gx"), lax.axis_size("gy")
    lo, hi = edge_rows((density, heat, cx, cy))
    left = lax.ppermute(hi, "gx", ring(nx, 1))
    right = lax.ppermute(lo, "gx", ring(nx, -1))
    x_e, cy_e, s_t, swept = inner(density, heat, cx, cy)
    h_t, hc_t, to_l, to_r = x_edge(density, heat, cx, cy, left, right, x_e, cy_e)
    sent, to_l, to_r = lax.optimization_barrier((swept, to_l, to_r))
    other = lax.ppermute(sent, "sa", ring(2, 1))
    from_l = lax.ppermute(to_r, "gy", ring(ny, 1))
    from_r = lax.ppermute(to_l, "gy", ring(ny, -1))
    gy, sh_t = inner_slopes(s_t, h_t, hc_t)
    sent, from_l, from_r = lax.optimization_barrier((gy, from_l, from_r))
    other_gy = lax.ppermute(sent, "sa", ring(2, 1))
    edges = y_edge(x_e, cy_e, h_t, hc_t, from_l, from_r, sh_t)
    other_edges = lax.ppermute(edges, "sa", ring(2, 1))
    advected, gradients, own, own_xy = own_slopes(owner, swept, gy, edges)
    gradients, wedge = gradients_of(owner, own, own_xy, other, other_gy, other_edges, gradients)
    return advected, gradients, wedge


def solution(mesh):
    block = P("sa", "gx", "gy")
    return jax.shard_map(
        per_device,
        mesh=mesh,
        in_specs=(block, block, block, block, P("gx", None)),
        out_specs=(
            P(None, "sa", "gx", "gy"),
            P(("gx", "sa"), None, None, None, None, "gy"),
            P(("gx", "sa"), None, None, "gy"),
        ),
        check_vma=False,
    )
```
